512 devices in a mesh: seq: 32 (over y, x, core), head: 16 (over z).
Axes of the slice: x: 4, y: 4, z: 16, core: 2. Of those that a mesh axis runs over, the one named last changes fastest.
Arguments:
- queries: bfloat16 [32768, 2048], P('seq', 'head'), may hold values from -72 to 72
- encodings: bfloat16 [224, 128, 896], P('seq'), may hold values from -6 to 6
- key_weight: bfloat16 [896, 2048], P(None, 'head'), may hold values from -0.1875 to 0.1875
- value_weight: bfloat16 [896, 2048], P(None, 'head'), may hold values from -0.1875 to 0.1875
- reads: int32 [512, 2], replicated, may hold values from 0 to 223, as said below
- out_grad: bfloat16 [32768, 2048], P('seq', 'head'), may hold values from -6 to 6
Outputs:
- attended: bfloat16 [32768, 2048], P('seq', 'head')
- query_grad: bfloat16 [32768, 2048], P('seq', 'head')
- encoding_grad: float32 [224, 128, 896], P('seq', 'head')
- key_weight_grad: float32 [896, 2048], P('seq', 'head')
- value_weight_grad: float32 [896, 2048], P('seq', 'head')
The draws below stay inside these ranges and needn't reach their ends.
Inputs may be any that keep to these rules, and one draw needn't show every extreme that they name: reads[c, k] is held by seq shard reads[c, k] // 7. Of the 32 reads of the segments of one seq shard, at most 2 fall on the encodings of one holder shard; in every draw one holder shard is read exactly 2 times by every seq shard.
All inputs are finite; a program needn't handle non-finite values.
Results may differ from the reference program's by a relative error of at most 0.012.
The reference program's roundings to bfloat16 on the way (of `key_rows`, `value_rows`, `probs_bf`, `score_grad`, `key_grad_rows` and `value_grad_rows`) count: a program that leaves them out, or rounds other values in their place, can miss the bound.
Values may be sent and summed in bfloat16 or wider, within the bound.
No kernel may reach another device: no remote copies, remote signals or barrier semaphores. Data moves between devices by JAX's collectives and lax.ppermute only.
A program may use at most 128 MiB of HBM per device.

```python
import math
import jax
import jax.numpy as jnp
from jax import lax

DH = 128
EW = 896
HEAD_DEV = 1
SEGMENT = 64
NTOK = 128
NEIGH = 2
CH_DEV = 16
CAP = 2
NB_DEV = 7
HD = 2048
GROUPS = 512
TOKENS = 32768
BLOCKS = 224
N_SEQ = 32
N_HEAD = 16


def draw_queries(key, part):
    key = jax.random.fold_in(key, 5)
    key_base = jax.random.fold_in(key, 0)
    base = jnp.clip(jax.random.normal(key_base, (TOKENS, HD), jnp.float32), -6.0, 6.0)
    return base.astype(jnp.bfloat16)


def draw_reads(key, part):
    key = jax.random.fold_in(key, 11)
    read_count = NEIGH * CH_DEV
    key_hot, key_rows = jax.random.split(key)
    hot_holder = jax.random.randint(key_hot, (), 0, N_SEQ)

    def one_shard(shard_key):
        key_rest, key_order, key_block = jax.random.split(shard_key, 3)
        rest = jax.random.permutation(key_rest, (N_SEQ - 1) * CAP)[:read_count - CAP]
        offsets = jnp.concatenate([jnp.zeros((CAP,), jnp.int32), 1 + rest // CAP]).astype(jnp.int32)
        holders = (hot_holder + offsets) % N_SEQ
        holders = jax.random.permutation(key_order, holders)
        in_shard = jax.random.randint(key_block, (read_count,), 0, NB_DEV)
        return holders * NB_DEV + in_shard
    table = jax.vmap(one_shard)(jax.random.split(key_rows, N_SEQ))
    return table.reshape(CH_DEV * N_SEQ, NEIGH).astype(jnp.int32)


def steps_of(rng, dims, cuts, low, high):
    level = 1.0
    for position, blocks in cuts:
        steps = jax.random.uniform(jax.random.fold_in(jax.random.fold_in(rng, 6), position), (blocks,), jnp.float32, low / len(cuts), high / len(cuts))
        level = level * jnp.repeat(jnp.exp(steps), dims[position] // blocks).reshape((-1,) + (1,) * (len(dims) - 1 - position))
    return level


def noise(rng, extent, deviation, most, pieces=(), dtype=jnp.bfloat16):
    factor_of = steps_of(rng, extent, pieces, -0.22, 0.18) if pieces else 1.0
    entries = jax.random.normal(rng, extent, jnp.float32) * deviation * factor_of
    return jnp.minimum(jnp.maximum(entries, -most), most).astype(dtype)


def setup_inputs(seed: int = 0) -> dict:
    splits = jax.random.split(jax.random.key(seed), 7)
    queries = draw_queries(jax.random.fold_in(splits[6], 71), 0)
    encodings = noise(splits[1], (BLOCKS, NTOK, EW), 1.0, 6.0, ((0, 32),))
    key_weight = noise(splits[2], (EW, HD), EW ** -0.5, 0.1875, ((1, 16),))
    value_weight = noise(splits[3], (EW, HD), EW ** -0.5, 0.1875, ((1, 16),))
    reads = draw_reads(jax.random.fold_in(splits[6], 71), 0)
    out_grad = noise(splits[5], (TOKENS, HD), 1.0, 6.0, ((0, 32), (1, 16)))
    return {"queries": queries, "encodings": encodings, "key_weight": key_weight, "value_weight": value_weight, "reads": reads, "out_grad": out_grad}


def reference(queries, encodings, key_weight, value_weight, reads, out_grad):
    heads = HEAD_DEV * N_HEAD
    score_scale = 1.0 / math.sqrt(DH)
    flat_enc = encodings.reshape(BLOCKS * NTOK, EW)
    key_rows = jnp.dot(flat_enc, key_weight, preferred_element_type=jnp.float32).astype(jnp.bfloat16)
    value_rows = jnp.dot(flat_enc, value_weight, preferred_element_type=jnp.float32).astype(jnp.bfloat16)
    key_blocks = key_rows.reshape(BLOCKS, NTOK, heads, DH)
    value_blocks = value_rows.reshape(BLOCKS, NTOK, heads, DH)
    query_segs = queries.reshape(GROUPS, SEGMENT, heads, DH)
    grad_segs = out_grad.reshape(GROUPS, SEGMENT, heads, DH)

    def one_segment(carry, inputs):
        key_acc, value_acc = carry
        query_seg, grad_seg, picked = inputs
        picked = picked.astype(jnp.int32)
        seg_keys = key_blocks[picked].reshape(NEIGH * NTOK, heads, DH).astype(jnp.float32)
        seg_values = value_blocks[picked].reshape(NEIGH * NTOK, heads, DH).astype(jnp.float32)
        query_f = query_seg.astype(jnp.float32)
        grad_f = grad_seg.astype(jnp.float32)
        scores = jnp.einsum('qhd,khd->hqk', query_f, seg_keys) * score_scale
        probs = jax.nn.softmax(scores, axis=-1)
        probs_bf = probs.astype(jnp.bfloat16).astype(jnp.float32)
        attended = jnp.einsum('hqk,khd->qhd', probs_bf, seg_values).astype(jnp.bfloat16)
        value_part = jnp.einsum('hqk,qhd->khd', probs_bf, grad_f)
        prob_grad = jnp.einsum('qhd,khd->hqk', grad_f, seg_values)
        delta_sum = lax.optimization_barrier(jnp.sum(probs * prob_grad, axis=-1, keepdims=True))
        score_grad = (probs * (prob_grad - delta_sum) * score_scale).astype(jnp.bfloat16).astype(jnp.float32)
        query_part = jnp.einsum('hqk,khd->qhd', score_grad, seg_keys).astype(jnp.bfloat16)
        key_part = jnp.einsum('hqk,qhd->khd', score_grad, query_f)
        key_acc = key_acc.at[picked].add(key_part.reshape(NEIGH, NTOK, heads, DH))
        value_acc = value_acc.at[picked].add(value_part.reshape(NEIGH, NTOK, heads, DH))
        return ((key_acc, value_acc), (attended, query_part))
    zeros_acc = jnp.zeros((BLOCKS, NTOK, heads, DH), jnp.float32)
    (key_total, value_total), (attended, query_part) = lax.scan(one_segment, (zeros_acc, zeros_acc), (query_segs, grad_segs, reads))
    key_grad_rows = key_total.reshape(BLOCKS * NTOK, HD).astype(jnp.bfloat16)
    value_grad_rows = value_total.reshape(BLOCKS * NTOK, HD).astype(jnp.bfloat16)
    key_weight_grad = jnp.dot(flat_enc.T, key_grad_rows, preferred_element_type=jnp.float32)
    value_weight_grad = jnp.dot(flat_enc.T, value_grad_rows, preferred_element_type=jnp.float32)
    encoding_grad = jnp.dot(key_grad_rows, key_weight.T, preferred_element_type=jnp.float32) + jnp.dot(value_grad_rows, value_weight.T, preferred_element_type=jnp.float32)
    return (attended.reshape(TOKENS, HD), query_part.reshape(TOKENS, HD), encoding_grad.reshape(BLOCKS, NTOK, EW), key_weight_grad, value_weight_grad)
```

```python
import math

import jax
import jax.numpy as jnp
from jax import lax
from jax.experimental import pallas as pl
from jax.experimental.pallas import tpu as pltpu
from jax.sharding import PartitionSpec as P

SEGMENT = 64
NEIGH = 2
CAP = 2
VMEM_LIMIT = 40 * 1024 * 1024
VMEM = pltpu.VMEM
SMEM = pltpu.SMEM


def params():
    return pltpu.CompilerParams(vmem_limit_bytes=VMEM_LIMIT)


def spec(space):
    return pl.BlockSpec(memory_space=space)


def nt_dot(a, b):
    return lax.dot_general(a, b, (((1,), (1,)), ((), ())), preferred_element_type=jnp.float32)


def tn_dot(a, b):
    return lax.dot_general(a, b, (((0,), (0,)), ((), ())), preferred_element_type=jnp.float32)


def nn_dot(a, b):
    return jnp.dot(a, b, preferred_element_type=jnp.float32)


def pack_kernel(block_count, seq_count, read_count, reads_ref, q_ref, g_ref, out_ref, slots_ref, used):
    head_dim = q_ref.shape[2]
    out_ref[...] = jnp.zeros_like(out_ref)

    def clear(h, _):
        used[h] = 0
        return 0

    lax.fori_loop(0, seq_count, clear, 0)

    def place(j, _):
        holder = lax.div(reads_ref[j], block_count)
        rank = used[holder]
        used[holder] = rank + 1
        slot = holder * CAP + rank
        slots_ref[j] = slot
        seg = lax.div(j, NEIGH)
        out_ref[slot, :, :head_dim] = q_ref[seg]
        out_ref[slot, :, head_dim:] = g_ref[seg]
        return 0

    lax.fori_loop(0, read_count, place, 0)


def pair_operands(x, kv_a, kv_b):
    head_dim = x.shape[1] // 2
    first = lax.broadcasted_iota(jnp.int32, (x.shape[0], head_dim), 0) < SEGMENT
    zero = jnp.zeros((x.shape[0], head_dim), x.dtype)
    q, g = x[:, :head_dim], x[:, head_dim:]
    q_diag = jnp.concatenate([jnp.where(first, q, zero), jnp.where(first, zero, q)], axis=1)
    g_diag = jnp.concatenate([jnp.where(first, g, zero), jnp.where(first, zero, g)], axis=1)
    keys = jnp.concatenate([kv_a[:, :head_dim], kv_b[:, :head_dim]], axis=1)
    values = jnp.concatenate([kv_a[:, head_dim:], kv_b[:, head_dim:]], axis=1)
    return q_diag, g_diag, keys, values, first


def stats_kernel(scale, blocks_ref, x_ref, kv_ref, out_ref):
    def step(s, _):
        kv_a = kv_ref[blocks_ref[CAP * s]]
        kv_b = kv_ref[blocks_ref[CAP * s + 1]]
        q_diag, g_diag, keys, values, _ = pair_operands(x_ref[s], kv_a, kv_b)
        scores = nt_dot(keys, q_diag) * scale
        top = jnp.max(scores, axis=0, keepdims=True)
        weight = jnp.exp(scores - top)
        total = jnp.sum(weight, axis=0, keepdims=True)
        prob_grad = nt_dot(values, g_diag)
        mean = jnp.sum(weight * prob_grad, axis=0, keepdims=True) / total
        both = jnp.concatenate([top + jnp.log(total), mean], axis=0)
        out_ref[CAP * s] = both
        out_ref[CAP * s + 1] = pltpu.roll(both, SEGMENT, 1)
        return 0

    lax.fori_loop(0, x_ref.shape[0], step, 0, unroll=2)


def merge_kernel(slots_ref, in_ref, out_ref):
    out_ref[...] = jnp.zeros_like(out_ref)
    for c in range(slots_ref.shape[0] // NEIGH):
        slot_a, slot_b = slots_ref[NEIGH * c], slots_ref[NEIGH * c + 1]
        one, two = in_ref[slot_a], in_ref[slot_b]
        lse_a, lse_b = one[0:1], two[0:1]
        top = jnp.maximum(lse_a, lse_b)
        lse = top + jnp.log(jnp.exp(lse_a - top) + jnp.exp(lse_b - top))
        delta = jnp.exp(lse_a - lse) * one[1:2] + jnp.exp(lse_b - lse) * two[1:2]
        both = jnp.concatenate([lse, delta], axis=0)
        out_ref[slot_a] = both
        out_ref[slot_b] = both


def grads_kernel(scale, blocks_ref, x_ref, kv_ref, stats_ref, enc_t_ref, out_ref, rows_ref, acc_k, acc_v):
    head_dim = kv_ref.shape[2] // 2
    pair = x_ref.shape[1]
    acc_k[...] = jnp.zeros_like(acc_k)
    acc_v[...] = jnp.zeros_like(acc_v)

    def step(s, _):
        block_a = blocks_ref[CAP * s]
        block_b = blocks_ref[CAP * s + 1]
        q_diag, g_diag, keys, values, first = pair_operands(x_ref[s], kv_ref[block_a], kv_ref[block_b])
        left = lax.broadcasted_iota(jnp.int32, (2, pair), 1) < SEGMENT
        both = jnp.where(left, stats_ref[CAP * s], pltpu.roll(stats_ref[CAP * s + 1], SEGMENT, 1))
        scores = nt_dot(keys, q_diag) * scale
        probs = jnp.exp(scores - both[0:1])
        prob_grad = nt_dot(values, g_diag)
        score_grad = (probs * (prob_grad - both[1:2]) * scale).astype(jnp.bfloat16)
        probs = probs.astype(jnp.bfloat16)
        attended = tn_dot(probs, values)
        query_grad = tn_dot(score_grad, keys)
        out_ref[s, :pair, :head_dim] = jnp.where(
            first, attended[:, :head_dim], attended[:, head_dim:]
        ).astype(jnp.bfloat16)
        out_ref[s, :pair, head_dim:] = jnp.where(
            first, query_grad[:, :head_dim], query_grad[:, head_dim:]
        ).astype(jnp.bfloat16)
        value_part = nn_dot(probs, g_diag)
        key_part = nn_dot(score_grad, q_diag)
        acc_k[block_a] += key_part[:, :head_dim]
        acc_v[block_a] += value_part[:, :head_dim]
        acc_k[block_b] += key_part[:, head_dim:]
        acc_v[block_b] += value_part[:, head_dim:]
        return 0

    lax.fori_loop(0, x_ref.shape[0], step, 0, unroll=2)
    rows_ref[:, :, :head_dim] = acc_k[...].astype(jnp.bfloat16)
    rows_ref[:, :, head_dim:] = acc_v[...].astype(jnp.bfloat16)
    rows = rows_ref[...].reshape(-1, 2 * head_dim)
    share = enc_t_ref.shape[0] // x_ref.shape[0]
    pad = out_ref.shape[1] - pair - share
    group = 4
    for s in range(0, x_ref.shape[0], group):
        term = nn_dot(enc_t_ref[s * share:(s + group) * share], rows).reshape(group, share, 2 * head_dim)
        if pad:
            term = jnp.concatenate([term, jnp.zeros((group, pad, 2 * head_dim), jnp.float32)], axis=1)
        out_ref[s:s + group, pair:] = term.astype(jnp.bfloat16)


def finish_kernel(slots_ref, in_ref, att_ref, qg_ref, kw_ref, vw_ref):
    head_dim = att_ref.shape[2]
    share = kw_ref.shape[0]
    pair = CAP * SEGMENT

    def step(c, _):
        slot_a, slot_b = slots_ref[NEIGH * c], slots_ref[NEIGH * c + 1]

        def part(slot):
            holder = lax.div(slot, CAP)
            row = pl.multiple_of((slot - holder * CAP) * SEGMENT, SEGMENT)
            return in_ref[holder, pl.ds(row, SEGMENT), :].astype(jnp.float32)

        total = (part(slot_a) + part(slot_b)).astype(jnp.bfloat16)
        att_ref[c] = total[:, :head_dim]
        qg_ref[c] = total[:, head_dim:]
        return 0

    lax.fori_loop(0, att_ref.shape[0], step, 0, unroll=2)
    total = in_ref[0, pair:, :].astype(jnp.float32)
    for s in range(1, in_ref.shape[0]):
        total = total + in_ref[s, pair:, :].astype(jnp.float32)
    kw_ref[...] = total[:share, :head_dim]
    vw_ref[...] = total[:share, head_dim:]


def project_kernel(rows_ref, weights_ref, out_ref):
    @pl.when(pl.program_id(0) == 0)
    def _():
        out_ref[...] = jnp.zeros_like(out_ref)

    out_ref[...] += nt_dot(rows_ref[0], weights_ref[0])


def on_device(queries, encodings, key_weight, value_weight, reads, out_grad):
    seq_count = lax.axis_size("seq")
    head_count = lax.axis_size("head")
    me = lax.axis_index("seq")
    block_count, block_len, enc_width = encodings.shape
    head_dim = key_weight.shape[1]
    segments = queries.shape[0] // SEGMENT
    read_count = NEIGH * segments
    slot_count = seq_count * CAP
    scale = 1.0 / math.sqrt(head_dim)
    bf16, f32 = jnp.bfloat16, jnp.float32

    tables = reads.reshape(seq_count, read_count)
    my_reads = lax.dynamic_index_in_dim(tables, me, 0, keepdims=False)
    packed, slots = pl.pallas_call(
        lambda *refs: pack_kernel(block_count, seq_count, read_count, *refs),
        out_shape=(
            jax.ShapeDtypeStruct((slot_count, SEGMENT, 2 * head_dim), bf16),
            jax.ShapeDtypeStruct((read_count,), jnp.int32),
        ),
        in_specs=[spec(SMEM), spec(VMEM), spec(VMEM)],
        out_specs=(spec(VMEM), spec(SMEM)),
        scratch_shapes=[pltpu.SMEM((seq_count,), jnp.int32)],
        compiler_params=params(),
        name="pack",
    )(
        my_reads,
        queries.reshape(segments, SEGMENT, head_dim),
        out_grad.reshape(segments, SEGMENT, head_dim),
    )
    arrived = lax.all_to_all(packed, "seq", split_axis=0, concat_axis=0, tiled=True)
    pairs = arrived.reshape(seq_count, CAP * SEGMENT, 2 * head_dim)

    weights = jnp.concatenate([key_weight, value_weight], axis=1)
    all_weights = lax.all_gather(weights, "head", axis=0, tiled=False)
    flat_enc = encodings.reshape(block_count * block_len, enc_width)
    kv = jnp.dot(flat_enc, weights, preferred_element_type=f32).astype(bf16)
    kv = kv.reshape(block_count, block_len, 2 * head_dim)
    enc_t = flat_enc.T

    mine = (tables // block_count) == me
    rank = jnp.cumsum(mine.astype(jnp.int32), axis=1)
    blocks = jnp.stack(
        [
            jnp.sum(jnp.where(mine & (rank == k + 1), tables % block_count, 0), axis=1)
            for k in range(CAP)
        ],
        axis=1,
    ).reshape(slot_count)

    stats = pl.pallas_call(
        lambda *refs: stats_kernel(scale, *refs),
        out_shape=jax.ShapeDtypeStruct((slot_count, 2, CAP * SEGMENT), f32),
        in_specs=[spec(SMEM), spec(VMEM), spec(VMEM)],
        out_specs=spec(VMEM),
        compiler_params=params(),
        name="stats",
    )(blocks, pairs, kv)
    stats = lax.all_to_all(stats, "seq", split_axis=0, concat_axis=0, tiled=True)
    merged = pl.pallas_call(
        merge_kernel,
        out_shape=jax.ShapeDtypeStruct(stats.shape, f32),
        in_specs=[spec(SMEM), spec(VMEM)],
        out_specs=spec(VMEM),
        compiler_params=params(),
        name="merge",
    )(slots, stats)
    merged = lax.all_to_all(merged, "seq", split_axis=0, concat_axis=0, tiled=True)

    share = enc_width // seq_count
    room = -(-share // 16) * 16
    back, grad_rows = pl.pallas_call(
        lambda *refs: grads_kernel(scale, *refs),
        out_shape=(
            jax.ShapeDtypeStruct((seq_count, CAP * SEGMENT + room, 2 * head_dim), bf16),
            jax.ShapeDtypeStruct((block_count, block_len, 2 * head_dim), bf16),
        ),
        in_specs=[spec(SMEM), spec(VMEM), spec(VMEM), spec(VMEM), spec(VMEM)],
        out_specs=(spec(VMEM), spec(VMEM)),
        scratch_shapes=[
            pltpu.VMEM((block_count, block_len, head_dim), f32),
            pltpu.VMEM((block_count, block_len, head_dim), f32),
        ],
        compiler_params=params(),
        name="grads",
    )(blocks, pairs, kv, merged, enc_t)

    row_share = block_len // head_count
    by_row = grad_rows.reshape(block_count, head_count, row_share, 2 * head_dim)
    by_row = by_row.transpose(1, 0, 2, 3).reshape(head_count, block_count * row_share, 2 * head_dim)
    row_parts = lax.all_to_all(by_row, "head", split_axis=0, concat_axis=0, tiled=True)
    encoding_grad = pl.pallas_call(
        project_kernel,
        grid=(head_count,),
        out_shape=jax.ShapeDtypeStruct((block_count * row_share, enc_width), f32),
        in_specs=[
            pl.BlockSpec((1, block_count * row_share, 2 * head_dim), lambda h: (h, 0, 0)),
            pl.BlockSpec((1, enc_width, 2 * head_dim), lambda h: (h, 0, 0)),
        ],
        out_specs=pl.BlockSpec((block_count * row_share, enc_width), lambda h: (0, 0)),
        compiler_params=params(),
        name="project",
    )(row_parts, all_weights)

    returned = lax.all_to_all(back, "seq", split_axis=0, concat_axis=0, tiled=True)
    attended, query_grad, key_weight_grad, value_weight_grad = pl.pallas_call(
        finish_kernel,
        out_shape=(
            jax.ShapeDtypeStruct((segments, SEGMENT, head_dim), bf16),
            jax.ShapeDtypeStruct((segments, SEGMENT, head_dim), bf16),
            jax.ShapeDtypeStruct((share, head_dim), f32),
            jax.ShapeDtypeStruct((share, head_dim), f32),
        ),
        in_specs=[spec(SMEM), spec(VMEM)],
        out_specs=(spec(VMEM),) * 4,
        compiler_params=params(),
        name="finish",
    )(slots, returned)
    return (
        attended.reshape(segments * SEGMENT, head_dim),
        query_grad.reshape(segments * SEGMENT, head_dim),
        encoding_grad.reshape(block_count, row_share, enc_width),
        key_weight_grad,
        value_weight_grad,
    )


def solution(mesh):
    in_specs = (
        P("seq", "head"),
        P("seq", None, None),
        P(None, "head"),
        P(None, "head"),
        P(),
        P("seq", "head"),
    )
    out_specs = (
        P("seq", "head"),
        P("seq", "head"),
        P("seq", "head", None),
        P("seq", "head"),
        P("seq", "head"),
    )
    return jax.shard_map(
        on_device, mesh=mesh, in_specs=in_specs, out_specs=out_specs, check_vma=False
    )
```

```python
import math

import jax
import jax.numpy as jnp
from jax import lax
from jax.experimental import pallas as pl
from jax.experimental.pallas import tpu as pltpu
from jax.sharding import PartitionSpec as P

SEGMENT = 64
NEIGH = 2
CAP = 2
STEPS_NEAR = (0, 1, -1, 2)
STEPS_FAR = (0, 4, -4, 8)
VMEM_LIMIT = 40 * 1024 * 1024
VMEM = pltpu.VMEM
SMEM = pltpu.SMEM


def params():
    return pltpu.CompilerParams(vmem_limit_bytes=VMEM_LIMIT)


def spec(space):
    return pl.BlockSpec(memory_space=space)


def nt_dot(a, b):
    return lax.dot_general(a, b, (((1,), (1,)), ((), ())), preferred_element_type=jnp.float32)


def tn_dot(a, b):
    return lax.dot_general(a, b, (((0,), (0,)), ((), ())), preferred_element_type=jnp.float32)


def nn_dot(a, b):
    return jnp.dot(a, b, preferred_element_type=jnp.float32)


def pack_kernel(block_count, reads_ref, q_ref, g_ref, out_ref, slots_ref, used, zeros, copied, cleared):
    seq_count = used.shape[0]
    read_count = slots_ref.shape[0]
    zeros[...] = jnp.zeros_like(zeros)

    def clear(h, _):
        used[h] = 0
        return 0

    lax.fori_loop(0, seq_count, clear, 0)

    def copies(j, slot):
        seg = lax.div(j, NEIGH)
        return (
            pltpu.make_async_copy(q_ref.at[seg], out_ref.at[slot, 0], copied.at[j, 0]),
            pltpu.make_async_copy(g_ref.at[seg], out_ref.at[slot, 1], copied.at[j, 1]),
        )

    def place(j, _):
        holder = lax.div(reads_ref[j], block_count)
        rank = used[holder]
        used[holder] = rank + 1
        slot = holder * CAP + rank
        slots_ref[j] = slot
        for copy in copies(j, slot):
            copy.start()
        return 0

    lax.fori_loop(0, read_count, place, 0)

    def blank(slot):
        return pltpu.make_async_copy(zeros, out_ref.at[slot], cleared.at[slot])

    def wipe(slot, finish):
        holder = lax.div(slot, CAP)

        @pl.when(slot - holder * CAP >= used[holder])
        def _():
            if finish:
                blank(slot).wait()
            else:
                blank(slot).start()

    def wipe_start(slot, _):
        wipe(slot, False)
        return 0

    def wipe_wait(slot, _):
        wipe(slot, True)
        return 0

    def arrive(j, _):
        for copy in copies(j, slots_ref[j]):
            copy.wait()
        return 0

    lax.fori_loop(0, CAP * seq_count, wipe_start, 0)
    lax.fori_loop(0, read_count, arrive, 0)
    lax.fori_loop(0, CAP * seq_count, wipe_wait, 0)


def pair_operands(x_ref, s, kv_a, kv_b):
    head_dim = x_ref.shape[3]

    def diagonal(i):
        one, two = x_ref[CAP * s, i], x_ref[CAP * s + 1, i]
        zero = jnp.zeros_like(one)
        return jnp.concatenate(
            [jnp.concatenate([one, zero], axis=1), jnp.concatenate([zero, two], axis=1)], axis=0
        )

    keys = jnp.concatenate([kv_a[:, :head_dim], kv_b[:, :head_dim]], axis=1)
    values = jnp.concatenate([kv_a[:, head_dim:], kv_b[:, head_dim:]], axis=1)
    return diagonal(0), diagonal(1), keys, values


def stats_kernel(scale, unroll, blocks_ref, x_ref, kv_ref, out_ref):
    def step(s, _):
        kv_a = kv_ref[blocks_ref[CAP * s]]
        kv_b = kv_ref[blocks_ref[CAP * s + 1]]
        q_diag, g_diag, keys, values = pair_operands(x_ref, s, kv_a, kv_b)
        scores = nt_dot(keys, q_diag) * scale
        top = jnp.max(scores, axis=0, keepdims=True)
        weight = jnp.exp(scores - top)
        total = jnp.sum(weight, axis=0, keepdims=True)
        prob_grad = nt_dot(values, g_diag)
        mean = jnp.sum(weight * prob_grad, axis=0, keepdims=True) / total
        both = jnp.concatenate([top + jnp.log(total), mean], axis=0)
        out_ref[CAP * s] = both
        out_ref[CAP * s + 1] = pltpu.roll(both, SEGMENT, 1)
        return 0

    lax.fori_loop(0, x_ref.shape[0] // CAP, step, 0, unroll=unroll)


def merge_kernel(slots_ref, in_ref, out_ref):
    out_ref[...] = jnp.zeros_like(out_ref)
    for c in range(slots_ref.shape[0] // NEIGH):
        slot_a, slot_b = slots_ref[NEIGH * c], slots_ref[NEIGH * c + 1]
        one, two = in_ref[slot_a], in_ref[slot_b]
        lse_a, lse_b = one[0:1], two[0:1]
        top = jnp.maximum(lse_a, lse_b)
        lse = top + jnp.log(jnp.exp(lse_a - top) + jnp.exp(lse_b - top))
        delta = jnp.exp(lse_a - lse) * one[1:2] + jnp.exp(lse_b - lse) * two[1:2]
        both = jnp.concatenate([lse, delta], axis=0)
        out_ref[slot_a] = both
        out_ref[slot_b] = both


def grads_kernel(
    scale, unroll, me_ref, blocks_ref, x_ref, kv_ref, stats_ref, enc_t_ref, *refs
):
    near = len(STEPS_NEAR)
    out_ref = refs[0]
    rows_refs = refs[1:1 + near]
    stage, rows_all, acc_k, acc_v, sems = refs[1 + near:]
    head_dim = kv_ref.shape[2] // 2
    seq_count = x_ref.shape[0] // CAP
    pair = CAP * SEGMENT
    parts = 2 * pair
    acc_k[...] = jnp.zeros_like(acc_k)
    acc_v[...] = jnp.zeros_like(acc_v)

    def leave(s):
        return pltpu.make_async_copy(stage.at[s], out_ref.at[s], sems.at[s])

    def step(s, _):
        block_a = blocks_ref[CAP * s]
        block_b = blocks_ref[CAP * s + 1]
        q_diag, g_diag, keys, values = pair_operands(x_ref, s, kv_ref[block_a], kv_ref[block_b])
        left = lax.broadcasted_iota(jnp.int32, (2, pair), 1) < SEGMENT
        both = jnp.where(left, stats_ref[CAP * s], pltpu.roll(stats_ref[CAP * s + 1], SEGMENT, 1))
        scores = nt_dot(keys, q_diag) * scale
        probs = jnp.exp(scores - both[0:1])
        prob_grad = nt_dot(values, g_diag)
        score_grad = (probs * (prob_grad - both[1:2]) * scale).astype(jnp.bfloat16)
        probs = probs.astype(jnp.bfloat16)
        attended = tn_dot(probs, values).astype(jnp.bfloat16)
        query_grad = tn_dot(score_grad, keys).astype(jnp.bfloat16)
        stage[s, :SEGMENT] = attended[:SEGMENT, :head_dim]
        stage[s, SEGMENT:pair] = query_grad[:SEGMENT, :head_dim]
        stage[s, pair:pair + SEGMENT] = attended[SEGMENT:, head_dim:]
        stage[s, pair + SEGMENT:parts] = query_grad[SEGMENT:, head_dim:]
        value_part = nn_dot(probs, g_diag)
        key_part = nn_dot(score_grad, q_diag)
        acc_k[block_a] += key_part[:, :head_dim]
        acc_v[block_a] += value_part[:, :head_dim]
        acc_k[block_b] += key_part[:, head_dim:]
        acc_v[block_b] += value_part[:, head_dim:]
        return 0

    lax.fori_loop(0, seq_count, step, 0, unroll=unroll)
    head_count = near * len(STEPS_FAR)
    block_count, block_len, _ = acc_k.shape
    row_share = block_len // head_count
    z = me_ref[0]
    for i, a in enumerate(STEPS_NEAR):
        for j, b in enumerate(STEPS_FAR):
            dest = lax.rem(z + (a + b + head_count), head_count)
            at = pl.ds(pl.multiple_of(dest * row_share, row_share), row_share)
            rows = jnp.concatenate([acc_k[:, at, :], acc_v[:, at, :]], axis=2)
            rows_refs[i][j] = rows.reshape(block_count * row_share, 2 * head_dim).astype(jnp.bfloat16)
    rows_all[:, :head_dim] = acc_k[...].reshape(-1, head_dim).astype(jnp.bfloat16)
    rows_all[:, head_dim:] = acc_v[...].reshape(-1, head_dim).astype(jnp.bfloat16)
    room = (stage.shape[1] - parts) // 2
    group = 8

    def weigh(i, _):
        at = pl.multiple_of(i * (group * room), group * room)
        term = nn_dot(enc_t_ref[pl.ds(at, group * room)], rows_all[...]).astype(jnp.bfloat16)
        term = term.reshape(group, room, 2 * head_dim)
        for g in range(group):
            stage[i * group + g, parts:parts + room] = term[g, :, :head_dim]
            stage[i * group + g, parts + room:] = term[g, :, head_dim:]
            leave(i * group + g).start()
        return 0

    lax.fori_loop(0, seq_count // group, weigh, 0)

    def left_all(s, _):
        leave(s).wait()
        return 0

    lax.fori_loop(0, seq_count, left_all, 0)


def finish_kernel(slots_ref, in_ref, att_ref, qg_ref, kw_ref, vw_ref):
    share = kw_ref.shape[0]
    parts = 2 * CAP * SEGMENT
    room = (in_ref.shape[1] - parts) // 2

    def step(c, _):
        slot_a, slot_b = slots_ref[NEIGH * c], slots_ref[NEIGH * c + 1]

        def part(slot):
            holder = lax.div(slot, CAP)
            row = pl.multiple_of((slot - holder * CAP) * 2 * SEGMENT, 2 * SEGMENT)
            return in_ref[holder, pl.ds(row, 2 * SEGMENT), :].astype(jnp.float32)

        total = (part(slot_a) + part(slot_b)).astype(jnp.bfloat16)
        att_ref[c] = total[:SEGMENT]
        qg_ref[c] = total[SEGMENT:]
        return 0

    lax.fori_loop(0, att_ref.shape[0], step, 0, unroll=2)
    total = in_ref[0, parts:, :].astype(jnp.float32)
    for s in range(1, in_ref.shape[0]):
        total = total + in_ref[s, parts:, :].astype(jnp.float32)
    kw_ref[...] = total[:share]
    vw_ref[...] = total[room:room + share]


def project_kernel(*refs):
    near = len(STEPS_NEAR)
    rows_refs, weight_refs, own_ref, far_refs = refs[:near], refs[near:2 * near], refs[2 * near], refs[2 * near + 1:]
    far, rows, width = rows_refs[0].shape
    half = far // 2
    for i in range(0, far, half):
        total = jnp.zeros((half * rows, own_ref.shape[1]), jnp.float32)
        for rows_ref, weight_ref in zip(rows_refs, weight_refs):
            total = total + nt_dot(rows_ref[i:i + half].reshape(half * rows, width), weight_ref[...])
        for j in range(half):
            part = total[j * rows:(j + 1) * rows]
            if i + j == 0:
                own_ref[...] = part
            else:
                far_refs[i + j - 1][...] = part.astype(jnp.bfloat16)


def shifted(x, step, count):
    return lax.ppermute(x, "head", [(z, (z + step) % count) for z in range(count)])


def on_device(queries, encodings, key_weight, value_weight, reads, out_grad):
    seq_count = lax.axis_size("seq")
    head_count = lax.axis_size("head")
    me = lax.axis_index("seq")
    block_count, block_len, enc_width = encodings.shape
    head_dim = key_weight.shape[1]
    segments = queries.shape[0] // SEGMENT
    read_count = NEIGH * segments
    slot_count = seq_count * CAP
    scale = 1.0 / math.sqrt(head_dim)
    bf16, f32 = jnp.bfloat16, jnp.float32

    tables = reads.reshape(seq_count, read_count)
    my_reads = lax.dynamic_index_in_dim(tables, me, 0, keepdims=False)
    packed, slots = pl.pallas_call(
        lambda *refs: pack_kernel(block_count, *refs),
        out_shape=(
            jax.ShapeDtypeStruct((slot_count, 2, SEGMENT, head_dim), bf16),
            jax.ShapeDtypeStruct((read_count,), jnp.int32),
        ),
        in_specs=[spec(SMEM), spec(pl.ANY), spec(pl.ANY)],
        out_specs=(spec(pl.ANY), spec(SMEM)),
        scratch_shapes=[
            pltpu.SMEM((seq_count,), jnp.int32),
            pltpu.VMEM((2, SEGMENT, head_dim), bf16),
            pltpu.SemaphoreType.DMA((read_count, 2)),
            pltpu.SemaphoreType.DMA((slot_count,)),
        ],
        compiler_params=params(),
        name="pack",
    )(
        my_reads,
        queries.reshape(segments, SEGMENT, head_dim),
        out_grad.reshape(segments, SEGMENT, head_dim),
    )
    arrived = lax.all_to_all(packed, "seq", split_axis=0, concat_axis=0, tiled=True)

    weights = jnp.concatenate([key_weight, value_weight], axis=1)
    near_weights = [weights if a == 0 else shifted(weights, a, head_count) for a in STEPS_NEAR]
    flat_enc = encodings.reshape(block_count * block_len, enc_width)
    kv = jnp.dot(flat_enc, weights, preferred_element_type=f32).astype(bf16)
    kv = kv.reshape(block_count, block_len, 2 * head_dim)
    share = enc_width // seq_count
    room = -(-share // 16) * 16
    enc_t = jnp.pad(flat_enc.T.reshape(seq_count, share, -1), ((0, 0), (0, room - share), (0, 0)))
    enc_t = enc_t.reshape(seq_count * room, block_count * block_len)

    mine = (tables // block_count) == me
    rank = jnp.cumsum(mine.astype(jnp.int32), axis=1)
    blocks = jnp.stack(
        [
            jnp.sum(jnp.where(mine & (rank == k + 1), tables % block_count, 0), axis=1)
            for k in range(CAP)
        ],
        axis=1,
    ).reshape(slot_count)
    kv, enc_t, blocks, *near_weights = lax.optimization_barrier((kv, enc_t, blocks, *near_weights))

    stats = pl.pallas_call(
        lambda *refs: stats_kernel(scale, 2, *refs),
        out_shape=jax.ShapeDtypeStruct((slot_count, 2, CAP * SEGMENT), f32),
        in_specs=[spec(SMEM), spec(VMEM), spec(VMEM)],
        out_specs=spec(VMEM),
        compiler_params=params(),
        name="stats",
    )(blocks, arrived, kv)
    stats = lax.all_to_all(stats, "seq", split_axis=0, concat_axis=0, tiled=True)
    merged = pl.pallas_call(
        merge_kernel,
        out_shape=jax.ShapeDtypeStruct(stats.shape, f32),
        in_specs=[spec(SMEM), spec(VMEM)],
        out_specs=spec(VMEM),
        compiler_params=params(),
        name="merge",
    )(slots, stats)
    merged = lax.all_to_all(merged, "seq", split_axis=0, concat_axis=0, tiled=True)

    row_share = block_len // head_count
    rows = block_count * row_share
    near, far = len(STEPS_NEAR), len(STEPS_FAR)
    back_shape = (seq_count, 2 * CAP * SEGMENT + 2 * room, head_dim)
    back, *near_rows = pl.pallas_call(
        lambda *refs: grads_kernel(scale, 2, *refs),
        out_shape=(
            jax.ShapeDtypeStruct(back_shape, bf16),
            *[jax.ShapeDtypeStruct((far, rows, 2 * head_dim), bf16)] * near,
        ),
        in_specs=[spec(SMEM), spec(SMEM), spec(VMEM), spec(VMEM), spec(VMEM), spec(VMEM)],
        out_specs=(spec(pl.ANY), *[spec(VMEM)] * near),
        scratch_shapes=[
            pltpu.VMEM(back_shape, bf16),
            pltpu.VMEM((block_count * block_len, 2 * head_dim), bf16),
            pltpu.VMEM((block_count, block_len, head_dim), f32),
            pltpu.VMEM((block_count, block_len, head_dim), f32),
            pltpu.SemaphoreType.DMA((seq_count,)),
        ],
        compiler_params=params(),
        name="grads",
    )(lax.axis_index("head").astype(jnp.int32).reshape(1), blocks, arrived, kv, merged, enc_t)

    returned = lax.all_to_all(back, "seq", split_axis=0, concat_axis=0, tiled=True)
    near_rows = [r if a == 0 else shifted(r, a, head_count) for a, r in zip(STEPS_NEAR, near_rows)]
    own, *far_sums = pl.pallas_call(
        project_kernel,
        out_shape=(
            jax.ShapeDtypeStruct((rows, enc_width), f32),
            *[jax.ShapeDtypeStruct((rows, enc_width), bf16)] * (far - 1),
        ),
        in_specs=[spec(VMEM)] * (2 * near),
        out_specs=(spec(VMEM),) * far,
        compiler_params=params(),
        name="project",
    )(*near_rows, *near_weights)
    encoding_grad = own
    for b, part in zip(STEPS_FAR[1:], far_sums):
        encoding_grad = encoding_grad + shifted(part, b, head_count).astype(f32)

    attended, query_grad, key_weight_grad, value_weight_grad = pl.pallas_call(
        finish_kernel,
        out_shape=(
            jax.ShapeDtypeStruct((segments, SEGMENT, head_dim), bf16),
            jax.ShapeDtypeStruct((segments, SEGMENT, head_dim), bf16),
            jax.ShapeDtypeStruct((share, head_dim), f32),
            jax.ShapeDtypeStruct((share, head_dim), f32),
        ),
        in_specs=[spec(SMEM), spec(VMEM)],
        out_specs=(spec(VMEM),) * 4,
        compiler_params=params(),
        name="finish",
    )(slots, returned)
    return (
        attended.reshape(segments * SEGMENT, head_dim),
        query_grad.reshape(segments * SEGMENT, head_dim),
        encoding_grad.reshape(block_count, row_share, enc_width),
        key_weight_grad,
        value_weight_grad,
    )


def solution(mesh):
    in_specs = (
        P("seq", "head"),
        P("seq", None, None),
        P(None, "head"),
        P(None, "head"),
        P(),
        P("seq", "head"),
    )
    out_specs = (
        P("seq", "head"),
        P("seq", "head"),
        P("seq", "head", None),
        P("seq", "head"),
        P("seq", "head"),
    )
    return jax.shard_map(
        on_device, mesh=mesh, in_specs=in_specs, out_specs=out_specs, check_vma=False
    )
```

```python
import math

import jax
import jax.numpy as jnp
from jax import lax
from jax.experimental import pallas as pl
from jax.experimental.pallas import tpu as pltpu
from jax.sharding import PartitionSpec as P

SEGMENT = 64
NEIGH = 2
CAP = 2
NEAR = 4
FAR = (0, 4, -4, 8)
VMEM_LIMIT = 40 * 1024 * 1024
PACK_LIMIT = 60 * 1024 * 1024
VMEM = pltpu.VMEM
SMEM = pltpu.SMEM
HBM = pltpu.HBM


def params(limit=VMEM_LIMIT):
    return pltpu.CompilerParams(vmem_limit_bytes=limit)


def spec(space):
    return pl.BlockSpec(memory_space=space)


def nt_dot(a, b):
    return lax.dot_general(a, b, (((1,), (1,)), ((), ())), preferred_element_type=jnp.float32)


def tn_dot(a, b):
    return lax.dot_general(a, b, (((0,), (0,)), ((), ())), preferred_element_type=jnp.float32)


def nn_dot(a, b):
    return jnp.dot(a, b, preferred_element_type=jnp.float32)


def pack_kernel(block_count, reads_ref, q_ref, g_ref, out_ref, slots_ref, used, stage, sem):
    seq_count = used.shape[0]
    read_count = slots_ref.shape[0]
    first = lax.axis_index("seq") * (read_count // NEIGH)

    def leave(slot):
        pltpu.make_async_copy(stage.at[slot], out_ref.at[slot], sem).start()

    for h in range(seq_count):
        used[h] = 0
    for j in range(read_count):
        holder = lax.div(reads_ref[j % NEIGH, first + j // NEIGH], block_count)
        rank = used[holder]
        used[holder] = rank + 1
        slot = holder * CAP + rank
        slots_ref[j] = slot
        stage[slot, 0] = q_ref[j // NEIGH]
        stage[slot, 1] = g_ref[j // NEIGH]
        leave(slot)

    def blank(h, _):
        for k in range(CAP):
            @pl.when(used[h] <= k)
            def _():
                stage[h * CAP + k] = jnp.zeros(stage.shape[1:], stage.dtype)
                leave(h * CAP + k)

        return 0

    lax.fori_loop(0, seq_count, blank, 0)
    pltpu.make_async_copy(stage, out_ref, sem).wait()


def pair_operands(x_ref, s, kv_a, kv_b):
    head_dim = x_ref.shape[3]

    def diagonal(i):
        one, two = x_ref[CAP * s, i], x_ref[CAP * s + 1, i]
        zero = jnp.zeros_like(one)
        return jnp.concatenate(
            [jnp.concatenate([one, zero], axis=1), jnp.concatenate([zero, two], axis=1)], axis=0
        )

    keys = jnp.concatenate([kv_a[:, :head_dim], kv_b[:, :head_dim]], axis=1)
    values = jnp.concatenate([kv_a[:, head_dim:], kv_b[:, head_dim:]], axis=1)
    return diagonal(0), diagonal(1), keys, values


def stats_kernel(scale, unroll, blocks_ref, x_ref, kv_ref, out_ref):
    def step(s, _):
        kv_a = kv_ref[blocks_ref[CAP * s]]
        kv_b = kv_ref[blocks_ref[CAP * s + 1]]
        q_diag, g_diag, keys, values = pair_operands(x_ref, s, kv_a, kv_b)
        scores = nt_dot(keys, q_diag) * scale
        top = jnp.max(scores, axis=0, keepdims=True)
        weight = jnp.exp(scores - top)
        total = jnp.sum(weight, axis=0, keepdims=True)
        prob_grad = nt_dot(values, g_diag)
        mean = jnp.sum(weight * prob_grad, axis=0, keepdims=True) / total
        both = jnp.concatenate([top + jnp.log(total), mean], axis=0)
        out_ref[CAP * s] = both
        out_ref[CAP * s + 1] = pltpu.roll(both, SEGMENT, 1)
        return 0

    lax.fori_loop(0, x_ref.shape[0] // CAP, step, 0, unroll=unroll)


def merge_kernel(slots_ref, in_ref, out_ref):
    out_ref[...] = jnp.zeros_like(out_ref)
    for c in range(slots_ref.shape[0] // NEIGH):
        slot_a, slot_b = slots_ref[NEIGH * c], slots_ref[NEIGH * c + 1]
        one, two = in_ref[slot_a], in_ref[slot_b]
        lse_a, lse_b = one[0:1], two[0:1]
        top = jnp.maximum(lse_a, lse_b)
        lse = top + jnp.log(jnp.exp(lse_a - top) + jnp.exp(lse_b - top))
        delta = jnp.exp(lse_a - lse) * one[1:2] + jnp.exp(lse_b - lse) * two[1:2]
        both = jnp.concatenate([lse, delta], axis=0)
        out_ref[slot_a] = both
        out_ref[slot_b] = both


def grads_kernel(scale, group, blocks_ref, x_ref, kv_ref, stats_ref, enc_hbm, *refs):
    near = NEAR
    out_ref = refs[0]
    rows_refs = refs[1:1 + near]
    stage, enc_t, rows_all, rows_near, acc_k, acc_v, enc_sem, rows_sems, out_sem = refs[1 + near:]
    head_dim = kv_ref.shape[2] // 2
    seq_count = x_ref.shape[0] // CAP
    pair = CAP * SEGMENT
    parts = 2 * pair
    fetch = pltpu.make_async_copy(enc_hbm, enc_t, enc_sem)
    fetch.start()
    acc_k[...] = jnp.zeros_like(acc_k)
    acc_v[...] = jnp.zeros_like(acc_v)
    left = lax.broadcasted_iota(jnp.int32, (2, pair), 1) < SEGMENT

    def step(i, _):
        sources = [i * group + g for g in range(group)]
        first = [blocks_ref[CAP * s] for s in sources]
        second = [blocks_ref[CAP * s + 1] for s in sources]
        operands = [
            pair_operands(x_ref, s, kv_ref[a], kv_ref[b]) for s, a, b in zip(sources, first, second)
        ]
        stats = [
            jnp.where(left, stats_ref[CAP * s], pltpu.roll(stats_ref[CAP * s + 1], SEGMENT, 1))
            for s in sources
        ]
        scores = [nt_dot(keys, q) * scale for q, _, keys, _ in operands]
        prob_grads = [nt_dot(values, g) for _, g, _, values in operands]
        probs = [jnp.exp(x - stat[0:1]) for x, stat in zip(scores, stats)]
        score_grads = [
            (p * (x - stat[1:2]) * scale).astype(jnp.bfloat16)
            for p, x, stat in zip(probs, prob_grads, stats)
        ]
        probs = [p.astype(jnp.bfloat16) for p in probs]
        attended = [tn_dot(p, ops[3]).astype(jnp.bfloat16) for p, ops in zip(probs, operands)]
        query_grads = [tn_dot(x, ops[2]).astype(jnp.bfloat16) for x, ops in zip(score_grads, operands)]
        value_parts = [nn_dot(p, ops[1]) for p, ops in zip(probs, operands)]
        key_parts = [nn_dot(x, ops[0]) for x, ops in zip(score_grads, operands)]
        for s, att, grad in zip(sources, attended, query_grads):
            stage[s, :SEGMENT] = att[:SEGMENT, :head_dim]
            stage[s, SEGMENT:pair] = grad[:SEGMENT, :head_dim]
            stage[s, pair:pair + SEGMENT] = att[SEGMENT:, head_dim:]
            stage[s, pair + SEGMENT:parts] = grad[SEGMENT:, head_dim:]
        for a, b, key_part, value_part in zip(first, second, key_parts, value_parts):
            acc_k[a] += key_part[:, :head_dim]
            acc_v[a] += value_part[:, :head_dim]
            acc_k[b] += key_part[:, head_dim:]
            acc_v[b] += value_part[:, head_dim:]
        at = pl.ds(i * group, group)
        pltpu.make_async_copy(stage.at[at, :parts], out_ref.at[at, :parts], out_sem).start()
        return 0

    lax.fori_loop(0, seq_count // group, step, 0)
    head_count = near * len(FAR)
    block_count, block_len, _ = acc_k.shape
    row_share = block_len // head_count
    z = lax.axis_index("head")
    rows_copies = []
    for i in range(near):
        partner = lax.bitwise_xor(z, i)
        for j, b in enumerate(FAR):
            dest = lax.rem(partner + (b + head_count), head_count)
            at = pl.ds(pl.multiple_of(dest * row_share, row_share), row_share)
            rows = jnp.concatenate([acc_k[:, at, :], acc_v[:, at, :]], axis=2)
            rows_near[i, j] = rows.reshape(block_count * row_share, 2 * head_dim).astype(jnp.bfloat16)
        rows_copies.append(pltpu.make_async_copy(rows_near.at[i], rows_refs[i], rows_sems.at[i]))
        rows_copies[i].start()
    rows_all[:, :head_dim] = acc_k[...].reshape(-1, head_dim).astype(jnp.bfloat16)
    rows_all[:, head_dim:] = acc_v[...].reshape(-1, head_dim).astype(jnp.bfloat16)
    room = (stage.shape[1] - parts) // 2
    share = enc_t.shape[0] // seq_count
    fetch.wait()
    batch = 8
    for i in range(0, seq_count, batch):
        term = nn_dot(enc_t[i * share:(i + batch) * share], rows_all[...])
        for s in range(batch):
            part = term[s * share:(s + 1) * share]
            if room > share:
                part = jnp.concatenate([part, jnp.zeros((room - share, 2 * head_dim), jnp.float32)], axis=0)
            part = part.astype(jnp.bfloat16)
            stage[i + s, parts:parts + room] = part[:, :head_dim]
            stage[i + s, parts + room:] = part[:, head_dim:]
        pltpu.make_async_copy(
            stage.at[i:i + batch, parts:], out_ref.at[i:i + batch, parts:], out_sem
        ).start()
    for copy in rows_copies:
        copy.wait()
    pltpu.make_async_copy(stage, out_ref, out_sem).wait()


def finish_kernel(slots_ref, in_ref, att_ref, qg_ref, kw_ref, vw_ref):
    share = kw_ref.shape[0]
    parts = 2 * CAP * SEGMENT
    room = (in_ref.shape[1] - parts) // 2

    def step(c, _):
        slot_a, slot_b = slots_ref[NEIGH * c], slots_ref[NEIGH * c + 1]

        def part(slot):
            holder = lax.div(slot, CAP)
            row = pl.multiple_of((slot - holder * CAP) * 2 * SEGMENT, 2 * SEGMENT)
            return in_ref[holder, pl.ds(row, 2 * SEGMENT), :].astype(jnp.float32)

        total = (part(slot_a) + part(slot_b)).astype(jnp.bfloat16)
        att_ref[c] = total[:SEGMENT]
        qg_ref[c] = total[SEGMENT:]
        return 0

    lax.fori_loop(0, att_ref.shape[0], step, 0, unroll=2)
    total = in_ref[0, parts:, :].astype(jnp.float32)
    for s in range(1, in_ref.shape[0]):
        total = total + in_ref[s, parts:, :].astype(jnp.float32)
    kw_ref[...] = total[:share]
    vw_ref[...] = total[room:room + share]


def project_kernel(weights_ref, *refs):
    rows_refs, own_ref, far_refs = refs[:NEAR], refs[NEAR], refs[NEAR + 1:]
    far, rows, width = rows_refs[0].shape
    place = lax.rem(lax.axis_index("head"), NEAR)
    half = far // 2
    for i in range(0, far, half):
        total = jnp.zeros((half * rows, own_ref.shape[1]), jnp.float32)
        for n, rows_ref in enumerate(rows_refs):
            weight = weights_ref[lax.bitwise_xor(place, n)]
            total = total + nt_dot(rows_ref[i:i + half].reshape(half * rows, width), weight)
        for j in range(half):
            part = total[j * rows:(j + 1) * rows]
            if i + j == 0:
                own_ref[...] = part
            else:
                far_refs[i + j - 1][...] = part.astype(jnp.bfloat16)


def moved(x, target):
    return lax.ppermute(x, "head", [(z, target(z)) for z in range(lax.axis_size("head"))])


def on_device(queries, encodings, key_weight, value_weight, reads, out_grad):
    seq_count = lax.axis_size("seq")
    head_count = lax.axis_size("head")
    me = lax.axis_index("seq")
    block_count, block_len, enc_width = encodings.shape
    head_dim = key_weight.shape[1]
    segments = queries.shape[0] // SEGMENT
    read_count = NEIGH * segments
    slot_count = seq_count * CAP
    scale = 1.0 / math.sqrt(head_dim)
    bf16, f32 = jnp.bfloat16, jnp.float32

    packed, slots = pl.pallas_call(
        lambda *refs: pack_kernel(block_count, *refs),
        out_shape=(
            jax.ShapeDtypeStruct((slot_count, 2, SEGMENT, head_dim), bf16),
            jax.ShapeDtypeStruct((read_count,), jnp.int32),
        ),
        in_specs=[spec(SMEM), spec(VMEM), spec(VMEM)],
        out_specs=(spec(HBM), spec(SMEM)),
        scratch_shapes=[
            pltpu.SMEM((seq_count,), jnp.int32),
            pltpu.VMEM((slot_count, 2, SEGMENT, head_dim), bf16),
            pltpu.SemaphoreType.DMA,
        ],
        compiler_params=params(PACK_LIMIT),
        name="pack",
    )(
        reads.T,
        queries.reshape(segments, SEGMENT, head_dim),
        out_grad.reshape(segments, SEGMENT, head_dim),
    )
    arrived = lax.all_to_all(packed, "seq", split_axis=0, concat_axis=0, tiled=True)

    key_weight, value_weight, slots = lax.optimization_barrier((key_weight, value_weight, slots))
    weights = jnp.concatenate([key_weight, value_weight], axis=1)
    groups = [list(range(z, z + NEAR)) for z in range(0, head_count, NEAR)]
    near_weights = lax.all_gather(weights, "head", axis_index_groups=groups)
    flat_enc = encodings.reshape(block_count * block_len, enc_width)
    kv = jnp.dot(flat_enc, weights, preferred_element_type=f32).astype(bf16)
    kv = kv.reshape(block_count, block_len, 2 * head_dim)
    share = enc_width // seq_count
    room = -(-share // 16) * 16
    enc_t = flat_enc.T

    tables = reads.reshape(seq_count, read_count)
    mine = (tables // block_count) == me
    rank = jnp.cumsum(mine.astype(jnp.int32), axis=1)
    blocks = jnp.stack(
        [
            jnp.sum(jnp.where(mine & (rank == k + 1), tables % block_count, 0), axis=1)
            for k in range(CAP)
        ],
        axis=1,
    ).reshape(slot_count)
    kv, enc_t, blocks = lax.optimization_barrier((kv, enc_t, blocks))

    stats = pl.pallas_call(
        lambda *refs: stats_kernel(scale, seq_count, *refs),
        out_shape=jax.ShapeDtypeStruct((slot_count, 2, CAP * SEGMENT), f32),
        in_specs=[spec(SMEM), spec(VMEM), spec(VMEM)],
        out_specs=spec(VMEM),
        compiler_params=params(),
        name="stats",
    )(blocks, arrived, kv)
    stats = lax.all_to_all(stats, "seq", split_axis=0, concat_axis=0, tiled=True)
    merged = pl.pallas_call(
        merge_kernel,
        out_shape=jax.ShapeDtypeStruct(stats.shape, f32),
        in_specs=[spec(SMEM), spec(VMEM)],
        out_specs=spec(VMEM),
        compiler_params=params(),
        name="merge",
    )(slots, stats)
    merged = lax.all_to_all(merged, "seq", split_axis=0, concat_axis=0, tiled=True)

    row_share = block_len // head_count
    rows = block_count * row_share
    near, far = NEAR, len(FAR)
    back_shape = (seq_count, 2 * CAP * SEGMENT + 2 * room, head_dim)
    back, *near_rows = pl.pallas_call(
        lambda *refs: grads_kernel(scale, 8, *refs),
        out_shape=(
            jax.ShapeDtypeStruct(back_shape, bf16),
            *[jax.ShapeDtypeStruct((far, rows, 2 * head_dim), bf16)] * near,
        ),
        in_specs=[spec(SMEM), spec(VMEM), spec(VMEM), spec(VMEM), spec(HBM)],
        out_specs=(spec(HBM), *[spec(HBM)] * near),
        scratch_shapes=[
            pltpu.VMEM(back_shape, bf16),
            pltpu.VMEM((enc_width, block_count * block_len), bf16),
            pltpu.VMEM((block_count * block_len, 2 * head_dim), bf16),
            pltpu.VMEM((near, far, rows, 2 * head_dim), bf16),
            pltpu.VMEM((block_count, block_len, head_dim), f32),
            pltpu.VMEM((block_count, block_len, head_dim), f32),
            pltpu.SemaphoreType.DMA,
            pltpu.SemaphoreType.DMA((near,)),
            pltpu.SemaphoreType.DMA,
        ],
        compiler_params=params(),
        name="grads",
    )(blocks, arrived, kv, merged, enc_t)

    returned = lax.all_to_all(back, "seq", split_axis=0, concat_axis=0, tiled=True)
    near_rows = [r if n == 0 else moved(r, lambda z: z ^ n) for n, r in enumerate(near_rows)]
    own, *far_sums = pl.pallas_call(
        project_kernel,
        out_shape=(
            jax.ShapeDtypeStruct((rows, enc_width), f32),
            *[jax.ShapeDtypeStruct((rows, enc_width), bf16)] * (far - 1),
        ),
        in_specs=[spec(VMEM)] * (1 + near),
        out_specs=(spec(VMEM),) * far,
        compiler_params=params(),
        name="project",
    )(near_weights, *near_rows)
    encoding_grad = own
    for b, part in zip(FAR[1:], far_sums):
        encoding_grad = encoding_grad + moved(part, lambda z: (z + b) % head_count).astype(f32)

    attended, query_grad, key_weight_grad, value_weight_grad = pl.pallas_call(
        finish_kernel,
        out_shape=(
            jax.ShapeDtypeStruct((segments, SEGMENT, head_dim), bf16),
            jax.ShapeDtypeStruct((segments, SEGMENT, head_dim), bf16),
            jax.ShapeDtypeStruct((share, head_dim), f32),
            jax.ShapeDtypeStruct((share, head_dim), f32),
        ),
        in_specs=[spec(SMEM), spec(VMEM)],
        out_specs=(spec(VMEM),) * 4,
        compiler_params=params(),
        name="finish",
    )(slots, returned)
    return (
        attended.reshape(segments * SEGMENT, head_dim),
        query_grad.reshape(segments * SEGMENT, head_dim),
        encoding_grad.reshape(block_count, row_share, enc_width),
        key_weight_grad,
        value_weight_grad,
    )


def solution(mesh):
    in_specs = (
        P("seq", "head"),
        P("seq", None, None),
        P(None, "head"),
        P(None, "head"),
        P(),
        P("seq", "head"),
    )
    out_specs = (
        P("seq", "head"),
        P("seq", "head"),
        P("seq", "head", None),
        P("seq", "head"),
        P("seq", "head"),
    )
    return jax.shard_map(
        on_device, mesh=mesh, in_specs=in_specs, out_specs=out_specs, check_vma=False
    )
```

```python
import math

import jax
import jax.numpy as jnp
from jax import lax
from jax.experimental import pallas as pl
from jax.experimental.pallas import tpu as pltpu
from jax.sharding import PartitionSpec as P

SEGMENT = 64
NEIGH = 2
CAP = 2
NEAR = (0, 1, -1, 2)
FAR = (0, 4, -4, 8)
LANES = 128
VMEM_LIMIT = 40 * 1024 * 1024
LARGE_LIMIT = 60 * 1024 * 1024
VMEM = pltpu.VMEM
SMEM = pltpu.SMEM
HBM = pltpu.HBM


def params(limit=VMEM_LIMIT):
    return pltpu.CompilerParams(vmem_limit_bytes=limit)


def spec(space):
    return pl.BlockSpec(memory_space=space)


def nt_dot(a, b):
    return lax.dot_general(a, b, (((1,), (1,)), ((), ())), preferred_element_type=jnp.float32)


def tn_dot(a, b):
    return lax.dot_general(a, b, (((0,), (0,)), ((), ())), preferred_element_type=jnp.float32)


def nn_dot(a, b):
    return jnp.dot(a, b, preferred_element_type=jnp.float32)


def pack_kernel(block_count, reads_ref, q_ref, g_ref, out_ref, slots_ref, used, stage, sem):
    seq_count = used.shape[0]
    read_count = slots_ref.shape[0]
    first = lax.axis_index("seq") * (read_count // NEIGH)

    def leave(slot):
        pltpu.make_async_copy(stage.at[slot], out_ref.at[slot], sem).start()

    for h in range(seq_count):
        used[h] = 0
    for j in range(read_count):
        holder = lax.div(reads_ref[j % NEIGH, first + j // NEIGH], block_count)
        rank = used[holder]
        used[holder] = rank + 1
        slot = holder * CAP + rank
        slots_ref[j] = slot
        stage[slot, 0] = q_ref[j // NEIGH]
        stage[slot, 1] = g_ref[j // NEIGH]
        leave(slot)

    def blank(h, _):
        for k in range(CAP):
            @pl.when(used[h] <= k)
            def _():
                stage[h * CAP + k] = jnp.zeros(stage.shape[1:], stage.dtype)
                leave(h * CAP + k)

        return 0

    lax.fori_loop(0, seq_count, blank, 0)
    pltpu.make_async_copy(stage, out_ref, sem).wait()


def pair_operands(x_ref, s, kv_a, kv_b):
    head_dim = x_ref.shape[3]

    def diagonal(i):
        one, two = x_ref[CAP * s, i], x_ref[CAP * s + 1, i]
        zero = jnp.zeros_like(one)
        return jnp.concatenate(
            [jnp.concatenate([one, zero], axis=1), jnp.concatenate([zero, two], axis=1)], axis=0
        )

    keys = jnp.concatenate([kv_a[:, :head_dim], kv_b[:, :head_dim]], axis=1)
    values = jnp.concatenate([kv_a[:, head_dim:], kv_b[:, head_dim:]], axis=1)
    return diagonal(0), diagonal(1), keys, values


def stats_kernel(scale, unroll, blocks_ref, x_ref, kv_ref, out_ref):
    def step(s, _):
        kv_a = kv_ref[blocks_ref[CAP * s]]
        kv_b = kv_ref[blocks_ref[CAP * s + 1]]
        q_diag, g_diag, keys, values = pair_operands(x_ref, s, kv_a, kv_b)
        scores = nt_dot(keys, q_diag) * scale
        top = jnp.max(scores, axis=0, keepdims=True)
        weight = jnp.exp(scores - top)
        total = jnp.sum(weight, axis=0, keepdims=True)
        prob_grad = nt_dot(values, g_diag)
        mean = jnp.sum(weight * prob_grad, axis=0, keepdims=True) / total
        both = jnp.concatenate([top + jnp.log(total), mean], axis=0)
        out_ref[CAP * s] = both
        out_ref[CAP * s + 1] = pltpu.roll(both, SEGMENT, 1)
        return 0

    lax.fori_loop(0, x_ref.shape[0] // CAP, step, 0, unroll=unroll)


def merge_kernel(slots_ref, in_ref, out_ref):
    out_ref[...] = jnp.zeros_like(out_ref)
    for c in range(slots_ref.shape[0] // NEIGH):
        slot_a, slot_b = slots_ref[NEIGH * c], slots_ref[NEIGH * c + 1]
        one, two = in_ref[slot_a], in_ref[slot_b]
        lse_a, lse_b = one[0:1], two[0:1]
        top = jnp.maximum(lse_a, lse_b)
        lse = top + jnp.log(jnp.exp(lse_a - top) + jnp.exp(lse_b - top))
        delta = jnp.exp(lse_a - lse) * one[1:2] + jnp.exp(lse_b - lse) * two[1:2]
        both = jnp.concatenate([lse, delta], axis=0)
        out_ref[slot_a] = both
        out_ref[slot_b] = both


def grads_kernel(scale, group, blocks_ref, x_hbm, kv_ref, stats_ref, enc_hbm, *refs):
    near = len(NEAR)
    out_ref = refs[0]
    rows_refs = refs[1:1 + near]
    x_ref, stage, enc_t, rows_all, rows_near, acc_k, acc_v, x_sems, enc_sem, rows_sems, out_sem = refs[1 + near:]
    head_dim = kv_ref.shape[2] // 2
    seq_count = x_ref.shape[0] // CAP
    pair = CAP * SEGMENT
    parts = 2 * pair

    def arrival(i):
        at = pl.ds(i * group * CAP, group * CAP)
        return pltpu.make_async_copy(x_hbm.at[at], x_ref.at[at], x_sems.at[i])

    for i in range(seq_count // group):
        arrival(i).start()
    fetch = pltpu.make_async_copy(enc_hbm, enc_t, enc_sem)
    fetch.start()
    acc_k[...] = jnp.zeros_like(acc_k)
    acc_v[...] = jnp.zeros_like(acc_v)
    left = lax.broadcasted_iota(jnp.int32, (2, pair), 1) < SEGMENT

    def step(i, _):
        arrival(i).wait()
        sources = [i * group + g for g in range(group)]
        first = [blocks_ref[CAP * s] for s in sources]
        second = [blocks_ref[CAP * s + 1] for s in sources]
        operands = [
            pair_operands(x_ref, s, kv_ref[a], kv_ref[b]) for s, a, b in zip(sources, first, second)
        ]
        stats = [
            jnp.where(left, stats_ref[CAP * s], pltpu.roll(stats_ref[CAP * s + 1], SEGMENT, 1))
            for s in sources
        ]
        scores = [nt_dot(keys, q) * scale for q, _, keys, _ in operands]
        prob_grads = [nt_dot(values, g) for _, g, _, values in operands]
        probs = [jnp.exp(x - stat[0:1]) for x, stat in zip(scores, stats)]
        score_grads = [
            (p * (x - stat[1:2]) * scale).astype(jnp.bfloat16)
            for p, x, stat in zip(probs, prob_grads, stats)
        ]
        probs = [p.astype(jnp.bfloat16) for p in probs]
        attended = [tn_dot(p, ops[3]).astype(jnp.bfloat16) for p, ops in zip(probs, operands)]
        query_grads = [tn_dot(x, ops[2]).astype(jnp.bfloat16) for x, ops in zip(score_grads, operands)]
        value_parts = [nn_dot(p, ops[1]) for p, ops in zip(probs, operands)]
        key_parts = [nn_dot(x, ops[0]) for x, ops in zip(score_grads, operands)]
        for s, att, grad in zip(sources, attended, query_grads):
            stage[s, :SEGMENT] = att[:SEGMENT, :head_dim]
            stage[s, SEGMENT:pair] = grad[:SEGMENT, :head_dim]
            stage[s, pair:pair + SEGMENT] = att[SEGMENT:, head_dim:]
            stage[s, pair + SEGMENT:parts] = grad[SEGMENT:, head_dim:]
        for a, b, key_part, value_part in zip(first, second, key_parts, value_parts):
            acc_k[a] += key_part[:, :head_dim]
            acc_v[a] += value_part[:, :head_dim]
            acc_k[b] += key_part[:, head_dim:]
            acc_v[b] += value_part[:, head_dim:]
        at = pl.ds(i * group, group)
        pltpu.make_async_copy(stage.at[at, :parts], out_ref.at[at, :parts], out_sem).start()
        return 0

    lax.fori_loop(0, seq_count // group, step, 0)
    head_count = near * len(FAR)
    block_count, block_len, _ = acc_k.shape
    row_share = block_len // head_count
    z = lax.axis_index("head")
    rows_copies = []
    for i, a in enumerate(NEAR):
        for j, b in enumerate(FAR):
            dest = lax.rem(z + (a + b + head_count), head_count)
            at = pl.ds(pl.multiple_of(dest * row_share, row_share), row_share)
            rows = jnp.concatenate([acc_k[:, at, :], acc_v[:, at, :]], axis=2)
            rows_near[i, j] = rows.reshape(block_count * row_share, 2 * head_dim).astype(jnp.bfloat16)
        rows_copies.append(pltpu.make_async_copy(rows_near.at[i], rows_refs[i], rows_sems.at[i]))
        rows_copies[i].start()
    rows_all[:, :head_dim] = acc_k[...].reshape(-1, head_dim).astype(jnp.bfloat16)
    rows_all[:, head_dim:] = acc_v[...].reshape(-1, head_dim).astype(jnp.bfloat16)
    room = (stage.shape[1] - parts) // 2
    share = enc_t.shape[0] // seq_count
    fetch.wait()
    batch = 8
    for i in range(0, seq_count, batch):
        term = nn_dot(enc_t[i * share:(i + batch) * share], rows_all[...])
        for s in range(batch):
            part = term[s * share:(s + 1) * share]
            if room > share:
                part = jnp.concatenate([part, jnp.zeros((room - share, 2 * head_dim), jnp.float32)], axis=0)
            part = part.astype(jnp.bfloat16)
            stage[i + s, parts:parts + room] = part[:, :head_dim]
            stage[i + s, parts + room:] = part[:, head_dim:]
        pltpu.make_async_copy(
            stage.at[i:i + batch, parts:], out_ref.at[i:i + batch, parts:], out_sem
        ).start()
    for copy in rows_copies:
        copy.wait()
    pltpu.make_async_copy(stage, out_ref, out_sem).wait()


def finish_kernel(slots_ref, in_ref, att_ref, qg_ref, kw_ref, vw_ref):
    share = kw_ref.shape[0]
    parts = 2 * CAP * SEGMENT
    room = (in_ref.shape[1] - parts) // 2

    def step(c, _):
        slot_a, slot_b = slots_ref[NEIGH * c], slots_ref[NEIGH * c + 1]

        def part(slot):
            holder = lax.div(slot, CAP)
            row = pl.multiple_of((slot - holder * CAP) * 2 * SEGMENT, 2 * SEGMENT)
            return in_ref[holder, pl.ds(row, 2 * SEGMENT), :].astype(jnp.float32)

        total = (part(slot_a) + part(slot_b)).astype(jnp.bfloat16)
        att_ref[c] = total[:SEGMENT]
        qg_ref[c] = total[SEGMENT:]
        return 0

    lax.fori_loop(0, att_ref.shape[0], step, 0, unroll=2)
    total = in_ref[0, parts:, :].astype(jnp.float32)
    for s in range(1, in_ref.shape[0]):
        total = total + in_ref[s, parts:, :].astype(jnp.float32)
    kw_ref[...] = total[:share]
    vw_ref[...] = total[room:room + share]


def project_kernel(*refs):
    near = len(NEAR)
    rows_refs, weight_refs, out_refs = refs[:near], refs[near:2 * near], refs[2 * near:]
    own_ref, up_ref, down_ref, across_up_ref, across_down_ref = out_refs
    far, rows, width = rows_refs[0].shape
    cut = across_up_ref.shape[1]
    half = far // 2
    sums = []
    for i in range(0, far, half):
        total = jnp.zeros((half * rows, own_ref.shape[1]), jnp.float32)
        for rows_ref, weight_ref in zip(rows_refs, weight_refs):
            total = total + nt_dot(rows_ref[i:i + half].reshape(half * rows, width), weight_ref[...])
        sums += [total[j * rows:(j + 1) * rows] for j in range(half)]
    own_ref[...], up_ref[...], down_ref[...] = sums[:3]
    across_up_ref[...] = sums[3][:, :cut].astype(jnp.bfloat16)
    across_down_ref[...] = sums[3][:, cut:].astype(jnp.bfloat16)


def fold_kernel(up_ref, down_ref, across_up_ref, across_down_ref, up_out_ref, down_out_ref):
    cut = across_up_ref.shape[1]
    up_out_ref[:, :cut] = (up_ref[:, :cut] + across_up_ref[...].astype(jnp.float32)).astype(jnp.bfloat16)
    up_out_ref[:, cut:] = up_ref[:, cut:].astype(jnp.bfloat16)
    down_out_ref[:, :cut] = down_ref[:, :cut].astype(jnp.bfloat16)
    down_out_ref[:, cut:] = (down_ref[:, cut:] + across_down_ref[...].astype(jnp.float32)).astype(jnp.bfloat16)


def shifted(x, step):
    count = lax.axis_size("head")
    return lax.ppermute(x, "head", [(z, (z + step) % count) for z in range(count)])


def on_device(queries, encodings, key_weight, value_weight, reads, out_grad):
    seq_count = lax.axis_size("seq")
    head_count = lax.axis_size("head")
    me = lax.axis_index("seq")
    block_count, block_len, enc_width = encodings.shape
    head_dim = key_weight.shape[1]
    segments = queries.shape[0] // SEGMENT
    read_count = NEIGH * segments
    slot_count = seq_count * CAP
    scale = 1.0 / math.sqrt(head_dim)
    bf16, f32 = jnp.bfloat16, jnp.float32

    packed, slots = pl.pallas_call(
        lambda *refs: pack_kernel(block_count, *refs),
        out_shape=(
            jax.ShapeDtypeStruct((slot_count, 2, SEGMENT, head_dim), bf16),
            jax.ShapeDtypeStruct((read_count,), jnp.int32),
        ),
        in_specs=[spec(SMEM), spec(VMEM), spec(VMEM)],
        out_specs=(spec(HBM), spec(SMEM)),
        scratch_shapes=[
            pltpu.SMEM((seq_count,), jnp.int32),
            pltpu.VMEM((slot_count, 2, SEGMENT, head_dim), bf16),
            pltpu.SemaphoreType.DMA,
        ],
        compiler_params=params(LARGE_LIMIT),
        name="pack",
    )(
        reads.T,
        queries.reshape(segments, SEGMENT, head_dim),
        out_grad.reshape(segments, SEGMENT, head_dim),
    )
    arrived = lax.all_to_all(packed, "seq", split_axis=0, concat_axis=0, tiled=True)

    key_weight, value_weight, slots = lax.optimization_barrier((key_weight, value_weight, slots))
    weights = jnp.concatenate([key_weight, value_weight], axis=1)
    near_weights = [weights if a == 0 else shifted(weights, a) for a in NEAR]
    flat_enc = encodings.reshape(block_count * block_len, enc_width)
    kv = jnp.dot(flat_enc, weights, preferred_element_type=f32).astype(bf16)
    kv = kv.reshape(block_count, block_len, 2 * head_dim)
    share = enc_width // seq_count
    room = -(-share // 16) * 16
    enc_t = flat_enc.T

    tables = reads.reshape(seq_count, read_count)
    mine = (tables // block_count) == me
    rank = jnp.cumsum(mine.astype(jnp.int32), axis=1)
    blocks = jnp.stack(
        [
            jnp.sum(jnp.where(mine & (rank == k + 1), tables % block_count, 0), axis=1)
            for k in range(CAP)
        ],
        axis=1,
    ).reshape(slot_count)
    kv, enc_t, blocks = lax.optimization_barrier((kv, enc_t, blocks))

    stats = pl.pallas_call(
        lambda *refs: stats_kernel(scale, seq_count, *refs),
        out_shape=jax.ShapeDtypeStruct((slot_count, 2, CAP * SEGMENT), f32),
        in_specs=[spec(SMEM), spec(VMEM), spec(VMEM)],
        out_specs=spec(VMEM),
        compiler_params=params(),
        name="stats",
    )(blocks, arrived, kv)
    stats = lax.all_to_all(stats, "seq", split_axis=0, concat_axis=0, tiled=True)
    merged = pl.pallas_call(
        merge_kernel,
        out_shape=jax.ShapeDtypeStruct(stats.shape, f32),
        in_specs=[spec(SMEM), spec(VMEM)],
        out_specs=spec(VMEM),
        compiler_params=params(),
        name="merge",
    )(slots, stats)
    merged, *near_weights = lax.optimization_barrier((merged, *near_weights))
    merged = lax.all_to_all(merged, "seq", split_axis=0, concat_axis=0, tiled=True)

    row_share = block_len // head_count
    rows = block_count * row_share
    near, far = len(NEAR), len(FAR)
    back_shape = (seq_count, 2 * CAP * SEGMENT + 2 * room, head_dim)
    group = 8
    back, *near_rows = pl.pallas_call(
        lambda *refs: grads_kernel(scale, group, *refs),
        out_shape=(
            jax.ShapeDtypeStruct(back_shape, bf16),
            *[jax.ShapeDtypeStruct((far, rows, 2 * head_dim), bf16)] * near,
        ),
        in_specs=[spec(SMEM), spec(HBM), spec(VMEM), spec(VMEM), spec(HBM)],
        out_specs=(spec(HBM), *[spec(HBM)] * near),
        scratch_shapes=[
            pltpu.VMEM(arrived.shape, bf16),
            pltpu.VMEM(back_shape, bf16),
            pltpu.VMEM((enc_width, block_count * block_len), bf16),
            pltpu.VMEM((block_count * block_len, 2 * head_dim), bf16),
            pltpu.VMEM((near, far, rows, 2 * head_dim), bf16),
            pltpu.VMEM((block_count, block_len, head_dim), f32),
            pltpu.VMEM((block_count, block_len, head_dim), f32),
            pltpu.SemaphoreType.DMA((seq_count // group,)),
            pltpu.SemaphoreType.DMA,
            pltpu.SemaphoreType.DMA((near,)),
            pltpu.SemaphoreType.DMA,
        ],
        compiler_params=params(LARGE_LIMIT),
        name="grads",
    )(blocks, arrived, kv, merged, enc_t)

    returned = lax.all_to_all(back, "seq", split_axis=0, concat_axis=0, tiled=True)
    near_rows = [r if a == 0 else shifted(r, a) for a, r in zip(NEAR, near_rows)]
    cut = -(-enc_width // (2 * LANES)) * LANES
    step = FAR[1]
    own, up, down, across_up, across_down = pl.pallas_call(
        project_kernel,
        out_shape=(
            *[jax.ShapeDtypeStruct((rows, enc_width), f32)] * (far - 1),
            jax.ShapeDtypeStruct((rows, cut), bf16),
            jax.ShapeDtypeStruct((rows, enc_width - cut), bf16),
        ),
        in_specs=[spec(VMEM)] * (2 * near),
        out_specs=(spec(VMEM),) * (far + 1),
        compiler_params=params(),
        name="project",
    )(*near_rows, *near_weights)
    up, down = pl.pallas_call(
        fold_kernel,
        out_shape=(jax.ShapeDtypeStruct((rows, enc_width), bf16),) * 2,
        in_specs=[spec(VMEM)] * 4,
        out_specs=(spec(VMEM),) * 2,
        compiler_params=params(),
        name="fold",
    )(up, down, shifted(across_up, step), shifted(across_down, -step))
    encoding_grad = own + shifted(up, step).astype(f32) + shifted(down, -step).astype(f32)

    attended, query_grad, key_weight_grad, value_weight_grad = pl.pallas_call(
        finish_kernel,
        out_shape=(
            jax.ShapeDtypeStruct((segments, SEGMENT, head_dim), bf16),
            jax.ShapeDtypeStruct((segments, SEGMENT, head_dim), bf16),
            jax.ShapeDtypeStruct((share, head_dim), f32),
            jax.ShapeDtypeStruct((share, head_dim), f32),
        ),
        in_specs=[spec(SMEM), spec(VMEM)],
        out_specs=(spec(VMEM),) * 4,
        compiler_params=params(),
        name="finish",
    )(slots, returned)
    return (
        attended.reshape(segments * SEGMENT, head_dim),
        query_grad.reshape(segments * SEGMENT, head_dim),
        encoding_grad.reshape(block_count, row_share, enc_width),
        key_weight_grad,
        value_weight_grad,
    )


def solution(mesh):
    in_specs = (
        P("seq", "head"),
        P("seq", None, None),
        P(None, "head"),
        P(None, "head"),
        P(),
        P("seq", "head"),
    )
    out_specs = (
        P("seq", "head"),
        P("seq", "head"),
        P("seq", "head", None),
        P("seq", "head"),
        P("seq", "head"),
    )
    return jax.shard_map(
        on_device, mesh=mesh, in_specs=in_specs, out_specs=out_specs, check_vma=False
    )
```

```python
import math

import jax
import jax.numpy as jnp
from jax import lax
from jax.experimental import pallas as pl
from jax.experimental.pallas import tpu as pltpu
from jax.sharding import PartitionSpec as P

SEGMENT = 64
NEIGH = 2
CAP = 2
NEAR = (0, 1, -1, 2)
FAR = (0, 4, -4, 8)
VMEM_LIMIT = 40 * 1024 * 1024
LARGE_LIMIT = 60 * 1024 * 1024
VMEM = pltpu.VMEM
SMEM = pltpu.SMEM
HBM = pltpu.HBM


def params(limit=VMEM_LIMIT):
    return pltpu.CompilerParams(vmem_limit_bytes=limit)


def spec(space):
    return pl.BlockSpec(memory_space=space)


def nt_dot(a, b):
    return lax.dot_general(a, b, (((1,), (1,)), ((), ())), preferred_element_type=jnp.float32)


def tn_dot(a, b):
    return lax.dot_general(a, b, (((0,), (0,)), ((), ())), preferred_element_type=jnp.float32)


def nn_dot(a, b):
    return jnp.dot(a, b, preferred_element_type=jnp.float32)


def pack_kernel(block_count, reads_ref, q_ref, g_ref, out_ref, slots_ref, used, stage, sem):
    seq_count = used.shape[0]
    read_count = slots_ref.shape[0]
    first = lax.axis_index("seq") * (read_count // NEIGH)

    def leave(slot):
        pltpu.make_async_copy(stage.at[slot], out_ref.at[slot], sem).start()

    for h in range(seq_count):
        used[h] = 0
    for j in range(read_count):
        holder = lax.div(reads_ref[j % NEIGH, first + j // NEIGH], block_count)
        rank = used[holder]
        used[holder] = rank + 1
        slot = holder * CAP + rank
        slots_ref[j] = slot
        stage[slot, 0] = q_ref[j // NEIGH]
        stage[slot, 1] = g_ref[j // NEIGH]
        leave(slot)

    def blank(h, _):
        for k in range(CAP):
            @pl.when(used[h] <= k)
            def _():
                stage[h * CAP + k] = jnp.zeros(stage.shape[1:], stage.dtype)
                leave(h * CAP + k)

        return 0

    lax.fori_loop(0, seq_count, blank, 0)
    pltpu.make_async_copy(stage, out_ref, sem).wait()


def pair_operands(x_ref, s, kv_a, kv_b):
    head_dim = x_ref.shape[3]

    def diagonal(i):
        one, two = x_ref[CAP * s, i], x_ref[CAP * s + 1, i]
        zero = jnp.zeros_like(one)
        return jnp.concatenate(
            [jnp.concatenate([one, zero], axis=1), jnp.concatenate([zero, two], axis=1)], axis=0
        )

    keys = jnp.concatenate([kv_a[:, :head_dim], kv_b[:, :head_dim]], axis=1)
    values = jnp.concatenate([kv_a[:, head_dim:], kv_b[:, head_dim:]], axis=1)
    return diagonal(0), diagonal(1), keys, values


def stats_kernel(scale, unroll, blocks_ref, x_ref, kv_ref, out_ref):
    def step(s, _):
        kv_a = kv_ref[blocks_ref[CAP * s]]
        kv_b = kv_ref[blocks_ref[CAP * s + 1]]
        q_diag, g_diag, keys, values = pair_operands(x_ref, s, kv_a, kv_b)
        scores = nt_dot(keys, q_diag) * scale
        top = jnp.max(scores, axis=0, keepdims=True)
        weight = jnp.exp(scores - top)
        total = jnp.sum(weight, axis=0, keepdims=True)
        prob_grad = nt_dot(values, g_diag)
        mean = jnp.sum(weight * prob_grad, axis=0, keepdims=True) / total
        both = jnp.concatenate([top + jnp.log(total), mean], axis=0)
        out_ref[CAP * s] = both
        out_ref[CAP * s + 1] = pltpu.roll(both, SEGMENT, 1)
        return 0

    lax.fori_loop(0, x_ref.shape[0] // CAP, step, 0, unroll=unroll)


def merge_kernel(slots_ref, in_ref, out_ref):
    out_ref[...] = jnp.zeros_like(out_ref)
    for c in range(slots_ref.shape[0] // NEIGH):
        slot_a, slot_b = slots_ref[NEIGH * c], slots_ref[NEIGH * c + 1]
        one, two = in_ref[slot_a], in_ref[slot_b]
        lse_a, lse_b = one[0:1], two[0:1]
        top = jnp.maximum(lse_a, lse_b)
        lse = top + jnp.log(jnp.exp(lse_a - top) + jnp.exp(lse_b - top))
        delta = jnp.exp(lse_a - lse) * one[1:2] + jnp.exp(lse_b - lse) * two[1:2]
        both = jnp.concatenate([lse, delta], axis=0)
        out_ref[slot_a] = both
        out_ref[slot_b] = both


def grads_kernel(scale, group, blocks_ref, x_hbm, kv_ref, stats_ref, enc_hbm, *refs):
    near = len(NEAR)
    out_ref = refs[0]
    rows_refs = refs[1:1 + near]
    x_ref, stage, enc_t, rows_all, rows_near, acc_k, acc_v, x_sems, enc_sem, rows_sems, out_sem = refs[1 + near:]
    head_dim = kv_ref.shape[2] // 2
    seq_count = x_ref.shape[0] // CAP
    pair = CAP * SEGMENT
    parts = 2 * pair

    def arrival(i):
        at = pl.ds(i * group * CAP, group * CAP)
        return pltpu.make_async_copy(x_hbm.at[at], x_ref.at[at], x_sems.at[i])

    for i in range(seq_count // group):
        arrival(i).start()
    fetch = pltpu.make_async_copy(enc_hbm, enc_t, enc_sem)
    fetch.start()
    acc_k[...] = jnp.zeros_like(acc_k)
    acc_v[...] = jnp.zeros_like(acc_v)
    left = lax.broadcasted_iota(jnp.int32, (2, pair), 1) < SEGMENT

    def step(i, _):
        arrival(i).wait()
        sources = [i * group + g for g in range(group)]
        first = [blocks_ref[CAP * s] for s in sources]
        second = [blocks_ref[CAP * s + 1] for s in sources]
        operands = [
            pair_operands(x_ref, s, kv_ref[a], kv_ref[b]) for s, a, b in zip(sources, first, second)
        ]
        stats = [
            jnp.where(left, stats_ref[CAP * s], pltpu.roll(stats_ref[CAP * s + 1], SEGMENT, 1))
            for s in sources
        ]
        scores = [nt_dot(keys, q) * scale for q, _, keys, _ in operands]
        prob_grads = [nt_dot(values, g) for _, g, _, values in operands]
        probs = [jnp.exp(x - stat[0:1]) for x, stat in zip(scores, stats)]
        score_grads = [
            (p * (x - stat[1:2]) * scale).astype(jnp.bfloat16)
            for p, x, stat in zip(probs, prob_grads, stats)
        ]
        probs = [p.astype(jnp.bfloat16) for p in probs]
        attended = [tn_dot(p, ops[3]).astype(jnp.bfloat16) for p, ops in zip(probs, operands)]
        query_grads = [tn_dot(x, ops[2]).astype(jnp.bfloat16) for x, ops in zip(score_grads, operands)]
        value_parts = [nn_dot(p, ops[1]) for p, ops in zip(probs, operands)]
        key_parts = [nn_dot(x, ops[0]) for x, ops in zip(score_grads, operands)]
        for s, att, grad in zip(sources, attended, query_grads):
            stage[s, :SEGMENT] = att[:SEGMENT, :head_dim]
            stage[s, SEGMENT:pair] = grad[:SEGMENT, :head_dim]
            stage[s, pair:pair + SEGMENT] = att[SEGMENT:, head_dim:]
            stage[s, pair + SEGMENT:parts] = grad[SEGMENT:, head_dim:]
        for a, b, key_part, value_part in zip(first, second, key_parts, value_parts):
            acc_k[a] += key_part[:, :head_dim]
            acc_v[a] += value_part[:, :head_dim]
            acc_k[b] += key_part[:, head_dim:]
            acc_v[b] += value_part[:, head_dim:]
        at = pl.ds(i * group, group)
        pltpu.make_async_copy(stage.at[at, :parts], out_ref.at[at, :parts], out_sem).start()
        return 0

    lax.fori_loop(0, seq_count // group, step, 0)
    head_count = near * len(FAR)
    block_count, block_len, _ = acc_k.shape
    row_share = block_len // head_count
    z = lax.axis_index("head")
    rows_copies = []
    for i, a in enumerate(NEAR):
        for j, b in enumerate(FAR):
            dest = lax.rem(z + (a + b + head_count), head_count)
            at = pl.ds(pl.multiple_of(dest * row_share, row_share), row_share)
            rows = jnp.concatenate([acc_k[:, at, :], acc_v[:, at, :]], axis=2)
            rows_near[i, j] = rows.reshape(block_count * row_share, 2 * head_dim).astype(jnp.bfloat16)
        rows_copies.append(pltpu.make_async_copy(rows_near.at[i], rows_refs[i], rows_sems.at[i]))
        rows_copies[i].start()
    rows_all[:, :head_dim] = acc_k[...].reshape(-1, head_dim).astype(jnp.bfloat16)
    rows_all[:, head_dim:] = acc_v[...].reshape(-1, head_dim).astype(jnp.bfloat16)
    room = (stage.shape[1] - parts) // 2
    share = enc_t.shape[0] // seq_count
    fetch.wait()
    batch = 8
    for i in range(0, seq_count, batch):
        term = nn_dot(enc_t[i * share:(i + batch) * share], rows_all[...])
        for s in range(batch):
            part = term[s * share:(s + 1) * share]
            if room > share:
                part = jnp.concatenate([part, jnp.zeros((room - share, 2 * head_dim), jnp.float32)], axis=0)
            part = part.astype(jnp.bfloat16)
            stage[i + s, parts:parts + room] = part[:, :head_dim]
            stage[i + s, parts + room:] = part[:, head_dim:]
        pltpu.make_async_copy(
            stage.at[i:i + batch, parts:], out_ref.at[i:i + batch, parts:], out_sem
        ).start()
    for copy in rows_copies:
        copy.wait()
    pltpu.make_async_copy(stage, out_ref, out_sem).wait()


def finish_kernel(slots_ref, in_ref, att_ref, qg_ref, kw_ref, vw_ref):
    share = kw_ref.shape[0]
    parts = 2 * CAP * SEGMENT
    room = (in_ref.shape[1] - parts) // 2

    def step(c, _):
        slot_a, slot_b = slots_ref[NEIGH * c], slots_ref[NEIGH * c + 1]

        def part(slot):
            holder = lax.div(slot, CAP)
            row = pl.multiple_of((slot - holder * CAP) * 2 * SEGMENT, 2 * SEGMENT)
            return in_ref[holder, pl.ds(row, 2 * SEGMENT), :].astype(jnp.float32)

        total = (part(slot_a) + part(slot_b)).astype(jnp.bfloat16)
        att_ref[c] = total[:SEGMENT]
        qg_ref[c] = total[SEGMENT:]
        return 0

    lax.fori_loop(0, att_ref.shape[0], step, 0, unroll=2)
    total = in_ref[0, parts:, :].astype(jnp.float32)
    for s in range(1, in_ref.shape[0]):
        total = total + in_ref[s, parts:, :].astype(jnp.float32)
    kw_ref[...] = total[:share]
    vw_ref[...] = total[room:room + share]


def project_kernel(*refs):
    near = len(NEAR)
    rows_refs, weight_refs, own_ref, far_refs = refs[:near], refs[near:2 * near], refs[2 * near + 1], refs[2 * near + 2:-1]
    far, rows, width = rows_refs[0].shape
    half = far // 2
    for i in range(0, far, half):
        total = jnp.zeros((half * rows, own_ref.shape[1]), jnp.float32)
        for rows_ref, weight_ref in zip(rows_refs, weight_refs):
            total = total + nt_dot(rows_ref[i:i + half].reshape(half * rows, width), weight_ref[...])
        for j in range(half):
            part = total[j * rows:(j + 1) * rows]
            if i + j == 0:
                own_ref[...] = part
            else:
                far_refs[i + j - 1][...] = part.astype(jnp.bfloat16)


def shifted(x, step):
    count = lax.axis_size("head")
    return lax.ppermute(x, "head", [(z, (z + step) % count) for z in range(count)])


def on_device(queries, encodings, key_weight, value_weight, reads, out_grad):
    seq_count = lax.axis_size("seq")
    head_count = lax.axis_size("head")
    me = lax.axis_index("seq")
    block_count, block_len, enc_width = encodings.shape
    head_dim = key_weight.shape[1]
    segments = queries.shape[0] // SEGMENT
    read_count = NEIGH * segments
    slot_count = seq_count * CAP
    scale = 1.0 / math.sqrt(head_dim)
    bf16, f32 = jnp.bfloat16, jnp.float32

    packed, slots = pl.pallas_call(
        lambda *refs: pack_kernel(block_count, *refs),
        out_shape=(
            jax.ShapeDtypeStruct((slot_count, 2, SEGMENT, head_dim), bf16),
            jax.ShapeDtypeStruct((read_count,), jnp.int32),
        ),
        in_specs=[spec(SMEM), spec(VMEM), spec(VMEM)],
        out_specs=(spec(HBM), spec(SMEM)),
        scratch_shapes=[
            pltpu.SMEM((seq_count,), jnp.int32),
            pltpu.VMEM((slot_count, 2, SEGMENT, head_dim), bf16),
            pltpu.SemaphoreType.DMA,
        ],
        compiler_params=params(LARGE_LIMIT),
        name="pack",
    )(
        reads.T,
        queries.reshape(segments, SEGMENT, head_dim),
        out_grad.reshape(segments, SEGMENT, head_dim),
    )
    arrived = lax.all_to_all(packed, "seq", split_axis=0, concat_axis=0, tiled=True)

    key_weight, value_weight, slots = lax.optimization_barrier((key_weight, value_weight, slots))
    weights = jnp.concatenate([key_weight, value_weight], axis=1)
    near_weights = [weights if a == 0 else shifted(weights, a) for a in NEAR]
    flat_enc = encodings.reshape(block_count * block_len, enc_width)
    kv = jnp.dot(flat_enc, weights, preferred_element_type=f32).astype(bf16)
    kv = kv.reshape(block_count, block_len, 2 * head_dim)
    share = enc_width // seq_count
    room = -(-share // 16) * 16
    enc_t = flat_enc.T

    tables = reads.reshape(seq_count, read_count)
    mine = (tables // block_count) == me
    rank = jnp.cumsum(mine.astype(jnp.int32), axis=1)
    blocks = jnp.stack(
        [
            jnp.sum(jnp.where(mine & (rank == k + 1), tables % block_count, 0), axis=1)
            for k in range(CAP)
        ],
        axis=1,
    ).reshape(slot_count)
    kv, enc_t, blocks = lax.optimization_barrier((kv, enc_t, blocks))

    stats = pl.pallas_call(
        lambda *refs: stats_kernel(scale, seq_count, *refs),
        out_shape=jax.ShapeDtypeStruct((slot_count, 2, CAP * SEGMENT), f32),
        in_specs=[spec(SMEM), spec(VMEM), spec(VMEM)],
        out_specs=spec(VMEM),
        compiler_params=params(),
        name="stats",
    )(blocks, arrived, kv)
    stats = lax.all_to_all(stats, "seq", split_axis=0, concat_axis=0, tiled=True)
    merged = pl.pallas_call(
        merge_kernel,
        out_shape=jax.ShapeDtypeStruct(stats.shape, f32),
        in_specs=[spec(SMEM), spec(VMEM)],
        out_specs=spec(VMEM),
        compiler_params=params(),
        name="merge",
    )(slots, stats)
    merged, *near_weights = lax.optimization_barrier((merged, *near_weights))
    merged = lax.all_to_all(merged, "seq", split_axis=0, concat_axis=0, tiled=True)

    row_share = block_len // head_count
    rows = block_count * row_share
    near, far = len(NEAR), len(FAR)
    back_shape = (seq_count, 2 * CAP * SEGMENT + 2 * room, head_dim)
    group = 8
    back, *near_rows = pl.pallas_call(
        lambda *refs: grads_kernel(scale, group, *refs),
        out_shape=(
            jax.ShapeDtypeStruct(back_shape, bf16),
            *[jax.ShapeDtypeStruct((far, rows, 2 * head_dim), bf16)] * near,
        ),
        in_specs=[spec(SMEM), spec(HBM), spec(VMEM), spec(VMEM), spec(HBM)],
        out_specs=(spec(HBM), *[spec(HBM)] * near),
        scratch_shapes=[
            pltpu.VMEM(arrived.shape, bf16),
            pltpu.VMEM(back_shape, bf16),
            pltpu.VMEM((enc_width, block_count * block_len), bf16),
            pltpu.VMEM((block_count * block_len, 2 * head_dim), bf16),
            pltpu.VMEM((near, far, rows, 2 * head_dim), bf16),
            pltpu.VMEM((block_count, block_len, head_dim), f32),
            pltpu.VMEM((block_count, block_len, head_dim), f32),
            pltpu.SemaphoreType.DMA((seq_count // group,)),
            pltpu.SemaphoreType.DMA,
            pltpu.SemaphoreType.DMA((near,)),
            pltpu.SemaphoreType.DMA,
        ],
        compiler_params=params(LARGE_LIMIT),
        name="grads",
    )(blocks, arrived, kv, merged, enc_t)

    near_rows = [r if a == 0 else shifted(r, a) for a, r in zip(NEAR, near_rows)]
    own, *far_sums, back = pl.pallas_call(
        project_kernel,
        out_shape=(
            jax.ShapeDtypeStruct((rows, enc_width), f32),
            *[jax.ShapeDtypeStruct((rows, enc_width), bf16)] * (far - 1),
            jax.ShapeDtypeStruct(back_shape, bf16),
        ),
        in_specs=[*[spec(VMEM)] * (2 * near), spec(HBM)],
        out_specs=(*[spec(VMEM)] * far, spec(HBM)),
        input_output_aliases={2 * near: far},
        compiler_params=params(LARGE_LIMIT),
        name="project",
    )(*near_rows, *near_weights, back)
    returned = lax.all_to_all(back, "seq", split_axis=0, concat_axis=0, tiled=True)
    encoding_grad = own
    for b, part in zip(FAR[1:], far_sums):
        encoding_grad = encoding_grad + shifted(part, b).astype(f32)

    attended, query_grad, key_weight_grad, value_weight_grad = pl.pallas_call(
        finish_kernel,
        out_shape=(
            jax.ShapeDtypeStruct((segments, SEGMENT, head_dim), bf16),
            jax.ShapeDtypeStruct((segments, SEGMENT, head_dim), bf16),
            jax.ShapeDtypeStruct((share, head_dim), f32),
            jax.ShapeDtypeStruct((share, head_dim), f32),
        ),
        in_specs=[spec(SMEM), spec(VMEM)],
        out_specs=(spec(VMEM),) * 4,
        compiler_params=params(),
        name="finish",
    )(slots, returned)
    return (
        attended.reshape(segments * SEGMENT, head_dim),
        query_grad.reshape(segments * SEGMENT, head_dim),
        encoding_grad.reshape(block_count, row_share, enc_width),
        key_weight_grad,
        value_weight_grad,
    )


def solution(mesh):
    in_specs = (
        P("seq", "head"),
        P("seq", None, None),
        P(None, "head"),
        P(None, "head"),
        P(),
        P("seq", "head"),
    )
    out_specs = (
        P("seq", "head"),
        P("seq", "head"),
        P("seq", "head", None),
        P("seq", "head"),
        P("seq", "head"),
    )
    return jax.shard_map(
        on_device, mesh=mesh, in_specs=in_specs, out_specs=out_specs, check_vma=False
    )
```

```python
import math

import jax
import jax.numpy as jnp
from jax import lax
from jax.experimental import pallas as pl
from jax.experimental.pallas import tpu as pltpu
from jax.sharding import PartitionSpec as P

SEGMENT = 64
NEIGH = 2
CAP = 2
PLACES = 8
NEAR = (0, 1, -1, 2)
FAR = (0, 4, 8, -4)
VMEM_LIMIT = 40 * 1024 * 1024
LARGE_LIMIT = 60 * 1024 * 1024
VMEM = pltpu.VMEM
SMEM = pltpu.SMEM
HBM = pltpu.HBM


def params(limit=VMEM_LIMIT):
    return pltpu.CompilerParams(vmem_limit_bytes=limit)


def spec(space):
    return pl.BlockSpec(memory_space=space)


def nt_dot(a, b):
    return lax.dot_general(a, b, (((1,), (1,)), ((), ())), preferred_element_type=jnp.float32)


def tn_dot(a, b):
    return lax.dot_general(a, b, (((0,), (0,)), ((), ())), preferred_element_type=jnp.float32)


def nn_dot(a, b):
    return jnp.dot(a, b, preferred_element_type=jnp.float32)


def pack_kernel(block_count, reads_ref, q_ref, g_ref, out_ref, slots_ref, used, stage, sem):
    seq_count = used.shape[0]
    read_count = slots_ref.shape[0]
    first = lax.axis_index("seq") * (read_count // NEIGH)

    def leave(slot):
        pltpu.make_async_copy(stage.at[slot], out_ref.at[slot], sem).start()

    for h in range(seq_count):
        used[h] = 0
    for j in range(read_count):
        holder = lax.div(reads_ref[j % NEIGH, first + j // NEIGH], block_count)
        rank = used[holder]
        used[holder] = rank + 1
        slot = holder * CAP + rank
        slots_ref[j] = slot
        stage[slot, 0] = q_ref[j // NEIGH]
        stage[slot, 1] = g_ref[j // NEIGH]
        leave(slot)

    def blank(h, _):
        for k in range(CAP):
            @pl.when(used[h] <= k)
            def _():
                stage[h * CAP + k] = jnp.zeros(stage.shape[1:], stage.dtype)
                leave(h * CAP + k)

        return 0

    lax.fori_loop(0, seq_count, blank, 0)
    pltpu.make_async_copy(stage, out_ref, sem).wait()


def pair_operands(x_ref, s, kv_a, kv_b):
    head_dim = x_ref.shape[3]

    def diagonal(i):
        one, two = x_ref[CAP * s, i], x_ref[CAP * s + 1, i]
        zero = jnp.zeros_like(one)
        return jnp.concatenate(
            [jnp.concatenate([one, zero], axis=1), jnp.concatenate([zero, two], axis=1)], axis=0
        )

    keys = jnp.concatenate([kv_a[:, :head_dim], kv_b[:, :head_dim]], axis=1)
    values = jnp.concatenate([kv_a[:, head_dim:], kv_b[:, head_dim:]], axis=1)
    return diagonal(0), diagonal(1), keys, values


def stats_kernel(scale, blocks_ref, to_ref, x_ref, kv_ref, pair_ref, slot_ref, send_ref, places):
    places[...] = jnp.zeros_like(places)
    left = lax.broadcasted_iota(jnp.int32, (1, CAP * SEGMENT), 1) < SEGMENT
    for s in range(x_ref.shape[0] // CAP):
        kv_a = kv_ref[blocks_ref[CAP * s]]
        kv_b = kv_ref[blocks_ref[CAP * s + 1]]
        q_diag, g_diag, keys, values = pair_operands(x_ref, s, kv_a, kv_b)
        scores = nt_dot(keys, q_diag) * scale
        top = jnp.max(scores, axis=0, keepdims=True)
        weight = jnp.exp(scores - top)
        total = jnp.sum(weight, axis=0, keepdims=True)
        prob_grad = nt_dot(values, g_diag)
        mean = jnp.sum(weight * prob_grad, axis=0, keepdims=True) / total
        lse = top + jnp.log(total)
        pair_ref[s] = jnp.concatenate([lse, mean], axis=0)
        row_a = jnp.where(left, lse, pltpu.roll(mean, SEGMENT, 1))
        row_b = jnp.where(left, pltpu.roll(lse, SEGMENT, 1), mean)
        slot_ref[CAP * s:CAP * s + 1, :] = row_a
        slot_ref[CAP * s + 1:CAP * s + 2, :] = row_b
        places[pl.ds(to_ref[CAP * s], 1), :] = row_a
        places[pl.ds(to_ref[CAP * s + 1], 1), :] = row_b
    send_ref[...] = places[:send_ref.shape[0]]


def swap_kernel(slots_ref, in_ref, out_ref):
    out_ref[...] = jnp.zeros_like(out_ref)
    for c in range(slots_ref.shape[0] // NEIGH):
        slot_a, slot_b = slots_ref[NEIGH * c], slots_ref[NEIGH * c + 1]
        out_ref[pl.ds(slot_a, 1), :] = in_ref[pl.ds(slot_b, 1), :]
        out_ref[pl.ds(slot_b, 1), :] = in_ref[pl.ds(slot_a, 1), :]


def merge_stats(own, row_a, row_b, left):
    other_lse = jnp.where(left, row_a, pltpu.roll(row_b, SEGMENT, 1))
    other_mean = jnp.where(left, pltpu.roll(row_a, SEGMENT, 1), row_b)
    lse, mean = own[0:1], own[1:2]
    top = jnp.maximum(lse, other_lse)
    merged = top + jnp.log(jnp.exp(lse - top) + jnp.exp(other_lse - top))
    delta = jnp.exp(lse - merged) * mean + jnp.exp(other_lse - merged) * other_mean
    return merged, delta


def grads_kernel(scale, group, blocks_ref, from_ref, x_hbm, kv_ref, own_ref, other_ref, enc_hbm, *refs):
    near = len(NEAR)
    out_ref = refs[0]
    rows_refs = refs[1:1 + near]
    x_ref, stage, enc_t, rows_all, rows_near, acc_k, acc_v, x_sems, enc_sem, rows_sems, out_sem = refs[1 + near:]
    head_dim = kv_ref.shape[2] // 2
    seq_count = x_ref.shape[0] // CAP
    pair = CAP * SEGMENT
    parts = 2 * pair

    def arrival(i):
        at = pl.ds(i * group * CAP, group * CAP)
        return pltpu.make_async_copy(x_hbm.at[at], x_ref.at[at], x_sems.at[i])

    for i in range(seq_count // group):
        arrival(i).start()
    fetch = pltpu.make_async_copy(enc_hbm, enc_t, enc_sem)
    fetch.start()
    acc_k[...] = jnp.zeros_like(acc_k)
    acc_v[...] = jnp.zeros_like(acc_v)
    left = lax.broadcasted_iota(jnp.int32, (1, pair), 1) < SEGMENT

    def step(i, _):
        arrival(i).wait()
        sources = [i * group + g for g in range(group)]
        first = [blocks_ref[CAP * s] for s in sources]
        second = [blocks_ref[CAP * s + 1] for s in sources]
        operands = [
            pair_operands(x_ref, s, kv_ref[a], kv_ref[b]) for s, a, b in zip(sources, first, second)
        ]
        stats = [
            merge_stats(
                own_ref[s],
                other_ref[pl.ds(from_ref[CAP * s], 1), :],
                other_ref[pl.ds(from_ref[CAP * s + 1], 1), :],
                left,
            )
            for s in sources
        ]
        scores = [nt_dot(keys, q) * scale for q, _, keys, _ in operands]
        prob_grads = [nt_dot(values, g) for _, g, _, values in operands]
        probs = [jnp.exp(x - stat[0]) for x, stat in zip(scores, stats)]
        score_grads = [
            (p * (x - stat[1]) * scale).astype(jnp.bfloat16)
            for p, x, stat in zip(probs, prob_grads, stats)
        ]
        probs = [p.astype(jnp.bfloat16) for p in probs]
        attended = [tn_dot(p, ops[3]).astype(jnp.bfloat16) for p, ops in zip(probs, operands)]
        query_grads = [tn_dot(x, ops[2]).astype(jnp.bfloat16) for x, ops in zip(score_grads, operands)]
        value_parts = [nn_dot(p, ops[1]) for p, ops in zip(probs, operands)]
        key_parts = [nn_dot(x, ops[0]) for x, ops in zip(score_grads, operands)]
        for s, att, grad in zip(sources, attended, query_grads):
            stage[s, :SEGMENT] = att[:SEGMENT, :head_dim]
            stage[s, SEGMENT:pair] = grad[:SEGMENT, :head_dim]
            stage[s, pair:pair + SEGMENT] = att[SEGMENT:, head_dim:]
            stage[s, pair + SEGMENT:parts] = grad[SEGMENT:, head_dim:]
        for a, b, key_part, value_part in zip(first, second, key_parts, value_parts):
            acc_k[a] += key_part[:, :head_dim]
            acc_v[a] += value_part[:, :head_dim]
            acc_k[b] += key_part[:, head_dim:]
            acc_v[b] += value_part[:, head_dim:]
        at = pl.ds(i * group, group)
        pltpu.make_async_copy(stage.at[at, :parts], out_ref.at[at, :parts], out_sem).start()
        return 0

    lax.fori_loop(0, seq_count // group, step, 0)
    head_count = near * len(FAR)
    block_count, block_len, _ = acc_k.shape
    row_share = block_len // head_count
    z = lax.axis_index("head")
    rows_copies = []
    for i, a in enumerate(NEAR):
        for j, b in enumerate(FAR):
            dest = lax.rem(z + (a + b + head_count), head_count)
            at = pl.ds(pl.multiple_of(dest * row_share, row_share), row_share)
            rows = jnp.concatenate([acc_k[:, at, :], acc_v[:, at, :]], axis=2)
            rows_near[i, j] = rows.reshape(block_count * row_share, 2 * head_dim).astype(jnp.bfloat16)
        rows_copies.append(pltpu.make_async_copy(rows_near.at[i], rows_refs[i], rows_sems.at[i]))
        rows_copies[i].start()
    rows_all[:, :head_dim] = acc_k[...].reshape(-1, head_dim).astype(jnp.bfloat16)
    rows_all[:, head_dim:] = acc_v[...].reshape(-1, head_dim).astype(jnp.bfloat16)
    room = (stage.shape[1] - parts) // 2
    share = enc_t.shape[0] // seq_count
    fetch.wait()
    batch = 8
    for i in range(0, seq_count, batch):
        term = nn_dot(enc_t[i * share:(i + batch) * share], rows_all[...])
        for s in range(batch):
            part = term[s * share:(s + 1) * share]
            if room > share:
                part = jnp.concatenate([part, jnp.zeros((room - share, 2 * head_dim), jnp.float32)], axis=0)
            part = part.astype(jnp.bfloat16)
            stage[i + s, parts:parts + room] = part[:, :head_dim]
            stage[i + s, parts + room:] = part[:, head_dim:]
        pltpu.make_async_copy(
            stage.at[i:i + batch, parts:], out_ref.at[i:i + batch, parts:], out_sem
        ).start()
    for copy in rows_copies:
        copy.wait()
    pltpu.make_async_copy(stage, out_ref, out_sem).wait()


def finish_kernel(slots_ref, in_ref, att_ref, qg_ref, kw_ref, vw_ref):
    share = kw_ref.shape[0]
    parts = 2 * CAP * SEGMENT
    room = (in_ref.shape[1] - parts) // 2

    def step(c, _):
        slot_a, slot_b = slots_ref[NEIGH * c], slots_ref[NEIGH * c + 1]

        def part(slot):
            holder = lax.div(slot, CAP)
            row = pl.multiple_of((slot - holder * CAP) * 2 * SEGMENT, 2 * SEGMENT)
            return in_ref[holder, pl.ds(row, 2 * SEGMENT), :].astype(jnp.float32)

        total = (part(slot_a) + part(slot_b)).astype(jnp.bfloat16)
        att_ref[c] = total[:SEGMENT]
        qg_ref[c] = total[SEGMENT:]
        return 0

    lax.fori_loop(0, att_ref.shape[0], step, 0, unroll=2)
    total = in_ref[0, parts:, :].astype(jnp.float32)
    for s in range(1, in_ref.shape[0]):
        total = total + in_ref[s, parts:, :].astype(jnp.float32)
    kw_ref[...] = total[:share]
    vw_ref[...] = total[room:room + share]


def project_kernel(*refs):
    near = len(NEAR)
    rows_refs, weight_refs, own_ref, far_refs = refs[:near], refs[near:2 * near], refs[2 * near], refs[2 * near + 1:]
    far, rows, width = rows_refs[0].shape
    half = far // 2
    for i in range(0, far, half):
        total = jnp.zeros((half * rows, own_ref.shape[1]), jnp.float32)
        for rows_ref, weight_ref in zip(rows_refs, weight_refs):
            total = total + nt_dot(rows_ref[i:i + half].reshape(half * rows, width), weight_ref[...])
        for j in range(half):
            part = total[j * rows:(j + 1) * rows]
            if i + j == 0:
                own_ref[...] = part
            else:
                far_refs[i + j - 1][...] = part.astype(jnp.bfloat16)


def shifted(x, step):
    count = lax.axis_size("head")
    return lax.ppermute(x, "head", [(z, (z + step) % count) for z in range(count)])


def on_device(queries, encodings, key_weight, value_weight, reads, out_grad):
    seq_count = lax.axis_size("seq")
    head_count = lax.axis_size("head")
    me = lax.axis_index("seq")
    block_count, block_len, enc_width = encodings.shape
    head_dim = key_weight.shape[1]
    segments = queries.shape[0] // SEGMENT
    read_count = NEIGH * segments
    slot_count = seq_count * CAP
    scale = 1.0 / math.sqrt(head_dim)
    bf16, f32 = jnp.bfloat16, jnp.float32

    packed, slots = pl.pallas_call(
        lambda *refs: pack_kernel(block_count, *refs),
        out_shape=(
            jax.ShapeDtypeStruct((slot_count, 2, SEGMENT, head_dim), bf16),
            jax.ShapeDtypeStruct((read_count,), jnp.int32),
        ),
        in_specs=[spec(SMEM), spec(VMEM), spec(VMEM)],
        out_specs=(spec(HBM), spec(SMEM)),
        scratch_shapes=[
            pltpu.SMEM((seq_count,), jnp.int32),
            pltpu.VMEM((slot_count, 2, SEGMENT, head_dim), bf16),
            pltpu.SemaphoreType.DMA,
        ],
        compiler_params=params(LARGE_LIMIT),
        name="pack",
    )(
        reads.T,
        queries.reshape(segments, SEGMENT, head_dim),
        out_grad.reshape(segments, SEGMENT, head_dim),
    )
    arrived = lax.all_to_all(packed, "seq", split_axis=0, concat_axis=0, tiled=True)

    key_weight, value_weight, slots = lax.optimization_barrier((key_weight, value_weight, slots))
    weights = jnp.concatenate([key_weight, value_weight], axis=1)
    flat_enc = encodings.reshape(block_count * block_len, enc_width)
    kv = jnp.dot(flat_enc, weights, preferred_element_type=f32).astype(bf16)
    kv = kv.reshape(block_count, block_len, 2 * head_dim)
    share = enc_width // seq_count
    room = -(-share // 16) * 16
    enc_t = flat_enc.T

    tables = reads.reshape(seq_count, read_count)
    holders = tables // block_count
    partners = holders.reshape(-1, NEIGH)[:, ::-1].reshape(seq_count, read_count)
    mine = holders == me
    rank = jnp.cumsum(mine.astype(jnp.int32), axis=1)
    code = (tables % block_count) + (partners + 1) * block_count
    code = jnp.stack(
        [jnp.sum(jnp.where(mine & (rank == k + 1), code, 0), axis=1) for k in range(CAP)], axis=1
    ).reshape(slot_count)
    blocks = code % block_count
    partner = code // block_count - 1
    taken = partner >= 0
    order = jnp.arange(slot_count)
    same = (partner[:, None] == partner[None, :]) & (order[None, :] < order[:, None])
    place = jnp.sum(same.astype(jnp.int32), axis=1)
    twin = place.reshape(-1, CAP)[:, ::-1].reshape(slot_count)
    send_to = jnp.where(taken, partner * PLACES + jnp.minimum(place, PLACES - 1), seq_count * PLACES)
    taken_from = jnp.minimum(jnp.where(partner == me, twin, place), PLACES - 1)
    taken_from = jnp.where(taken, partner * PLACES + taken_from, 0)
    pairs = jax.nn.one_hot(holders.reshape(-1, NEIGH), seq_count, dtype=bf16)
    shared = lax.dot_general(
        pairs[:, 0], pairs[:, 1], (((0,), (0,)), ((), ())), preferred_element_type=f32
    )
    fits = jnp.max(shared + shared.T) <= PLACES
    taken_from = jnp.where(fits, taken_from, order)
    kv, enc_t, blocks, send_to, taken_from, fits, weights = lax.optimization_barrier(
        (kv, enc_t, blocks, send_to, taken_from, fits, weights)
    )
    near_weights = [weights if a == 0 else shifted(weights, a) for a in NEAR]

    place_count = seq_count * PLACES
    own_stats, slot_stats, sent = pl.pallas_call(
        lambda *refs: stats_kernel(scale, *refs),
        out_shape=(
            jax.ShapeDtypeStruct((seq_count, 2, CAP * SEGMENT), f32),
            jax.ShapeDtypeStruct((slot_count, CAP * SEGMENT), f32),
            jax.ShapeDtypeStruct((place_count, CAP * SEGMENT), f32),
        ),
        in_specs=[spec(SMEM), spec(SMEM), spec(VMEM), spec(VMEM)],
        out_specs=(spec(VMEM),) * 3,
        scratch_shapes=[pltpu.VMEM((place_count + 8, CAP * SEGMENT), f32)],
        compiler_params=params(),
        name="stats",
    )(blocks, send_to, arrived, kv)

    def one_hop(sent, slot_stats, slots):
        return lax.all_to_all(sent, "seq", split_axis=0, concat_axis=0, tiled=True)

    def two_hops(sent, slot_stats, slots):
        at_reader = lax.all_to_all(slot_stats, "seq", split_axis=0, concat_axis=0, tiled=True)
        swapped = pl.pallas_call(
            swap_kernel,
            out_shape=jax.ShapeDtypeStruct(slot_stats.shape, f32),
            in_specs=[spec(SMEM), spec(VMEM)],
            out_specs=spec(VMEM),
            compiler_params=params(),
            name="swap",
        )(slots, at_reader)
        swapped = lax.all_to_all(swapped, "seq", split_axis=0, concat_axis=0, tiled=True)
        return jnp.pad(swapped, ((0, place_count - slot_count), (0, 0)))

    other_stats = lax.cond(fits, one_hop, two_hops, sent, slot_stats, slots)

    row_share = block_len // head_count
    rows = block_count * row_share
    near, far = len(NEAR), len(FAR)
    back_shape = (seq_count, 2 * CAP * SEGMENT + 2 * room, head_dim)
    group = 8
    back, *near_rows = pl.pallas_call(
        lambda *refs: grads_kernel(scale, group, *refs),
        out_shape=(
            jax.ShapeDtypeStruct(back_shape, bf16),
            *[jax.ShapeDtypeStruct((far, rows, 2 * head_dim), bf16)] * near,
        ),
        in_specs=[spec(SMEM), spec(SMEM), spec(HBM), spec(VMEM), spec(VMEM), spec(VMEM), spec(HBM)],
        out_specs=(spec(HBM), *[spec(HBM)] * near),
        scratch_shapes=[
            pltpu.VMEM(arrived.shape, bf16),
            pltpu.VMEM(back_shape, bf16),
            pltpu.VMEM((enc_width, block_count * block_len), bf16),
            pltpu.VMEM((block_count * block_len, 2 * head_dim), bf16),
            pltpu.VMEM((near, far, rows, 2 * head_dim), bf16),
            pltpu.VMEM((block_count, block_len, head_dim), f32),
            pltpu.VMEM((block_count, block_len, head_dim), f32),
            pltpu.SemaphoreType.DMA((seq_count // group,)),
            pltpu.SemaphoreType.DMA,
            pltpu.SemaphoreType.DMA((near,)),
            pltpu.SemaphoreType.DMA,
        ],
        compiler_params=params(LARGE_LIMIT),
        name="grads",
    )(blocks, taken_from, arrived, kv, own_stats, other_stats, enc_t)

    back, *near_weights = lax.optimization_barrier((back, *near_weights))
    returned = lax.all_to_all(back, "seq", split_axis=0, concat_axis=0, tiled=True)
    near_rows = [r if a == 0 else shifted(r, a) for a, r in zip(NEAR, near_rows)]
    own, *far_sums = pl.pallas_call(
        project_kernel,
        out_shape=(
            jax.ShapeDtypeStruct((rows, enc_width), f32),
            *[jax.ShapeDtypeStruct((rows, enc_width), bf16)] * (far - 1),
        ),
        in_specs=[spec(VMEM)] * (2 * near),
        out_specs=(spec(VMEM),) * far,
        compiler_params=params(),
        name="project",
    )(*near_rows, *near_weights)
    encoding_grad = own
    for b, part in zip(FAR[1:], far_sums):
        encoding_grad = encoding_grad + shifted(part, b).astype(f32)

    attended, query_grad, key_weight_grad, value_weight_grad = pl.pallas_call(
        finish_kernel,
        out_shape=(
            jax.ShapeDtypeStruct((segments, SEGMENT, head_dim), bf16),
            jax.ShapeDtypeStruct((segments, SEGMENT, head_dim), bf16),
            jax.ShapeDtypeStruct((share, head_dim), f32),
            jax.ShapeDtypeStruct((share, head_dim), f32),
        ),
        in_specs=[spec(SMEM), spec(VMEM)],
        out_specs=(spec(VMEM),) * 4,
        compiler_params=params(),
        name="finish",
    )(slots, returned)
    return (
        attended.reshape(segments * SEGMENT, head_dim),
        query_grad.reshape(segments * SEGMENT, head_dim),
        encoding_grad.reshape(block_count, row_share, enc_width),
        key_weight_grad,
        value_weight_grad,
    )


def solution(mesh):
    in_specs = (
        P("seq", "head"),
        P("seq", None, None),
        P(None, "head"),
        P(None, "head"),
        P(),
        P("seq", "head"),
    )
    out_specs = (
        P("seq", "head"),
        P("seq", "head"),
        P("seq", "head", None),
        P("seq", "head"),
        P("seq", "head"),
    )
    return jax.shard_map(
        on_device, mesh=mesh, in_specs=in_specs, out_specs=out_specs, check_vma=False
    )
```

```python
import math

import jax
import jax.numpy as jnp
from jax import lax
from jax.experimental import pallas as pl
from jax.experimental.pallas import tpu as pltpu
from jax.sharding import PartitionSpec as P

SEGMENT = 64
NEIGH = 2
CAP = 2
PLACES = 8
NEAR = (0, 1, -1, 2)
FAR = (0, 4, 8, -4)
VMEM_LIMIT = 40 * 1024 * 1024
LARGE_LIMIT = 60 * 1024 * 1024
VMEM = pltpu.VMEM
SMEM = pltpu.SMEM
HBM = pltpu.HBM


def params(limit=VMEM_LIMIT):
    return pltpu.CompilerParams(vmem_limit_bytes=limit)


def spec(space):
    return pl.BlockSpec(memory_space=space)


def nt_dot(a, b):
    return lax.dot_general(a, b, (((1,), (1,)), ((), ())), preferred_element_type=jnp.float32)


def tn_dot(a, b):
    return lax.dot_general(a, b, (((0,), (0,)), ((), ())), preferred_element_type=jnp.float32)


def nn_dot(a, b):
    return jnp.dot(a, b, preferred_element_type=jnp.float32)


def pack_kernel(block_count, reads_ref, q_ref, g_ref, out_ref, slots_ref, used, stage, sem):
    seq_count = used.shape[0]
    read_count = slots_ref.shape[0]
    first = lax.axis_index("seq") * (read_count // NEIGH)

    def leave(slot):
        pltpu.make_async_copy(stage.at[slot], out_ref.at[slot], sem).start()

    for h in range(seq_count):
        used[h] = 0
    for j in range(read_count):
        holder = lax.div(reads_ref[j % NEIGH, first + j // NEIGH], block_count)
        rank = used[holder]
        used[holder] = rank + 1
        slot = holder * CAP + rank
        slots_ref[j] = slot
        stage[slot, 0] = q_ref[j // NEIGH]
        stage[slot, 1] = g_ref[j // NEIGH]
        leave(slot)

    def blank(h, _):
        for k in range(CAP):
            @pl.when(used[h] <= k)
            def _():
                stage[h * CAP + k] = jnp.zeros(stage.shape[1:], stage.dtype)
                leave(h * CAP + k)

        return 0

    lax.fori_loop(0, seq_count, blank, 0)
    pltpu.make_async_copy(stage, out_ref, sem).wait()


def pair_operands(x_ref, s, kv_a, kv_b):
    head_dim = x_ref.shape[3]

    def diagonal(i):
        one, two = x_ref[CAP * s, i], x_ref[CAP * s + 1, i]
        zero = jnp.zeros_like(one)
        return jnp.concatenate(
            [jnp.concatenate([one, zero], axis=1), jnp.concatenate([zero, two], axis=1)], axis=0
        )

    keys = jnp.concatenate([kv_a[:, :head_dim], kv_b[:, :head_dim]], axis=1)
    values = jnp.concatenate([kv_a[:, head_dim:], kv_b[:, head_dim:]], axis=1)
    return diagonal(0), diagonal(1), keys, values


def stats_kernel(scale, blocks_ref, to_ref, x_ref, kv_ref, pair_ref, slot_ref, send_ref, places):
    places[...] = jnp.zeros_like(places)
    left = lax.broadcasted_iota(jnp.int32, (1, CAP * SEGMENT), 1) < SEGMENT
    for s in range(x_ref.shape[0] // CAP):
        kv_a = kv_ref[blocks_ref[CAP * s]]
        kv_b = kv_ref[blocks_ref[CAP * s + 1]]
        q_diag, g_diag, keys, values = pair_operands(x_ref, s, kv_a, kv_b)
        scores = nt_dot(keys, q_diag) * scale
        top = jnp.max(scores, axis=0, keepdims=True)
        weight = jnp.exp(scores - top)
        total = jnp.sum(weight, axis=0, keepdims=True)
        prob_grad = nt_dot(values, g_diag)
        mean = jnp.sum(weight * prob_grad, axis=0, keepdims=True) / total
        lse = top + jnp.log(total)
        pair_ref[s] = jnp.concatenate([lse, mean], axis=0)
        row_a = jnp.where(left, lse, pltpu.roll(mean, SEGMENT, 1))
        row_b = jnp.where(left, pltpu.roll(lse, SEGMENT, 1), mean)
        slot_ref[CAP * s:CAP * s + 1, :] = row_a
        slot_ref[CAP * s + 1:CAP * s + 2, :] = row_b
        places[pl.ds(to_ref[CAP * s], 1), :] = row_a
        places[pl.ds(to_ref[CAP * s + 1], 1), :] = row_b
    send_ref[...] = places[:send_ref.shape[0]]


def swap_kernel(slots_ref, in_ref, out_ref):
    out_ref[...] = jnp.zeros_like(out_ref)
    for c in range(slots_ref.shape[0] // NEIGH):
        slot_a, slot_b = slots_ref[NEIGH * c], slots_ref[NEIGH * c + 1]
        out_ref[pl.ds(slot_a, 1), :] = in_ref[pl.ds(slot_b, 1), :]
        out_ref[pl.ds(slot_b, 1), :] = in_ref[pl.ds(slot_a, 1), :]


def merge_stats(own, row_a, row_b, left):
    other_lse = jnp.where(left, row_a, pltpu.roll(row_b, SEGMENT, 1))
    other_mean = jnp.where(left, pltpu.roll(row_a, SEGMENT, 1), row_b)
    lse, mean = own[0:1], own[1:2]
    top = jnp.maximum(lse, other_lse)
    merged = top + jnp.log(jnp.exp(lse - top) + jnp.exp(other_lse - top))
    delta = jnp.exp(lse - merged) * mean + jnp.exp(other_lse - merged) * other_mean
    return merged, delta


def grads_kernel(scale, group, blocks_ref, from_ref, x_hbm, kv_ref, own_ref, other_ref, *refs):
    near = len(NEAR)
    out_ref = refs[0]
    rows_refs = refs[1:1 + near]
    all_ref, x_ref, stage, rows_all, rows_near, acc_k, acc_v, x_sems, rows_sems, out_sem = refs[1 + near:]
    head_dim = kv_ref.shape[2] // 2
    seq_count = x_ref.shape[0] // CAP
    pair = CAP * SEGMENT
    parts = 2 * pair

    def arrival(i):
        at = pl.ds(i * group * CAP, group * CAP)
        return pltpu.make_async_copy(x_hbm.at[at], x_ref.at[at], x_sems.at[i])

    for i in range(seq_count // group):
        arrival(i).start()
    acc_k[...] = jnp.zeros_like(acc_k)
    acc_v[...] = jnp.zeros_like(acc_v)
    left = lax.broadcasted_iota(jnp.int32, (1, pair), 1) < SEGMENT

    def step(i, _):
        arrival(i).wait()
        sources = [i * group + g for g in range(group)]
        first = [blocks_ref[CAP * s] for s in sources]
        second = [blocks_ref[CAP * s + 1] for s in sources]
        operands = [
            pair_operands(x_ref, s, kv_ref[a], kv_ref[b]) for s, a, b in zip(sources, first, second)
        ]
        stats = [
            merge_stats(
                own_ref[s],
                other_ref[pl.ds(from_ref[CAP * s], 1), :],
                other_ref[pl.ds(from_ref[CAP * s + 1], 1), :],
                left,
            )
            for s in sources
        ]
        scores = [nt_dot(keys, q) * scale for q, _, keys, _ in operands]
        prob_grads = [nt_dot(values, g) for _, g, _, values in operands]
        probs = [jnp.exp(x - stat[0]) for x, stat in zip(scores, stats)]
        score_grads = [
            (p * (x - stat[1]) * scale).astype(jnp.bfloat16)
            for p, x, stat in zip(probs, prob_grads, stats)
        ]
        probs = [p.astype(jnp.bfloat16) for p in probs]
        attended = [tn_dot(p, ops[3]).astype(jnp.bfloat16) for p, ops in zip(probs, operands)]
        query_grads = [tn_dot(x, ops[2]).astype(jnp.bfloat16) for x, ops in zip(score_grads, operands)]
        value_parts = [nn_dot(p, ops[1]) for p, ops in zip(probs, operands)]
        key_parts = [nn_dot(x, ops[0]) for x, ops in zip(score_grads, operands)]
        for s, att, grad in zip(sources, attended, query_grads):
            stage[s, :SEGMENT] = att[:SEGMENT, :head_dim]
            stage[s, SEGMENT:pair] = grad[:SEGMENT, :head_dim]
            stage[s, pair:pair + SEGMENT] = att[SEGMENT:, head_dim:]
            stage[s, pair + SEGMENT:parts] = grad[SEGMENT:, head_dim:]
        for a, b, key_part, value_part in zip(first, second, key_parts, value_parts):
            acc_k[a] += key_part[:, :head_dim]
            acc_v[a] += value_part[:, :head_dim]
            acc_k[b] += key_part[:, head_dim:]
            acc_v[b] += value_part[:, head_dim:]
        at = pl.ds(i * group, group)
        pltpu.make_async_copy(stage.at[at], out_ref.at[at, :parts], out_sem).start()
        return 0

    lax.fori_loop(0, seq_count // group, step, 0)
    head_count = near * len(FAR)
    block_count, block_len, _ = acc_k.shape
    row_share = block_len // head_count
    z = lax.axis_index("head")
    rows_copies = []
    for i, a in enumerate(NEAR):
        for j, b in enumerate(FAR):
            dest = lax.rem(z + (a + b + head_count), head_count)
            at = pl.ds(pl.multiple_of(dest * row_share, row_share), row_share)
            rows = jnp.concatenate([acc_k[:, at, :], acc_v[:, at, :]], axis=2)
            rows_near[i, j] = rows.reshape(block_count * row_share, 2 * head_dim).astype(jnp.bfloat16)
        rows_copies.append(pltpu.make_async_copy(rows_near.at[i], rows_refs[i], rows_sems.at[i]))
        rows_copies[i].start()
    rows_all[:, :head_dim] = acc_k[...].reshape(-1, head_dim).astype(jnp.bfloat16)
    rows_all[:, head_dim:] = acc_v[...].reshape(-1, head_dim).astype(jnp.bfloat16)
    rows_copies.append(pltpu.make_async_copy(rows_all, all_ref, rows_sems.at[near]))
    rows_copies[near].start()
    for copy in rows_copies:
        copy.wait()
    pltpu.make_async_copy(stage, out_ref.at[:, :parts], out_sem).wait()


def weigh_kernel(parts, rows_ref, enc_t_ref, back_ref, out_ref, stage, sem):
    head_dim = rows_ref.shape[1] // 2
    seq_count, room = stage.shape[0], stage.shape[1] // 2
    share = enc_t_ref.shape[0] // seq_count
    batch = 8
    for i in range(0, seq_count, batch):
        term = nn_dot(enc_t_ref[i * share:(i + batch) * share], rows_ref[...])
        for s in range(batch):
            part = term[s * share:(s + 1) * share]
            if room > share:
                part = jnp.concatenate([part, jnp.zeros((room - share, 2 * head_dim), jnp.float32)], axis=0)
            part = part.astype(jnp.bfloat16)
            stage[i + s, :room] = part[:, :head_dim]
            stage[i + s, room:] = part[:, head_dim:]
        at = pl.ds(i, batch)
        pltpu.make_async_copy(stage.at[at], out_ref.at[at, parts:], sem).start()
    pltpu.make_async_copy(stage, out_ref.at[:, parts:], sem).wait()


def finish_kernel(slots_ref, in_ref, att_ref, qg_ref, kw_ref, vw_ref):
    share = kw_ref.shape[0]
    parts = 2 * CAP * SEGMENT
    room = (in_ref.shape[1] - parts) // 2

    def step(c, _):
        slot_a, slot_b = slots_ref[NEIGH * c], slots_ref[NEIGH * c + 1]

        def part(slot):
            holder = lax.div(slot, CAP)
            row = pl.multiple_of((slot - holder * CAP) * 2 * SEGMENT, 2 * SEGMENT)
            return in_ref[holder, pl.ds(row, 2 * SEGMENT), :].astype(jnp.float32)

        total = (part(slot_a) + part(slot_b)).astype(jnp.bfloat16)
        att_ref[c] = total[:SEGMENT]
        qg_ref[c] = total[SEGMENT:]
        return 0

    lax.fori_loop(0, att_ref.shape[0], step, 0, unroll=2)
    total = in_ref[0, parts:, :].astype(jnp.float32)
    for s in range(1, in_ref.shape[0]):
        total = total + in_ref[s, parts:, :].astype(jnp.float32)
    kw_ref[...] = total[:share]
    vw_ref[...] = total[room:room + share]


def project_kernel(*refs):
    near = len(NEAR)
    rows_refs, weight_refs, own_ref, far_refs = refs[:near], refs[near:2 * near], refs[2 * near], refs[2 * near + 1:]
    far, rows, width = rows_refs[0].shape
    half = far // 2
    for i in range(0, far, half):
        total = jnp.zeros((half * rows, own_ref.shape[1]), jnp.float32)
        for rows_ref, weight_ref in zip(rows_refs, weight_refs):
            total = total + nt_dot(rows_ref[i:i + half].reshape(half * rows, width), weight_ref[...])
        for j in range(half):
            part = total[j * rows:(j + 1) * rows]
            if i + j == 0:
                own_ref[...] = part
            else:
                far_refs[i + j - 1][...] = part.astype(jnp.bfloat16)


def total_kernel(own_ref, one_ref, two_ref, three_ref, done_ref, out_ref):
    total = own_ref[...] + one_ref[...].astype(jnp.float32)
    out_ref[...] = total + two_ref[...].astype(jnp.float32) + three_ref[...].astype(jnp.float32)


def shifted(x, step):
    count = lax.axis_size("head")
    return lax.ppermute(x, "head", [(z, (z + step) % count) for z in range(count)])


def on_device(queries, encodings, key_weight, value_weight, reads, out_grad):
    seq_count = lax.axis_size("seq")
    head_count = lax.axis_size("head")
    me = lax.axis_index("seq")
    block_count, block_len, enc_width = encodings.shape
    head_dim = key_weight.shape[1]
    segments = queries.shape[0] // SEGMENT
    read_count = NEIGH * segments
    slot_count = seq_count * CAP
    scale = 1.0 / math.sqrt(head_dim)
    bf16, f32 = jnp.bfloat16, jnp.float32

    packed, slots = pl.pallas_call(
        lambda *refs: pack_kernel(block_count, *refs),
        out_shape=(
            jax.ShapeDtypeStruct((slot_count, 2, SEGMENT, head_dim), bf16),
            jax.ShapeDtypeStruct((read_count,), jnp.int32),
        ),
        in_specs=[spec(SMEM), spec(VMEM), spec(VMEM)],
        out_specs=(spec(HBM), spec(SMEM)),
        scratch_shapes=[
            pltpu.SMEM((seq_count,), jnp.int32),
            pltpu.VMEM((slot_count, 2, SEGMENT, head_dim), bf16),
            pltpu.SemaphoreType.DMA,
        ],
        compiler_params=params(LARGE_LIMIT),
        name="pack",
    )(
        reads.T,
        queries.reshape(segments, SEGMENT, head_dim),
        out_grad.reshape(segments, SEGMENT, head_dim),
    )
    arrived = lax.all_to_all(packed, "seq", split_axis=0, concat_axis=0, tiled=True)

    key_weight, value_weight, slots = lax.optimization_barrier((key_weight, value_weight, slots))
    weights = jnp.concatenate([key_weight, value_weight], axis=1)
    flat_enc = encodings.reshape(block_count * block_len, enc_width)
    kv = jnp.dot(flat_enc, weights, preferred_element_type=f32).astype(bf16)
    kv = kv.reshape(block_count, block_len, 2 * head_dim)
    share = enc_width // seq_count
    room = -(-share // 16) * 16
    enc_t = flat_enc.T

    tables = reads.reshape(seq_count, read_count)
    holders = tables // block_count
    partners = holders.reshape(-1, NEIGH)[:, ::-1].reshape(seq_count, read_count)
    mine = holders == me
    rank = jnp.cumsum(mine.astype(jnp.int32), axis=1)
    code = (tables % block_count) + (partners + 1) * block_count
    code = jnp.stack(
        [jnp.sum(jnp.where(mine & (rank == k + 1), code, 0), axis=1) for k in range(CAP)], axis=1
    ).reshape(slot_count)
    blocks = code % block_count
    partner = code // block_count - 1
    taken = partner >= 0
    order = jnp.arange(slot_count)
    same = (partner[:, None] == partner[None, :]) & (order[None, :] < order[:, None])
    place = jnp.sum(same.astype(jnp.int32), axis=1)
    twin = place.reshape(-1, CAP)[:, ::-1].reshape(slot_count)
    send_to = jnp.where(taken, partner * PLACES + jnp.minimum(place, PLACES - 1), seq_count * PLACES)
    taken_from = jnp.minimum(jnp.where(partner == me, twin, place), PLACES - 1)
    taken_from = jnp.where(taken, partner * PLACES + taken_from, 0)
    pairs = jax.nn.one_hot(holders.reshape(-1, NEIGH), seq_count, dtype=bf16)
    shared = lax.dot_general(
        pairs[:, 0], pairs[:, 1], (((0,), (0,)), ((), ())), preferred_element_type=f32
    )
    fits = jnp.max(shared + shared.T) <= PLACES
    taken_from = jnp.where(fits, taken_from, order)
    kv, enc_t, blocks, send_to, taken_from, fits, weights = lax.optimization_barrier(
        (kv, enc_t, blocks, send_to, taken_from, fits, weights)
    )
    near_weights = [weights if a == 0 else shifted(weights, a) for a in NEAR]

    place_count = seq_count * PLACES
    own_stats, slot_stats, sent = pl.pallas_call(
        lambda *refs: stats_kernel(scale, *refs),
        out_shape=(
            jax.ShapeDtypeStruct((seq_count, 2, CAP * SEGMENT), f32),
            jax.ShapeDtypeStruct((slot_count, CAP * SEGMENT), f32),
            jax.ShapeDtypeStruct((place_count, CAP * SEGMENT), f32),
        ),
        in_specs=[spec(SMEM), spec(SMEM), spec(VMEM), spec(VMEM)],
        out_specs=(spec(VMEM),) * 3,
        scratch_shapes=[pltpu.VMEM((place_count + 8, CAP * SEGMENT), f32)],
        compiler_params=params(),
        name="stats",
    )(blocks, send_to, arrived, kv)

    def one_hop(sent, slot_stats, slots):
        return lax.all_to_all(sent, "seq", split_axis=0, concat_axis=0, tiled=True)

    def two_hops(sent, slot_stats, slots):
        at_reader = lax.all_to_all(slot_stats, "seq", split_axis=0, concat_axis=0, tiled=True)
        swapped = pl.pallas_call(
            swap_kernel,
            out_shape=jax.ShapeDtypeStruct(slot_stats.shape, f32),
            in_specs=[spec(SMEM), spec(VMEM)],
            out_specs=spec(VMEM),
            compiler_params=params(),
            name="swap",
        )(slots, at_reader)
        swapped = lax.all_to_all(swapped, "seq", split_axis=0, concat_axis=0, tiled=True)
        return jnp.pad(swapped, ((0, place_count - slot_count), (0, 0)))

    other_stats = lax.cond(fits, one_hop, two_hops, sent, slot_stats, slots)

    row_share = block_len // head_count
    rows = block_count * row_share
    near, far = len(NEAR), len(FAR)
    parts = 2 * CAP * SEGMENT
    back_shape = (seq_count, parts + 2 * room, head_dim)
    group = 8
    back, *near_rows, grad_rows = pl.pallas_call(
        lambda *refs: grads_kernel(scale, group, *refs),
        out_shape=(
            jax.ShapeDtypeStruct(back_shape, bf16),
            *[jax.ShapeDtypeStruct((far, rows, 2 * head_dim), bf16)] * near,
            jax.ShapeDtypeStruct((block_count * block_len, 2 * head_dim), bf16),
        ),
        in_specs=[spec(SMEM), spec(SMEM), spec(HBM), spec(VMEM), spec(VMEM), spec(VMEM)],
        out_specs=(spec(HBM),) * (near + 2),
        scratch_shapes=[
            pltpu.VMEM(arrived.shape, bf16),
            pltpu.VMEM((seq_count, parts, head_dim), bf16),
            pltpu.VMEM((block_count * block_len, 2 * head_dim), bf16),
            pltpu.VMEM((near, far, rows, 2 * head_dim), bf16),
            pltpu.VMEM((block_count, block_len, head_dim), f32),
            pltpu.VMEM((block_count, block_len, head_dim), f32),
            pltpu.SemaphoreType.DMA((seq_count // group,)),
            pltpu.SemaphoreType.DMA((near + 1,)),
            pltpu.SemaphoreType.DMA,
        ],
        compiler_params=params(LARGE_LIMIT),
        name="grads",
    )(blocks, taken_from, arrived, kv, own_stats, other_stats)

    back, *near_weights = lax.optimization_barrier((back, *near_weights))
    near_rows = [r if a == 0 else shifted(r, a) for a, r in zip(NEAR, near_rows)]
    back = pl.pallas_call(
        lambda *refs: weigh_kernel(parts, *refs),
        out_shape=jax.ShapeDtypeStruct(back_shape, bf16),
        in_specs=[spec(VMEM), spec(VMEM), spec(HBM)],
        out_specs=spec(HBM),
        scratch_shapes=[pltpu.VMEM((seq_count, 2 * room, head_dim), bf16), pltpu.SemaphoreType.DMA],
        input_output_aliases={2: 0},
        compiler_params=params(LARGE_LIMIT),
        name="weigh",
    )(grad_rows, enc_t, back)
    returned = lax.all_to_all(back, "seq", split_axis=0, concat_axis=0, tiled=True)
    own, *far_sums = pl.pallas_call(
        project_kernel,
        out_shape=(
            jax.ShapeDtypeStruct((rows, enc_width), f32),
            *[jax.ShapeDtypeStruct((rows, enc_width), bf16)] * (far - 1),
        ),
        in_specs=[spec(VMEM)] * (2 * near),
        out_specs=(spec(VMEM),) * far,
        compiler_params=params(),
        cost_estimate=pl.CostEstimate(flops=6 * 10**10, bytes_accessed=2 * 10**6, transcendentals=0),
        name="project",
    )(*near_rows, *near_weights)
    attended, query_grad, key_weight_grad, value_weight_grad = pl.pallas_call(
        finish_kernel,
        out_shape=(
            jax.ShapeDtypeStruct((segments, SEGMENT, head_dim), bf16),
            jax.ShapeDtypeStruct((segments, SEGMENT, head_dim), bf16),
            jax.ShapeDtypeStruct((share, head_dim), f32),
            jax.ShapeDtypeStruct((share, head_dim), f32),
        ),
        in_specs=[spec(SMEM), spec(VMEM)],
        out_specs=(spec(VMEM),) * 4,
        compiler_params=params(),
        name="finish",
    )(slots, returned)
    encoding_grad = pl.pallas_call(
        total_kernel,
        out_shape=jax.ShapeDtypeStruct((rows, enc_width), f32),
        in_specs=[*[spec(VMEM)] * far, spec(HBM)],
        out_specs=spec(VMEM),
        compiler_params=params(),
        name="total",
    )(own, *[shifted(part, b) for b, part in zip(FAR[1:], far_sums)], key_weight_grad)
    return (
        attended.reshape(segments * SEGMENT, head_dim),
        query_grad.reshape(segments * SEGMENT, head_dim),
        encoding_grad.reshape(block_count, row_share, enc_width),
        key_weight_grad,
        value_weight_grad,
    )


def solution(mesh):
    in_specs = (
        P("seq", "head"),
        P("seq", None, None),
        P(None, "head"),
        P(None, "head"),
        P(),
        P("seq", "head"),
    )
    out_specs = (
        P("seq", "head"),
        P("seq", "head"),
        P("seq", "head", None),
        P("seq", "head"),
        P("seq", "head"),
    )
    return jax.shard_map(
        on_device, mesh=mesh, in_specs=in_specs, out_specs=out_specs, check_vma=False
    )
```

```python
import math

import jax
import jax.numpy as jnp
from jax import lax
from jax.experimental import pallas as pl
from jax.experimental.pallas import tpu as pltpu
from jax.sharding import PartitionSpec as P

SEGMENT = 64
NEIGH = 2
CAP = 2
PLACES = 8
NEAR = (0, 1, -1, 2)
FAR = (0, 4, 8, -4)
VMEM_LIMIT = 40 * 1024 * 1024
LARGE_LIMIT = 60 * 1024 * 1024
SMALL_LIMIT = 16 * 1024 * 1024
VMEM = pltpu.VMEM
SMEM = pltpu.SMEM
HBM = pltpu.HBM


def params(limit=VMEM_LIMIT):
    return pltpu.CompilerParams(vmem_limit_bytes=limit)


def spec(space):
    return pl.BlockSpec(memory_space=space)


def nt_dot(a, b):
    return lax.dot_general(a, b, (((1,), (1,)), ((), ())), preferred_element_type=jnp.float32)


def tn_dot(a, b):
    return lax.dot_general(a, b, (((0,), (0,)), ((), ())), preferred_element_type=jnp.float32)


def nn_dot(a, b):
    return jnp.dot(a, b, preferred_element_type=jnp.float32)


def pack_kernel(block_count, reads_ref, q_ref, g_ref, out_ref, slots_ref, used, stage, sem):
    seq_count = used.shape[0]
    read_count = slots_ref.shape[0]
    first = lax.axis_index("seq") * (read_count // NEIGH)

    def leave(slot):
        pltpu.make_async_copy(stage.at[slot], out_ref.at[slot], sem).start()

    for h in range(seq_count):
        used[h] = 0
    for j in range(read_count):
        holder = lax.div(reads_ref[j % NEIGH, first + j // NEIGH], block_count)
        rank = used[holder]
        used[holder] = rank + 1
        slot = holder * CAP + rank
        slots_ref[j] = slot
        stage[slot, 0] = q_ref[j // NEIGH]
        stage[slot, 1] = g_ref[j // NEIGH]
        leave(slot)

    def blank(h, _):
        for k in range(CAP):
            @pl.when(used[h] <= k)
            def _():
                stage[h * CAP + k] = jnp.zeros(stage.shape[1:], stage.dtype)
                leave(h * CAP + k)

        return 0

    lax.fori_loop(0, seq_count, blank, 0)
    pltpu.make_async_copy(stage, out_ref, sem).wait()


def pair_operands(x_ref, s, kv_a, kv_b):
    head_dim = x_ref.shape[3]

    def diagonal(i):
        one, two = x_ref[CAP * s, i], x_ref[CAP * s + 1, i]
        zero = jnp.zeros_like(one)
        return jnp.concatenate(
            [jnp.concatenate([one, zero], axis=1), jnp.concatenate([zero, two], axis=1)], axis=0
        )

    keys = jnp.concatenate([kv_a[:, :head_dim], kv_b[:, :head_dim]], axis=1)
    values = jnp.concatenate([kv_a[:, head_dim:], kv_b[:, head_dim:]], axis=1)
    return diagonal(0), diagonal(1), keys, values


def stats_kernel(scale, blocks_ref, to_ref, x_ref, kv_ref, pair_ref, slot_ref, send_ref, places):
    places[...] = jnp.zeros_like(places)
    left = lax.broadcasted_iota(jnp.int32, (1, CAP * SEGMENT), 1) < SEGMENT
    for s in range(x_ref.shape[0] // CAP):
        kv_a = kv_ref[blocks_ref[CAP * s]]
        kv_b = kv_ref[blocks_ref[CAP * s + 1]]
        q_diag, g_diag, keys, values = pair_operands(x_ref, s, kv_a, kv_b)
        scores = nt_dot(keys, q_diag) * scale
        top = jnp.max(scores, axis=0, keepdims=True)
        weight = jnp.exp(scores - top)
        total = jnp.sum(weight, axis=0, keepdims=True)
        prob_grad = nt_dot(values, g_diag)
        mean = jnp.sum(weight * prob_grad, axis=0, keepdims=True) / total
        lse = top + jnp.log(total)
        pair_ref[s] = jnp.concatenate([lse, mean], axis=0)
        row_a = jnp.where(left, lse, pltpu.roll(mean, SEGMENT, 1))
        row_b = jnp.where(left, pltpu.roll(lse, SEGMENT, 1), mean)
        slot_ref[CAP * s:CAP * s + 1, :] = row_a
        slot_ref[CAP * s + 1:CAP * s + 2, :] = row_b
        places[pl.ds(to_ref[CAP * s], 1), :] = row_a
        places[pl.ds(to_ref[CAP * s + 1], 1), :] = row_b
    send_ref[...] = places[:send_ref.shape[0]]


def swap_kernel(slots_ref, in_ref, out_ref):
    out_ref[...] = jnp.zeros_like(out_ref)
    for c in range(slots_ref.shape[0] // NEIGH):
        slot_a, slot_b = slots_ref[NEIGH * c], slots_ref[NEIGH * c + 1]
        out_ref[pl.ds(slot_a, 1), :] = in_ref[pl.ds(slot_b, 1), :]
        out_ref[pl.ds(slot_b, 1), :] = in_ref[pl.ds(slot_a, 1), :]


def merge_stats(own, row_a, row_b, left):
    other_lse = jnp.where(left, row_a, pltpu.roll(row_b, SEGMENT, 1))
    other_mean = jnp.where(left, pltpu.roll(row_a, SEGMENT, 1), row_b)
    lse, mean = own[0:1], own[1:2]
    top = jnp.maximum(lse, other_lse)
    merged = top + jnp.log(jnp.exp(lse - top) + jnp.exp(other_lse - top))
    delta = jnp.exp(lse - merged) * mean + jnp.exp(other_lse - merged) * other_mean
    return merged, delta


def grads_kernel(scale, group, blocks_ref, from_ref, x_hbm, kv_ref, own_ref, other_ref, *refs):
    near = len(NEAR)
    out_ref = refs[0]
    rows_refs = refs[1:1 + near]
    all_ref, x_ref, stage, rows_all, rows_near, acc_k, acc_v, x_sems, rows_sems, out_sem = refs[1 + near:]
    head_dim = kv_ref.shape[2] // 2
    seq_count = x_ref.shape[0] // CAP
    pair = CAP * SEGMENT
    parts = 2 * pair

    def arrival(i):
        at = pl.ds(i * group * CAP, group * CAP)
        return pltpu.make_async_copy(x_hbm.at[at], x_ref.at[at], x_sems.at[i])

    for i in range(seq_count // group):
        arrival(i).start()
    acc_k[...] = jnp.zeros_like(acc_k)
    acc_v[...] = jnp.zeros_like(acc_v)
    left = lax.broadcasted_iota(jnp.int32, (1, pair), 1) < SEGMENT

    def step(i, _):
        arrival(i).wait()
        sources = [i * group + g for g in range(group)]
        first = [blocks_ref[CAP * s] for s in sources]
        second = [blocks_ref[CAP * s + 1] for s in sources]
        operands = [
            pair_operands(x_ref, s, kv_ref[a], kv_ref[b]) for s, a, b in zip(sources, first, second)
        ]
        stats = [
            merge_stats(
                own_ref[s],
                other_ref[pl.ds(from_ref[CAP * s], 1), :],
                other_ref[pl.ds(from_ref[CAP * s + 1], 1), :],
                left,
            )
            for s in sources
        ]
        scores = [nt_dot(keys, q) * scale for q, _, keys, _ in operands]
        prob_grads = [nt_dot(values, g) for _, g, _, values in operands]
        probs = [jnp.exp(x - stat[0]) for x, stat in zip(scores, stats)]
        score_grads = [
            (p * (x - stat[1]) * scale).astype(jnp.bfloat16)
            for p, x, stat in zip(probs, prob_grads, stats)
        ]
        probs = [p.astype(jnp.bfloat16) for p in probs]
        attended = [tn_dot(p, ops[3]).astype(jnp.bfloat16) for p, ops in zip(probs, operands)]
        query_grads = [tn_dot(x, ops[2]).astype(jnp.bfloat16) for x, ops in zip(score_grads, operands)]
        value_parts = [nn_dot(p, ops[1]) for p, ops in zip(probs, operands)]
        key_parts = [nn_dot(x, ops[0]) for x, ops in zip(score_grads, operands)]
        for s, att, grad in zip(sources, attended, query_grads):
            stage[s, :SEGMENT] = att[:SEGMENT, :head_dim]
            stage[s, SEGMENT:pair] = grad[:SEGMENT, :head_dim]
            stage[s, pair:pair + SEGMENT] = att[SEGMENT:, head_dim:]
            stage[s, pair + SEGMENT:parts] = grad[SEGMENT:, head_dim:]
        for a, b, key_part, value_part in zip(first, second, key_parts, value_parts):
            acc_k[a] += key_part[:, :head_dim]
            acc_v[a] += value_part[:, :head_dim]
            acc_k[b] += key_part[:, head_dim:]
            acc_v[b] += value_part[:, head_dim:]
        at = pl.ds(i * group, group)
        pltpu.make_async_copy(stage.at[at], out_ref.at[at, :parts], out_sem).start()
        return 0

    lax.fori_loop(0, seq_count // group, step, 0)
    head_count = near * len(FAR)
    block_count, block_len, _ = acc_k.shape
    row_share = block_len // head_count
    z = lax.axis_index("head")
    rows_copies = []
    for i, a in enumerate(NEAR):
        for j, b in enumerate(FAR):
            dest = lax.rem(z + (a + b + head_count), head_count)
            at = pl.ds(pl.multiple_of(dest * row_share, row_share), row_share)
            rows = jnp.concatenate([acc_k[:, at, :], acc_v[:, at, :]], axis=2)
            rows_near[i, j] = rows.reshape(block_count * row_share, 2 * head_dim).astype(jnp.bfloat16)
        rows_copies.append(pltpu.make_async_copy(rows_near.at[i], rows_refs[i], rows_sems.at[i]))
        rows_copies[i].start()
    rows_all[:, :head_dim] = acc_k[...].reshape(-1, head_dim).astype(jnp.bfloat16)
    rows_all[:, head_dim:] = acc_v[...].reshape(-1, head_dim).astype(jnp.bfloat16)
    rows_copies.append(pltpu.make_async_copy(rows_all, all_ref, rows_sems.at[near]))
    rows_copies[near].start()
    for copy in rows_copies:
        copy.wait()
    pltpu.make_async_copy(stage, out_ref.at[:, :parts], out_sem).wait()


def weigh_kernel(parts, rows_ref, enc_hbm, back_ref, out_ref, enc_t, stage, enc_sems, sem):
    head_dim = rows_ref.shape[1] // 2
    seq_count, room = stage.shape[0], stage.shape[1] // 2
    share = enc_t.shape[0] // seq_count
    batch = seq_count // enc_sems.shape[0]

    def fetch(i):
        at = pl.ds(i * batch * share, batch * share)
        return pltpu.make_async_copy(enc_hbm.at[at], enc_t.at[at], enc_sems.at[i])

    for i in range(enc_sems.shape[0]):
        fetch(i).start()
    for i in range(enc_sems.shape[0]):
        fetch(i).wait()
        term = nn_dot(enc_t[i * batch * share:(i + 1) * batch * share], rows_ref[...])
        for s in range(batch):
            part = term[s * share:(s + 1) * share]
            if room > share:
                part = jnp.concatenate([part, jnp.zeros((room - share, 2 * head_dim), jnp.float32)], axis=0)
            part = part.astype(jnp.bfloat16)
            stage[i * batch + s, :room] = part[:, :head_dim]
            stage[i * batch + s, room:] = part[:, head_dim:]
        at = pl.ds(i * batch, batch)
        pltpu.make_async_copy(stage.at[at], out_ref.at[at, parts:], sem).start()
    pltpu.make_async_copy(stage, out_ref.at[:, parts:], sem).wait()


def finish_kernel(slots_ref, in_ref, own_ref, one_ref, two_ref, three_ref, att_ref, qg_ref, enc_ref, kw_ref, vw_ref):
    share = kw_ref.shape[0]
    parts = 2 * CAP * SEGMENT
    room = (in_ref.shape[1] - parts) // 2

    def step(c, _):
        slot_a, slot_b = slots_ref[NEIGH * c], slots_ref[NEIGH * c + 1]

        def part(slot):
            holder = lax.div(slot, CAP)
            row = pl.multiple_of((slot - holder * CAP) * 2 * SEGMENT, 2 * SEGMENT)
            return in_ref[holder, pl.ds(row, 2 * SEGMENT), :].astype(jnp.float32)

        total = (part(slot_a) + part(slot_b)).astype(jnp.bfloat16)
        att_ref[c] = total[:SEGMENT]
        qg_ref[c] = total[SEGMENT:]
        return 0

    lax.fori_loop(0, att_ref.shape[0], step, 0, unroll=4)
    total = in_ref[0, parts:, :].astype(jnp.float32)
    for s in range(1, in_ref.shape[0]):
        total = total + in_ref[s, parts:, :].astype(jnp.float32)
    kw_ref[...] = total[:share]
    vw_ref[...] = total[room:room + share]
    total = own_ref[...] + one_ref[...].astype(jnp.float32)
    enc_ref[...] = total + two_ref[...].astype(jnp.float32) + three_ref[...].astype(jnp.float32)


def project_kernel(*refs):
    near = len(NEAR)
    rows_hbm, weights_hbm, own_ref, far_refs = refs[:near], refs[near:2 * near], refs[2 * near], refs[2 * near + 1:-3]
    rows_ref, weights_ref, sems = refs[-3:]
    _, far, rows, width = rows_ref.shape
    copies = []
    for n in range(near):
        copies.append(pltpu.make_async_copy(weights_hbm[n], weights_ref.at[n], sems.at[n]))
        copies.append(pltpu.make_async_copy(rows_hbm[n], rows_ref.at[n], sems.at[near + n]))
    for copy in copies:
        copy.start()
    for copy in copies:
        copy.wait()
    half = far // 2
    for i in range(0, far, half):
        total = jnp.zeros((half * rows, own_ref.shape[1]), jnp.float32)
        for n in range(near):
            total = total + nt_dot(rows_ref[n, i:i + half].reshape(half * rows, width), weights_ref[n])
        for j in range(half):
            part = total[j * rows:(j + 1) * rows]
            if i + j == 0:
                own_ref[...] = part
            else:
                far_refs[i + j - 1][...] = part.astype(jnp.bfloat16)


def shifted(x, step):
    count = lax.axis_size("head")
    return lax.ppermute(x, "head", [(z, (z + step) % count) for z in range(count)])


def on_device(queries, encodings, key_weight, value_weight, reads, out_grad):
    seq_count = lax.axis_size("seq")
    head_count = lax.axis_size("head")
    me = lax.axis_index("seq")
    block_count, block_len, enc_width = encodings.shape
    head_dim = key_weight.shape[1]
    segments = queries.shape[0] // SEGMENT
    read_count = NEIGH * segments
    slot_count = seq_count * CAP
    scale = 1.0 / math.sqrt(head_dim)
    bf16, f32 = jnp.bfloat16, jnp.float32

    packed, slots = pl.pallas_call(
        lambda *refs: pack_kernel(block_count, *refs),
        out_shape=(
            jax.ShapeDtypeStruct((slot_count, 2, SEGMENT, head_dim), bf16),
            jax.ShapeDtypeStruct((read_count,), jnp.int32),
        ),
        in_specs=[spec(SMEM), spec(VMEM), spec(VMEM)],
        out_specs=(spec(HBM), spec(SMEM)),
        scratch_shapes=[
            pltpu.SMEM((seq_count,), jnp.int32),
            pltpu.VMEM((slot_count, 2, SEGMENT, head_dim), bf16),
            pltpu.SemaphoreType.DMA,
        ],
        compiler_params=params(LARGE_LIMIT),
        name="pack",
    )(
        reads.T,
        queries.reshape(segments, SEGMENT, head_dim),
        out_grad.reshape(segments, SEGMENT, head_dim),
    )
    arrived = lax.all_to_all(packed, "seq", split_axis=0, concat_axis=0, tiled=True)

    key_weight, value_weight, slots = lax.optimization_barrier((key_weight, value_weight, slots))
    weights = jnp.concatenate([key_weight, value_weight], axis=1)
    flat_enc = encodings.reshape(block_count * block_len, enc_width)
    kv = jnp.dot(flat_enc, weights, preferred_element_type=f32).astype(bf16)
    kv = kv.reshape(block_count, block_len, 2 * head_dim)
    share = enc_width // seq_count
    room = -(-share // 16) * 16
    enc_t = flat_enc.T

    tables = reads.reshape(seq_count, read_count)
    holders = tables // block_count
    partners = holders.reshape(-1, NEIGH)[:, ::-1].reshape(seq_count, read_count)
    mine = holders == me
    rank = jnp.cumsum(mine.astype(jnp.int32), axis=1)
    code = (tables % block_count) + (partners + 1) * block_count
    code = jnp.stack(
        [jnp.sum(jnp.where(mine & (rank == k + 1), code, 0), axis=1) for k in range(CAP)], axis=1
    ).reshape(slot_count)
    blocks = code % block_count
    partner = code // block_count - 1
    taken = partner >= 0
    order = jnp.arange(slot_count)
    same = (partner[:, None] == partner[None, :]) & (order[None, :] < order[:, None])
    place = jnp.sum(same.astype(jnp.int32), axis=1)
    twin = place.reshape(-1, CAP)[:, ::-1].reshape(slot_count)
    send_to = jnp.where(taken, partner * PLACES + jnp.minimum(place, PLACES - 1), seq_count * PLACES)
    taken_from = jnp.minimum(jnp.where(partner == me, twin, place), PLACES - 1)
    taken_from = jnp.where(taken, partner * PLACES + taken_from, 0)
    pairs = jax.nn.one_hot(holders.reshape(-1, NEIGH), seq_count, dtype=bf16)
    shared = lax.dot_general(
        pairs[:, 0], pairs[:, 1], (((0,), (0,)), ((), ())), preferred_element_type=f32
    )
    fits = jnp.max(shared + shared.T) <= PLACES
    taken_from = jnp.where(fits, taken_from, order)
    kv, enc_t, blocks, send_to, taken_from, fits, weights = lax.optimization_barrier(
        (kv, enc_t, blocks, send_to, taken_from, fits, weights)
    )
    near_weights = [weights if a == 0 else shifted(weights, a) for a in NEAR]

    place_count = seq_count * PLACES
    own_stats, slot_stats, sent = pl.pallas_call(
        lambda *refs: stats_kernel(scale, *refs),
        out_shape=(
            jax.ShapeDtypeStruct((seq_count, 2, CAP * SEGMENT), f32),
            jax.ShapeDtypeStruct((slot_count, CAP * SEGMENT), f32),
            jax.ShapeDtypeStruct((place_count, CAP * SEGMENT), f32),
        ),
        in_specs=[spec(SMEM), spec(SMEM), spec(VMEM), spec(VMEM)],
        out_specs=(spec(VMEM),) * 3,
        scratch_shapes=[pltpu.VMEM((place_count + 8, CAP * SEGMENT), f32)],
        compiler_params=params(),
        name="stats",
    )(blocks, send_to, arrived, kv)

    def one_hop(sent, slot_stats, slots):
        return lax.all_to_all(sent, "seq", split_axis=0, concat_axis=0, tiled=True)

    def two_hops(sent, slot_stats, slots):
        at_reader = lax.all_to_all(slot_stats, "seq", split_axis=0, concat_axis=0, tiled=True)
        swapped = pl.pallas_call(
            swap_kernel,
            out_shape=jax.ShapeDtypeStruct(slot_stats.shape, f32),
            in_specs=[spec(SMEM), spec(VMEM)],
            out_specs=spec(VMEM),
            compiler_params=params(),
            name="swap",
        )(slots, at_reader)
        swapped = lax.all_to_all(swapped, "seq", split_axis=0, concat_axis=0, tiled=True)
        return jnp.pad(swapped, ((0, place_count - slot_count), (0, 0)))

    other_stats = lax.cond(fits, one_hop, two_hops, sent, slot_stats, slots)

    row_share = block_len // head_count
    rows = block_count * row_share
    near, far = len(NEAR), len(FAR)
    parts = 2 * CAP * SEGMENT
    back_shape = (seq_count, parts + 2 * room, head_dim)
    group = 8
    back, *near_rows, grad_rows = pl.pallas_call(
        lambda *refs: grads_kernel(scale, group, *refs),
        out_shape=(
            jax.ShapeDtypeStruct(back_shape, bf16),
            *[jax.ShapeDtypeStruct((far, rows, 2 * head_dim), bf16)] * near,
            jax.ShapeDtypeStruct((block_count * block_len, 2 * head_dim), bf16),
        ),
        in_specs=[spec(SMEM), spec(SMEM), spec(HBM), spec(VMEM), spec(VMEM), spec(VMEM)],
        out_specs=(spec(HBM),) * (near + 2),
        scratch_shapes=[
            pltpu.VMEM(arrived.shape, bf16),
            pltpu.VMEM((seq_count, parts, head_dim), bf16),
            pltpu.VMEM((block_count * block_len, 2 * head_dim), bf16),
            pltpu.VMEM((near, far, rows, 2 * head_dim), bf16),
            pltpu.VMEM((block_count, block_len, head_dim), f32),
            pltpu.VMEM((block_count, block_len, head_dim), f32),
            pltpu.SemaphoreType.DMA((seq_count // group,)),
            pltpu.SemaphoreType.DMA((near + 1,)),
            pltpu.SemaphoreType.DMA,
        ],
        compiler_params=params(LARGE_LIMIT),
        name="grads",
    )(blocks, taken_from, arrived, kv, own_stats, other_stats)

    back, *near_weights = lax.optimization_barrier((back, *near_weights))
    near_rows = [r if a == 0 else shifted(r, a) for a, r in zip(NEAR, near_rows)]
    back = pl.pallas_call(
        lambda *refs: weigh_kernel(parts, *refs),
        out_shape=jax.ShapeDtypeStruct(back_shape, bf16),
        in_specs=[spec(VMEM), spec(HBM), spec(HBM)],
        out_specs=spec(HBM),
        scratch_shapes=[
            pltpu.VMEM(enc_t.shape, bf16),
            pltpu.VMEM((seq_count, 2 * room, head_dim), bf16),
            pltpu.SemaphoreType.DMA((4,)),
            pltpu.SemaphoreType.DMA,
        ],
        input_output_aliases={2: 0},
        compiler_params=params(LARGE_LIMIT),
        name="weigh",
    )(grad_rows, enc_t, back)
    returned = lax.all_to_all(back, "seq", split_axis=0, concat_axis=0, tiled=True)
    own, *far_sums = pl.pallas_call(
        project_kernel,
        out_shape=(
            jax.ShapeDtypeStruct((rows, enc_width), f32),
            *[jax.ShapeDtypeStruct((rows, enc_width), bf16)] * (far - 1),
        ),
        in_specs=[spec(HBM)] * (2 * near),
        out_specs=(spec(VMEM),) * far,
        scratch_shapes=[
            pltpu.VMEM((near, far, rows, 2 * head_dim), bf16),
            pltpu.VMEM((near, enc_width, 2 * head_dim), bf16),
            pltpu.SemaphoreType.DMA((2 * near,)),
        ],
        compiler_params=params(SMALL_LIMIT),
        cost_estimate=pl.CostEstimate(flops=6 * 10**10, bytes_accessed=2 * 10**6, transcendentals=0),
        name="project",
    )(*near_rows, *near_weights)
    far_sums = [shifted(part, b) for b, part in zip(FAR[1:], far_sums)]
    attended, query_grad, encoding_grad, key_weight_grad, value_weight_grad = pl.pallas_call(
        finish_kernel,
        out_shape=(
            jax.ShapeDtypeStruct((segments, SEGMENT, head_dim), bf16),
            jax.ShapeDtypeStruct((segments, SEGMENT, head_dim), bf16),
            jax.ShapeDtypeStruct((rows, enc_width), f32),
            jax.ShapeDtypeStruct((share, head_dim), f32),
            jax.ShapeDtypeStruct((share, head_dim), f32),
        ),
        in_specs=[spec(SMEM), *[spec(VMEM)] * (1 + far)],
        out_specs=(spec(VMEM),) * 5,
        compiler_params=params(),
        name="finish",
    )(slots, returned, own, *far_sums)
    return (
        attended.reshape(segments * SEGMENT, head_dim),
        query_grad.reshape(segments * SEGMENT, head_dim),
        encoding_grad.reshape(block_count, row_share, enc_width),
        key_weight_grad,
        value_weight_grad,
    )


def solution(mesh):
    in_specs = (
        P("seq", "head"),
        P("seq", None, None),
        P(None, "head"),
        P(None, "head"),
        P(),
        P("seq", "head"),
    )
    out_specs = (
        P("seq", "head"),
        P("seq", "head"),
        P("seq", "head", None),
        P("seq", "head"),
        P("seq", "head"),
    )
    return jax.shard_map(
        on_device, mesh=mesh, in_specs=in_specs, out_specs=out_specs, check_vma=False
    )
```

```python
import math

import jax
import jax.numpy as jnp
from jax import lax
from jax.experimental import pallas as pl
from jax.experimental.pallas import tpu as pltpu
from jax.sharding import PartitionSpec as P

SEGMENT = 64
NEIGH = 2
CAP = 2
PLACES = 8
NEAR = (0, 1, -1, 2)
FAR = (0, 4, 8, -4)
VMEM_LIMIT = 40 * 1024 * 1024
LARGE_LIMIT = 60 * 1024 * 1024
SMALL_LIMIT = 16 * 1024 * 1024
VMEM = pltpu.VMEM
SMEM = pltpu.SMEM
HBM = pltpu.HBM


def params(limit=VMEM_LIMIT):
    return pltpu.CompilerParams(vmem_limit_bytes=limit)


def spec(space):
    return pl.BlockSpec(memory_space=space)


def nt_dot(a, b):
    return lax.dot_general(a, b, (((1,), (1,)), ((), ())), preferred_element_type=jnp.float32)


def tn_dot(a, b):
    return lax.dot_general(a, b, (((0,), (0,)), ((), ())), preferred_element_type=jnp.float32)


def nn_dot(a, b):
    return jnp.dot(a, b, preferred_element_type=jnp.float32)


def pack_kernel(block_count, reads_ref, q_ref, g_ref, out_ref, slots_ref, used, stage, sem):
    seq_count = used.shape[0]
    read_count = slots_ref.shape[0]
    first = lax.axis_index("seq") * (read_count // NEIGH)

    def leave(slot):
        pltpu.make_async_copy(stage.at[slot], out_ref.at[slot], sem).start()

    for h in range(seq_count):
        used[h] = 0
    for j in range(read_count):
        holder = lax.div(reads_ref[j % NEIGH, first + j // NEIGH], block_count)
        rank = used[holder]
        used[holder] = rank + 1
        slot = holder * CAP + rank
        slots_ref[j] = slot
        stage[slot, 0] = q_ref[j // NEIGH]
        stage[slot, 1] = g_ref[j // NEIGH]
        leave(slot)

    def blank(h, _):
        for k in range(CAP):
            @pl.when(used[h] <= k)
            def _():
                stage[h * CAP + k] = jnp.zeros(stage.shape[1:], stage.dtype)
                leave(h * CAP + k)

        return 0

    lax.fori_loop(0, seq_count, blank, 0)
    pltpu.make_async_copy(stage, out_ref, sem).wait()


def pair_operands(x_ref, s, kv_a, kv_b):
    head_dim = x_ref.shape[3]

    def diagonal(i):
        one, two = x_ref[CAP * s, i], x_ref[CAP * s + 1, i]
        zero = jnp.zeros_like(one)
        return jnp.concatenate(
            [jnp.concatenate([one, zero], axis=1), jnp.concatenate([zero, two], axis=1)], axis=0
        )

    keys = jnp.concatenate([kv_a[:, :head_dim], kv_b[:, :head_dim]], axis=1)
    values = jnp.concatenate([kv_a[:, head_dim:], kv_b[:, head_dim:]], axis=1)
    return diagonal(0), diagonal(1), keys, values


def stats_kernel(scale, blocks_ref, to_ref, x_ref, kv_ref, pair_ref, slot_ref, send_ref, places):
    places[...] = jnp.zeros_like(places)
    left = lax.broadcasted_iota(jnp.int32, (1, CAP * SEGMENT), 1) < SEGMENT
    for s in range(x_ref.shape[0] // CAP):
        kv_a = kv_ref[blocks_ref[CAP * s]]
        kv_b = kv_ref[blocks_ref[CAP * s + 1]]
        q_diag, g_diag, keys, values = pair_operands(x_ref, s, kv_a, kv_b)
        scores = nt_dot(keys, q_diag) * scale
        top = jnp.max(scores, axis=0, keepdims=True)
        weight = jnp.exp(scores - top)
        total = jnp.sum(weight, axis=0, keepdims=True)
        prob_grad = nt_dot(values, g_diag)
        mean = jnp.sum(weight * prob_grad, axis=0, keepdims=True) / total
        lse = top + jnp.log(total)
        pair_ref[s] = jnp.concatenate([lse, mean], axis=0)
        row_a = jnp.where(left, lse, pltpu.roll(mean, SEGMENT, 1))
        row_b = jnp.where(left, pltpu.roll(lse, SEGMENT, 1), mean)
        slot_ref[CAP * s:CAP * s + 1, :] = row_a
        slot_ref[CAP * s + 1:CAP * s + 2, :] = row_b
        places[pl.ds(to_ref[CAP * s], 1), :] = row_a
        places[pl.ds(to_ref[CAP * s + 1], 1), :] = row_b
    send_ref[...] = places[:send_ref.shape[0]]


def swap_kernel(slots_ref, in_ref, out_ref):
    out_ref[...] = jnp.zeros_like(out_ref)
    for c in range(slots_ref.shape[0] // NEIGH):
        slot_a, slot_b = slots_ref[NEIGH * c], slots_ref[NEIGH * c + 1]
        out_ref[pl.ds(slot_a, 1), :] = in_ref[pl.ds(slot_b, 1), :]
        out_ref[pl.ds(slot_b, 1), :] = in_ref[pl.ds(slot_a, 1), :]


def merge_stats(own, row_a, row_b, left):
    other_lse = jnp.where(left, row_a, pltpu.roll(row_b, SEGMENT, 1))
    other_mean = jnp.where(left, pltpu.roll(row_a, SEGMENT, 1), row_b)
    lse, mean = own[0:1], own[1:2]
    top = jnp.maximum(lse, other_lse)
    merged = top + jnp.log(jnp.exp(lse - top) + jnp.exp(other_lse - top))
    delta = jnp.exp(lse - merged) * mean + jnp.exp(other_lse - merged) * other_mean
    return merged, delta


def grads_kernel(scale, group, blocks_ref, from_ref, x_hbm, kv_ref, own_ref, other_ref, enc_hbm, *refs):
    near = len(NEAR)
    out_ref = refs[0]
    rows_refs = refs[1:1 + near]
    x_ref, stage, enc_t, rows_all, rows_near, acc_k, acc_v, x_sems, enc_sem, rows_sems, out_sem = refs[1 + near:]
    head_dim = kv_ref.shape[2] // 2
    seq_count = x_ref.shape[0] // CAP
    pair = CAP * SEGMENT
    parts = 2 * pair

    def arrival(i):
        at = pl.ds(i * group * CAP, group * CAP)
        return pltpu.make_async_copy(x_hbm.at[at], x_ref.at[at], x_sems.at[i])

    for i in range(seq_count // group):
        arrival(i).start()
    fetch = pltpu.make_async_copy(enc_hbm, enc_t, enc_sem)
    fetch.start()
    acc_k[...] = jnp.zeros_like(acc_k)
    acc_v[...] = jnp.zeros_like(acc_v)
    left = lax.broadcasted_iota(jnp.int32, (1, pair), 1) < SEGMENT

    def step(i, _):
        arrival(i).wait()
        sources = [i * group + g for g in range(group)]
        first = [blocks_ref[CAP * s] for s in sources]
        second = [blocks_ref[CAP * s + 1] for s in sources]
        operands = [
            pair_operands(x_ref, s, kv_ref[a], kv_ref[b]) for s, a, b in zip(sources, first, second)
        ]
        stats = [
            merge_stats(
                own_ref[s],
                other_ref[pl.ds(from_ref[CAP * s], 1), :],
                other_ref[pl.ds(from_ref[CAP * s + 1], 1), :],
                left,
            )
            for s in sources
        ]
        scores = [nt_dot(keys, q) * scale for q, _, keys, _ in operands]
        prob_grads = [nt_dot(values, g) for _, g, _, values in operands]
        probs = [jnp.exp(x - stat[0]) for x, stat in zip(scores, stats)]
        score_grads = [
            (p * (x - stat[1]) * scale).astype(jnp.bfloat16)
            for p, x, stat in zip(probs, prob_grads, stats)
        ]
        probs = [p.astype(jnp.bfloat16) for p in probs]
        attended = [tn_dot(p, ops[3]).astype(jnp.bfloat16) for p, ops in zip(probs, operands)]
        query_grads = [tn_dot(x, ops[2]).astype(jnp.bfloat16) for x, ops in zip(score_grads, operands)]
        value_parts = [nn_dot(p, ops[1]) for p, ops in zip(probs, operands)]
        key_parts = [nn_dot(x, ops[0]) for x, ops in zip(score_grads, operands)]
        for s, att, grad in zip(sources, attended, query_grads):
            stage[s, :SEGMENT] = att[:SEGMENT, :head_dim]
            stage[s, SEGMENT:pair] = grad[:SEGMENT, :head_dim]
            stage[s, pair:pair + SEGMENT] = att[SEGMENT:, head_dim:]
            stage[s, pair + SEGMENT:parts] = grad[SEGMENT:, head_dim:]
        for a, b, key_part, value_part in zip(first, second, key_parts, value_parts):
            acc_k[a] += key_part[:, :head_dim]
            acc_v[a] += value_part[:, :head_dim]
            acc_k[b] += key_part[:, head_dim:]
            acc_v[b] += value_part[:, head_dim:]
        at = pl.ds(i * group, group)
        pltpu.make_async_copy(stage.at[at, :parts], out_ref.at[at, :parts], out_sem).start()
        return 0

    lax.fori_loop(0, seq_count // group, step, 0)
    head_count = near * len(FAR)
    block_count, block_len, _ = acc_k.shape
    row_share = block_len // head_count
    z = lax.axis_index("head")
    rows_copies = []
    for i, a in enumerate(NEAR):
        for j, b in enumerate(FAR):
            dest = lax.rem(z + (a + b + head_count), head_count)
            at = pl.ds(pl.multiple_of(dest * row_share, row_share), row_share)
            rows = jnp.concatenate([acc_k[:, at, :], acc_v[:, at, :]], axis=2)
            rows_near[i, j] = rows.reshape(block_count * row_share, 2 * head_dim).astype(jnp.bfloat16)
        rows_copies.append(pltpu.make_async_copy(rows_near.at[i], rows_refs[i], rows_sems.at[i]))
        rows_copies[i].start()
    rows_all[:, :head_dim] = acc_k[...].reshape(-1, head_dim).astype(jnp.bfloat16)
    rows_all[:, head_dim:] = acc_v[...].reshape(-1, head_dim).astype(jnp.bfloat16)
    room = (stage.shape[1] - parts) // 2
    share = enc_t.shape[0] // seq_count
    fetch.wait()
    batch = 8
    for i in range(0, seq_count, batch):
        term = nn_dot(enc_t[i * share:(i + batch) * share], rows_all[...])
        for s in range(batch):
            part = term[s * share:(s + 1) * share]
            if room > share:
                part = jnp.concatenate([part, jnp.zeros((room - share, 2 * head_dim), jnp.float32)], axis=0)
            part = part.astype(jnp.bfloat16)
            stage[i + s, parts:parts + room] = part[:, :head_dim]
            stage[i + s, parts + room:] = part[:, head_dim:]
        pltpu.make_async_copy(
            stage.at[i:i + batch, parts:], out_ref.at[i:i + batch, parts:], out_sem
        ).start()
    for copy in rows_copies:
        copy.wait()
    pltpu.make_async_copy(stage, out_ref, out_sem).wait()


def finish_kernel(slots_ref, in_ref, own_ref, one_ref, two_ref, three_ref, att_ref, qg_ref, enc_ref, kw_ref, vw_ref):
    share = kw_ref.shape[0]
    parts = 2 * CAP * SEGMENT
    room = (in_ref.shape[1] - parts) // 2

    def step(c, _):
        slot_a, slot_b = slots_ref[NEIGH * c], slots_ref[NEIGH * c + 1]

        def part(slot):
            holder = lax.div(slot, CAP)
            row = pl.multiple_of((slot - holder * CAP) * 2 * SEGMENT, 2 * SEGMENT)
            return in_ref[holder, pl.ds(row, 2 * SEGMENT), :].astype(jnp.float32)

        total = (part(slot_a) + part(slot_b)).astype(jnp.bfloat16)
        att_ref[c] = total[:SEGMENT]
        qg_ref[c] = total[SEGMENT:]
        return 0

    lax.fori_loop(0, att_ref.shape[0], step, 0, unroll=4)
    total = in_ref[0, parts:, :].astype(jnp.float32)
    for s in range(1, in_ref.shape[0]):
        total = total + in_ref[s, parts:, :].astype(jnp.float32)
    kw_ref[...] = total[:share]
    vw_ref[...] = total[room:room + share]
    total = own_ref[...] + one_ref[...].astype(jnp.float32)
    enc_ref[...] = total + two_ref[...].astype(jnp.float32) + three_ref[...].astype(jnp.float32)


def project_kernel(*refs):
    near = len(NEAR)
    rows_hbm, weights_hbm, own_ref, far_refs = refs[:near], refs[near:2 * near], refs[2 * near], refs[2 * near + 1:-3]
    rows_ref, weights_ref, sems = refs[-3:]
    _, far, rows, width = rows_ref.shape
    copies = []
    for n in range(near):
        copies.append(pltpu.make_async_copy(weights_hbm[n], weights_ref.at[n], sems.at[n]))
        copies.append(pltpu.make_async_copy(rows_hbm[n], rows_ref.at[n], sems.at[near + n]))
    for copy in copies:
        copy.start()
    for copy in copies:
        copy.wait()
    half = far // 2
    for i in range(0, far, half):
        total = jnp.zeros((half * rows, own_ref.shape[1]), jnp.float32)
        for n in range(near):
            total = total + nt_dot(rows_ref[n, i:i + half].reshape(half * rows, width), weights_ref[n])
        for j in range(half):
            part = total[j * rows:(j + 1) * rows]
            if i + j == 0:
                own_ref[...] = part
            else:
                far_refs[i + j - 1][...] = part.astype(jnp.bfloat16)


def shifted(x, step):
    count = lax.axis_size("head")
    return lax.ppermute(x, "head", [(z, (z + step) % count) for z in range(count)])


def on_device(queries, encodings, key_weight, value_weight, reads, out_grad):
    seq_count = lax.axis_size("seq")
    head_count = lax.axis_size("head")
    me = lax.axis_index("seq")
    block_count, block_len, enc_width = encodings.shape
    head_dim = key_weight.shape[1]
    segments = queries.shape[0] // SEGMENT
    read_count = NEIGH * segments
    slot_count = seq_count * CAP
    scale = 1.0 / math.sqrt(head_dim)
    bf16, f32 = jnp.bfloat16, jnp.float32

    packed, slots = pl.pallas_call(
        lambda *refs: pack_kernel(block_count, *refs),
        out_shape=(
            jax.ShapeDtypeStruct((slot_count, 2, SEGMENT, head_dim), bf16),
            jax.ShapeDtypeStruct((read_count,), jnp.int32),
        ),
        in_specs=[spec(SMEM), spec(VMEM), spec(VMEM)],
        out_specs=(spec(HBM), spec(SMEM)),
        scratch_shapes=[
            pltpu.SMEM((seq_count,), jnp.int32),
            pltpu.VMEM((slot_count, 2, SEGMENT, head_dim), bf16),
            pltpu.SemaphoreType.DMA,
        ],
        compiler_params=params(LARGE_LIMIT),
        name="pack",
    )(
        reads.T,
        queries.reshape(segments, SEGMENT, head_dim),
        out_grad.reshape(segments, SEGMENT, head_dim),
    )
    arrived = lax.all_to_all(packed, "seq", split_axis=0, concat_axis=0, tiled=True)

    key_weight, value_weight, slots = lax.optimization_barrier((key_weight, value_weight, slots))
    weights = jnp.concatenate([key_weight, value_weight], axis=1)
    flat_enc = encodings.reshape(block_count * block_len, enc_width)
    kv = jnp.dot(flat_enc, weights, preferred_element_type=f32).astype(bf16)
    kv = kv.reshape(block_count, block_len, 2 * head_dim)
    share = enc_width // seq_count
    room = -(-share // 16) * 16
    enc_t = flat_enc.T

    tables = reads.reshape(seq_count, read_count)
    holders = tables // block_count
    partners = holders.reshape(-1, NEIGH)[:, ::-1].reshape(seq_count, read_count)
    mine = holders == me
    rank = jnp.cumsum(mine.astype(jnp.int32), axis=1)
    code = (tables % block_count) + (partners + 1) * block_count
    code = jnp.stack(
        [jnp.sum(jnp.where(mine & (rank == k + 1), code, 0), axis=1) for k in range(CAP)], axis=1
    ).reshape(slot_count)
    blocks = code % block_count
    partner = code // block_count - 1
    taken = partner >= 0
    order = jnp.arange(slot_count)
    same = (partner[:, None] == partner[None, :]) & (order[None, :] < order[:, None])
    place = jnp.sum(same.astype(jnp.int32), axis=1)
    twin = place.reshape(-1, CAP)[:, ::-1].reshape(slot_count)
    send_to = jnp.where(taken, partner * PLACES + jnp.minimum(place, PLACES - 1), seq_count * PLACES)
    taken_from = jnp.minimum(jnp.where(partner == me, twin, place), PLACES - 1)
    taken_from = jnp.where(taken, partner * PLACES + taken_from, 0)
    pairs = jax.nn.one_hot(holders.reshape(-1, NEIGH), seq_count, dtype=bf16)
    shared = lax.dot_general(
        pairs[:, 0], pairs[:, 1], (((0,), (0,)), ((), ())), preferred_element_type=f32
    )
    fits = jnp.max(shared + shared.T) <= PLACES
    taken_from = jnp.where(fits, taken_from, order)
    kv, enc_t, blocks, send_to, taken_from, fits, weights = lax.optimization_barrier(
        (kv, enc_t, blocks, send_to, taken_from, fits, weights)
    )
    near_weights = [weights if a == 0 else shifted(weights, a) for a in NEAR]

    place_count = seq_count * PLACES
    own_stats, slot_stats, sent = pl.pallas_call(
        lambda *refs: stats_kernel(scale, *refs),
        out_shape=(
            jax.ShapeDtypeStruct((seq_count, 2, CAP * SEGMENT), f32),
            jax.ShapeDtypeStruct((slot_count, CAP * SEGMENT), f32),
            jax.ShapeDtypeStruct((place_count, CAP * SEGMENT), f32),
        ),
        in_specs=[spec(SMEM), spec(SMEM), spec(VMEM), spec(VMEM)],
        out_specs=(spec(VMEM),) * 3,
        scratch_shapes=[pltpu.VMEM((place_count + 8, CAP * SEGMENT), f32)],
        compiler_params=params(),
        name="stats",
    )(blocks, send_to, arrived, kv)

    def one_hop(sent, slot_stats, slots):
        return lax.all_to_all(sent, "seq", split_axis=0, concat_axis=0, tiled=True)

    def two_hops(sent, slot_stats, slots):
        at_reader = lax.all_to_all(slot_stats, "seq", split_axis=0, concat_axis=0, tiled=True)
        swapped = pl.pallas_call(
            swap_kernel,
            out_shape=jax.ShapeDtypeStruct(slot_stats.shape, f32),
            in_specs=[spec(SMEM), spec(VMEM)],
            out_specs=spec(VMEM),
            compiler_params=params(),
            name="swap",
        )(slots, at_reader)
        swapped = lax.all_to_all(swapped, "seq", split_axis=0, concat_axis=0, tiled=True)
        return jnp.pad(swapped, ((0, place_count - slot_count), (0, 0)))

    other_stats = lax.cond(fits, one_hop, two_hops, sent, slot_stats, slots)

    row_share = block_len // head_count
    rows = block_count * row_share
    near, far = len(NEAR), len(FAR)
    back_shape = (seq_count, 2 * CAP * SEGMENT + 2 * room, head_dim)
    group = 8
    back, *near_rows = pl.pallas_call(
        lambda *refs: grads_kernel(scale, group, *refs),
        out_shape=(
            jax.ShapeDtypeStruct(back_shape, bf16),
            *[jax.ShapeDtypeStruct((far, rows, 2 * head_dim), bf16)] * near,
        ),
        in_specs=[spec(SMEM), spec(SMEM), spec(HBM), spec(VMEM), spec(VMEM), spec(VMEM), spec(HBM)],
        out_specs=(spec(HBM), *[spec(HBM)] * near),
        scratch_shapes=[
            pltpu.VMEM(arrived.shape, bf16),
            pltpu.VMEM(back_shape, bf16),
            pltpu.VMEM((enc_width, block_count * block_len), bf16),
            pltpu.VMEM((block_count * block_len, 2 * head_dim), bf16),
            pltpu.VMEM((near, far, rows, 2 * head_dim), bf16),
            pltpu.VMEM((block_count, block_len, head_dim), f32),
            pltpu.VMEM((block_count, block_len, head_dim), f32),
            pltpu.SemaphoreType.DMA((seq_count // group,)),
            pltpu.SemaphoreType.DMA,
            pltpu.SemaphoreType.DMA((near,)),
            pltpu.SemaphoreType.DMA,
        ],
        compiler_params=params(LARGE_LIMIT),
        name="grads",
    )(blocks, taken_from, arrived, kv, own_stats, other_stats, enc_t)

    back, *near_weights = lax.optimization_barrier((back, *near_weights))
    near_rows = [r if a == 0 else shifted(r, a) for a, r in zip(NEAR, near_rows)]
    returned = lax.all_to_all(back, "seq", split_axis=0, concat_axis=0, tiled=True)
    own, *far_sums = pl.pallas_call(
        project_kernel,
        out_shape=(
            jax.ShapeDtypeStruct((rows, enc_width), f32),
            *[jax.ShapeDtypeStruct((rows, enc_width), bf16)] * (far - 1),
        ),
        in_specs=[spec(HBM)] * (2 * near),
        out_specs=(spec(VMEM),) * far,
        scratch_shapes=[
            pltpu.VMEM((near, far, rows, 2 * head_dim), bf16),
            pltpu.VMEM((near, enc_width, 2 * head_dim), bf16),
            pltpu.SemaphoreType.DMA((2 * near,)),
        ],
        compiler_params=params(SMALL_LIMIT),
        cost_estimate=pl.CostEstimate(flops=6 * 10**10, bytes_accessed=2 * 10**6, transcendentals=0),
        name="project",
    )(*near_rows, *near_weights)
    far_sums = [shifted(part, b) for b, part in zip(FAR[1:], far_sums)]
    attended, query_grad, encoding_grad, key_weight_grad, value_weight_grad = pl.pallas_call(
        finish_kernel,
        out_shape=(
            jax.ShapeDtypeStruct((segments, SEGMENT, head_dim), bf16),
            jax.ShapeDtypeStruct((segments, SEGMENT, head_dim), bf16),
            jax.ShapeDtypeStruct((rows, enc_width), f32),
            jax.ShapeDtypeStruct((share, head_dim), f32),
            jax.ShapeDtypeStruct((share, head_dim), f32),
        ),
        in_specs=[spec(SMEM), *[spec(VMEM)] * (1 + far)],
        out_specs=(spec(VMEM),) * 5,
        compiler_params=params(),
        name="finish",
    )(slots, returned, own, *far_sums)
    return (
        attended.reshape(segments * SEGMENT, head_dim),
        query_grad.reshape(segments * SEGMENT, head_dim),
        encoding_grad.reshape(block_count, row_share, enc_width),
        key_weight_grad,
        value_weight_grad,
    )


def solution(mesh):
    in_specs = (
        P("seq", "head"),
        P("seq", None, None),
        P(None, "head"),
        P(None, "head"),
        P(),
        P("seq", "head"),
    )
    out_specs = (
        P("seq", "head"),
        P("seq", "head"),
        P("seq", "head", None),
        P("seq", "head"),
        P("seq", "head"),
    )
    return jax.shard_map(
        on_device, mesh=mesh, in_specs=in_specs, out_specs=out_specs, check_vma=False
    )
```

```python
import math

import jax
import jax.numpy as jnp
from jax import lax
from jax.experimental import pallas as pl
from jax.experimental.pallas import tpu as pltpu
from jax.sharding import PartitionSpec as P

SEGMENT = 64
NEIGH = 2
CAP = 2
PLACES = 8
NEAR = (0, -1, 2, 1)
FAR = (0, -4, 8, 4)
VMEM_LIMIT = 40 * 1024 * 1024
LARGE_LIMIT = 60 * 1024 * 1024
SMALL_LIMIT = 16 * 1024 * 1024
VMEM = pltpu.VMEM
SMEM = pltpu.SMEM
HBM = pltpu.HBM


def params(limit=VMEM_LIMIT):
    return pltpu.CompilerParams(vmem_limit_bytes=limit)


def spec(space):
    return pl.BlockSpec(memory_space=space)


def nt_dot(a, b):
    return lax.dot_general(a, b, (((1,), (1,)), ((), ())), preferred_element_type=jnp.float32)


def tn_dot(a, b):
    return lax.dot_general(a, b, (((0,), (0,)), ((), ())), preferred_element_type=jnp.float32)


def nn_dot(a, b):
    return jnp.dot(a, b, preferred_element_type=jnp.float32)


def pack_kernel(block_count, reads_ref, q_ref, g_ref, out_ref, slots_ref, used, stage, sem):
    seq_count = used.shape[0]
    read_count = slots_ref.shape[0]
    first = lax.axis_index("seq") * (read_count // NEIGH)

    def leave(slot):
        pltpu.make_async_copy(stage.at[slot], out_ref.at[slot], sem).start()

    for h in range(seq_count):
        used[h] = 0
    for j in range(read_count):
        holder = lax.div(reads_ref[j % NEIGH, first + j // NEIGH], block_count)
        rank = used[holder]
        used[holder] = rank + 1
        slot = holder * CAP + rank
        slots_ref[j] = slot
        stage[slot, 0] = q_ref[j // NEIGH]
        stage[slot, 1] = g_ref[j // NEIGH]
        leave(slot)

    def blank(h, _):
        for k in range(CAP):
            @pl.when(used[h] <= k)
            def _():
                stage[h * CAP + k] = jnp.zeros(stage.shape[1:], stage.dtype)
                leave(h * CAP + k)

        return 0

    lax.fori_loop(0, seq_count, blank, 0)
    pltpu.make_async_copy(stage, out_ref, sem).wait()


def pair_operands(x_ref, s, kv_a, kv_b):
    head_dim = x_ref.shape[3]

    def diagonal(i):
        one, two = x_ref[CAP * s, i], x_ref[CAP * s + 1, i]
        zero = jnp.zeros_like(one)
        return jnp.concatenate(
            [jnp.concatenate([one, zero], axis=1), jnp.concatenate([zero, two], axis=1)], axis=0
        )

    keys = jnp.concatenate([kv_a[:, :head_dim], kv_b[:, :head_dim]], axis=1)
    values = jnp.concatenate([kv_a[:, head_dim:], kv_b[:, head_dim:]], axis=1)
    return diagonal(0), diagonal(1), keys, values


def stats_kernel(scale, blocks_ref, to_ref, x_ref, kv_ref, pair_ref, slot_ref, send_ref, places):
    places[...] = jnp.zeros_like(places)
    left = lax.broadcasted_iota(jnp.int32, (1, CAP * SEGMENT), 1) < SEGMENT
    for s in range(x_ref.shape[0] // CAP):
        kv_a = kv_ref[blocks_ref[CAP * s]]
        kv_b = kv_ref[blocks_ref[CAP * s + 1]]
        q_diag, g_diag, keys, values = pair_operands(x_ref, s, kv_a, kv_b)
        scores = nt_dot(keys, q_diag) * scale
        top = jnp.max(scores, axis=0, keepdims=True)
        weight = jnp.exp(scores - top)
        total = jnp.sum(weight, axis=0, keepdims=True)
        prob_grad = nt_dot(values, g_diag)
        mean = jnp.sum(weight * prob_grad, axis=0, keepdims=True) / total
        lse = top + jnp.log(total)
        pair_ref[s] = jnp.concatenate([lse, mean], axis=0)
        row_a = jnp.where(left, lse, pltpu.roll(mean, SEGMENT, 1))
        row_b = jnp.where(left, pltpu.roll(lse, SEGMENT, 1), mean)
        slot_ref[CAP * s:CAP * s + 1, :] = row_a
        slot_ref[CAP * s + 1:CAP * s + 2, :] = row_b
        places[pl.ds(to_ref[CAP * s], 1), :] = row_a
        places[pl.ds(to_ref[CAP * s + 1], 1), :] = row_b
    send_ref[...] = places[:send_ref.shape[0]]


def swap_kernel(slots_ref, in_ref, out_ref):
    out_ref[...] = jnp.zeros_like(out_ref)
    for c in range(slots_ref.shape[0] // NEIGH):
        slot_a, slot_b = slots_ref[NEIGH * c], slots_ref[NEIGH * c + 1]
        out_ref[pl.ds(slot_a, 1), :] = in_ref[pl.ds(slot_b, 1), :]
        out_ref[pl.ds(slot_b, 1), :] = in_ref[pl.ds(slot_a, 1), :]


def merge_stats(own, row_a, row_b, left):
    other_lse = jnp.where(left, row_a, pltpu.roll(row_b, SEGMENT, 1))
    other_mean = jnp.where(left, pltpu.roll(row_a, SEGMENT, 1), row_b)
    lse, mean = own[0:1], own[1:2]
    top = jnp.maximum(lse, other_lse)
    merged = top + jnp.log(jnp.exp(lse - top) + jnp.exp(other_lse - top))
    delta = jnp.exp(lse - merged) * mean + jnp.exp(other_lse - merged) * other_mean
    return merged, delta


def grads_kernel(scale, group, blocks_ref, from_ref, x_hbm, kv_ref, own_ref, other_ref, enc_hbm, *refs):
    near = len(NEAR)
    out_ref = refs[0]
    rows_refs = refs[1:1 + near]
    x_ref, stage, enc_t, rows_all, rows_near, acc_k, acc_v, x_sems, enc_sem, rows_sems, out_sem = refs[1 + near:]
    head_dim = kv_ref.shape[2] // 2
    seq_count = x_ref.shape[0] // CAP
    pair = CAP * SEGMENT
    parts = 2 * pair

    def arrival(i):
        at = pl.ds(i * group * CAP, group * CAP)
        return pltpu.make_async_copy(x_hbm.at[at], x_ref.at[at], x_sems.at[i])

    for i in range(seq_count // group):
        arrival(i).start()
    fetch = pltpu.make_async_copy(enc_hbm, enc_t, enc_sem)
    fetch.start()
    acc_k[...] = jnp.zeros_like(acc_k)
    acc_v[...] = jnp.zeros_like(acc_v)
    left = lax.broadcasted_iota(jnp.int32, (1, pair), 1) < SEGMENT

    def step(i, _):
        arrival(i).wait()
        sources = [i * group + g for g in range(group)]
        first = [blocks_ref[CAP * s] for s in sources]
        second = [blocks_ref[CAP * s + 1] for s in sources]
        operands = [
            pair_operands(x_ref, s, kv_ref[a], kv_ref[b]) for s, a, b in zip(sources, first, second)
        ]
        stats = [
            merge_stats(
                own_ref[s],
                other_ref[pl.ds(from_ref[CAP * s], 1), :],
                other_ref[pl.ds(from_ref[CAP * s + 1], 1), :],
                left,
            )
            for s in sources
        ]
        scores = [nt_dot(keys, q) * scale for q, _, keys, _ in operands]
        prob_grads = [nt_dot(values, g) for _, g, _, values in operands]
        probs = [jnp.exp(x - stat[0]) for x, stat in zip(scores, stats)]
        score_grads = [
            (p * (x - stat[1]) * scale).astype(jnp.bfloat16)
            for p, x, stat in zip(probs, prob_grads, stats)
        ]
        probs = [p.astype(jnp.bfloat16) for p in probs]
        attended = [tn_dot(p, ops[3]).astype(jnp.bfloat16) for p, ops in zip(probs, operands)]
        query_grads = [tn_dot(x, ops[2]).astype(jnp.bfloat16) for x, ops in zip(score_grads, operands)]
        value_parts = [nn_dot(p, ops[1]) for p, ops in zip(probs, operands)]
        key_parts = [nn_dot(x, ops[0]) for x, ops in zip(score_grads, operands)]
        for s, att, grad in zip(sources, attended, query_grads):
            stage[s, :SEGMENT] = att[:SEGMENT, :head_dim]
            stage[s, SEGMENT:pair] = grad[:SEGMENT, :head_dim]
            stage[s, pair:pair + SEGMENT] = att[SEGMENT:, head_dim:]
            stage[s, pair + SEGMENT:parts] = grad[SEGMENT:, head_dim:]
        for a, b, key_part, value_part in zip(first, second, key_parts, value_parts):
            acc_k[a] += key_part[:, :head_dim]
            acc_v[a] += value_part[:, :head_dim]
            acc_k[b] += key_part[:, head_dim:]
            acc_v[b] += value_part[:, head_dim:]
        at = pl.ds(i * group, group)
        pltpu.make_async_copy(stage.at[at, :parts], out_ref.at[at, :parts], out_sem).start()
        return 0

    lax.fori_loop(0, seq_count // group, step, 0)
    head_count = near * len(FAR)
    block_count, block_len, _ = acc_k.shape
    row_share = block_len // head_count
    z = lax.axis_index("head")
    rows_copies = []
    for i, a in enumerate(NEAR):
        for j, b in enumerate(FAR):
            dest = lax.rem(z + (a + b + head_count), head_count)
            at = pl.ds(pl.multiple_of(dest * row_share, row_share), row_share)
            rows = jnp.concatenate([acc_k[:, at, :], acc_v[:, at, :]], axis=2)
            rows_near[i, j] = rows.reshape(block_count * row_share, 2 * head_dim).astype(jnp.bfloat16)
        rows_copies.append(pltpu.make_async_copy(rows_near.at[i], rows_refs[i], rows_sems.at[i]))
        rows_copies[i].start()
    rows_all[:, :head_dim] = acc_k[...].reshape(-1, head_dim).astype(jnp.bfloat16)
    rows_all[:, head_dim:] = acc_v[...].reshape(-1, head_dim).astype(jnp.bfloat16)
    room = (stage.shape[1] - parts) // 2
    share = enc_t.shape[0] // seq_count
    fetch.wait()
    batch = 8
    for i in range(0, seq_count, batch):
        term = nn_dot(enc_t[i * share:(i + batch) * share], rows_all[...])
        for s in range(batch):
            part = term[s * share:(s + 1) * share]
            if room > share:
                part = jnp.concatenate([part, jnp.zeros((room - share, 2 * head_dim), jnp.float32)], axis=0)
            part = part.astype(jnp.bfloat16)
            stage[i + s, parts:parts + room] = part[:, :head_dim]
            stage[i + s, parts + room:] = part[:, head_dim:]
        pltpu.make_async_copy(
            stage.at[i:i + batch, parts:], out_ref.at[i:i + batch, parts:], out_sem
        ).start()
    for copy in rows_copies:
        copy.wait()
    pltpu.make_async_copy(stage, out_ref, out_sem).wait()


def finish_kernel(slots_ref, in_ref, own_ref, one_ref, two_ref, three_ref, att_ref, qg_ref, enc_ref, kw_ref, vw_ref):
    share = kw_ref.shape[0]
    parts = 2 * CAP * SEGMENT
    room = (in_ref.shape[1] - parts) // 2

    def step(c, _):
        slot_a, slot_b = slots_ref[NEIGH * c], slots_ref[NEIGH * c + 1]

        def part(slot):
            holder = lax.div(slot, CAP)
            row = pl.multiple_of((slot - holder * CAP) * 2 * SEGMENT, 2 * SEGMENT)
            return in_ref[holder, pl.ds(row, 2 * SEGMENT), :].astype(jnp.float32)

        total = (part(slot_a) + part(slot_b)).astype(jnp.bfloat16)
        att_ref[c] = total[:SEGMENT]
        qg_ref[c] = total[SEGMENT:]
        return 0

    lax.fori_loop(0, att_ref.shape[0], step, 0, unroll=4)
    total = in_ref[0, parts:, :].astype(jnp.float32)
    for s in range(1, in_ref.shape[0]):
        total = total + in_ref[s, parts:, :].astype(jnp.float32)
    kw_ref[...] = total[:share]
    vw_ref[...] = total[room:room + share]
    total = own_ref[...] + one_ref[...].astype(jnp.float32)
    enc_ref[...] = total + two_ref[...].astype(jnp.float32) + three_ref[...].astype(jnp.float32)


def project_kernel(*refs):
    near = len(NEAR)
    rows_hbm, weights_hbm, own_ref, far_refs = refs[:near], refs[near:2 * near], refs[2 * near], refs[2 * near + 1:-3]
    rows_ref, weights_ref, sems = refs[-3:]
    _, far, rows, width = rows_ref.shape
    copies = []
    for n in range(near):
        copies.append(pltpu.make_async_copy(weights_hbm[n], weights_ref.at[n], sems.at[n]))
        copies.append(pltpu.make_async_copy(rows_hbm[n], rows_ref.at[n], sems.at[near + n]))
    for copy in copies:
        copy.start()
    for copy in copies:
        copy.wait()
    half = far // 2
    for i in range(0, far, half):
        total = jnp.zeros((half * rows, own_ref.shape[1]), jnp.float32)
        for n in range(near):
            total = total + nt_dot(rows_ref[n, i:i + half].reshape(half * rows, width), weights_ref[n])
        for j in range(half):
            part = total[j * rows:(j + 1) * rows]
            if i + j == 0:
                own_ref[...] = part
            else:
                far_refs[i + j - 1][...] = part.astype(jnp.bfloat16)


def shifted(x, step):
    count = lax.axis_size("head")
    return lax.ppermute(x, "head", [(z, (z + step) % count) for z in range(count)])


def on_device(queries, encodings, key_weight, value_weight, reads, out_grad):
    seq_count = lax.axis_size("seq")
    head_count = lax.axis_size("head")
    me = lax.axis_index("seq")
    block_count, block_len, enc_width = encodings.shape
    head_dim = key_weight.shape[1]
    segments = queries.shape[0] // SEGMENT
    read_count = NEIGH * segments
    slot_count = seq_count * CAP
    scale = 1.0 / math.sqrt(head_dim)
    bf16, f32 = jnp.bfloat16, jnp.float32

    packed, slots = pl.pallas_call(
        lambda *refs: pack_kernel(block_count, *refs),
        out_shape=(
            jax.ShapeDtypeStruct((slot_count, 2, SEGMENT, head_dim), bf16),
            jax.ShapeDtypeStruct((read_count,), jnp.int32),
        ),
        in_specs=[spec(SMEM), spec(VMEM), spec(VMEM)],
        out_specs=(spec(HBM), spec(SMEM)),
        scratch_shapes=[
            pltpu.SMEM((seq_count,), jnp.int32),
            pltpu.VMEM((slot_count, 2, SEGMENT, head_dim), bf16),
            pltpu.SemaphoreType.DMA,
        ],
        compiler_params=params(LARGE_LIMIT),
        name="pack",
    )(
        reads.T,
        queries.reshape(segments, SEGMENT, head_dim),
        out_grad.reshape(segments, SEGMENT, head_dim),
    )
    arrived = lax.all_to_all(packed, "seq", split_axis=0, concat_axis=0, tiled=True)

    key_weight, value_weight, slots = lax.optimization_barrier((key_weight, value_weight, slots))
    weights = jnp.concatenate([key_weight, value_weight], axis=1)
    flat_enc = encodings.reshape(block_count * block_len, enc_width)
    kv = jnp.dot(flat_enc, weights, preferred_element_type=f32).astype(bf16)
    kv = kv.reshape(block_count, block_len, 2 * head_dim)
    share = enc_width // seq_count
    room = -(-share // 16) * 16
    enc_t = flat_enc.T

    tables = reads.reshape(seq_count, read_count)
    holders = tables // block_count
    partners = holders.reshape(-1, NEIGH)[:, ::-1].reshape(seq_count, read_count)
    mine = holders == me
    rank = jnp.cumsum(mine.astype(jnp.int32), axis=1)
    code = (tables % block_count) + (partners + 1) * block_count
    code = jnp.stack(
        [jnp.sum(jnp.where(mine & (rank == k + 1), code, 0), axis=1) for k in range(CAP)], axis=1
    ).reshape(slot_count)
    blocks = code % block_count
    partner = code // block_count - 1
    taken = partner >= 0
    order = jnp.arange(slot_count)
    same = (partner[:, None] == partner[None, :]) & (order[None, :] < order[:, None])
    place = jnp.sum(same.astype(jnp.int32), axis=1)
    twin = place.reshape(-1, CAP)[:, ::-1].reshape(slot_count)
    send_to = jnp.where(taken, partner * PLACES + jnp.minimum(place, PLACES - 1), seq_count * PLACES)
    taken_from = jnp.minimum(jnp.where(partner == me, twin, place), PLACES - 1)
    taken_from = jnp.where(taken, partner * PLACES + taken_from, 0)
    pairs = jax.nn.one_hot(holders.reshape(-1, NEIGH), seq_count, dtype=bf16)
    shared = lax.dot_general(
        pairs[:, 0], pairs[:, 1], (((0,), (0,)), ((), ())), preferred_element_type=f32
    )
    fits = jnp.max(shared + shared.T) <= PLACES
    taken_from = jnp.where(fits, taken_from, order)
    kv, enc_t, blocks, send_to, taken_from, fits, weights = lax.optimization_barrier(
        (kv, enc_t, blocks, send_to, taken_from, fits, weights)
    )
    near_weights = [weights if a == 0 else shifted(weights, a) for a in NEAR]

    place_count = seq_count * PLACES
    own_stats, slot_stats, sent = pl.pallas_call(
        lambda *refs: stats_kernel(scale, *refs),
        out_shape=(
            jax.ShapeDtypeStruct((seq_count, 2, CAP * SEGMENT), f32),
            jax.ShapeDtypeStruct((slot_count, CAP * SEGMENT), f32),
            jax.ShapeDtypeStruct((place_count, CAP * SEGMENT), f32),
        ),
        in_specs=[spec(SMEM), spec(SMEM), spec(VMEM), spec(VMEM)],
        out_specs=(spec(VMEM),) * 3,
        scratch_shapes=[pltpu.VMEM((place_count + 8, CAP * SEGMENT), f32)],
        compiler_params=params(),
        name="stats",
    )(blocks, send_to, arrived, kv)

    def one_hop(sent, slot_stats, slots):
        return lax.all_to_all(sent, "seq", split_axis=0, concat_axis=0, tiled=True)

    def two_hops(sent, slot_stats, slots):
        at_reader = lax.all_to_all(slot_stats, "seq", split_axis=0, concat_axis=0, tiled=True)
        swapped = pl.pallas_call(
            swap_kernel,
            out_shape=jax.ShapeDtypeStruct(slot_stats.shape, f32),
            in_specs=[spec(SMEM), spec(VMEM)],
            out_specs=spec(VMEM),
            compiler_params=params(),
            name="swap",
        )(slots, at_reader)
        swapped = lax.all_to_all(swapped, "seq", split_axis=0, concat_axis=0, tiled=True)
        return jnp.pad(swapped, ((0, place_count - slot_count), (0, 0)))

    other_stats = lax.cond(fits, one_hop, two_hops, sent, slot_stats, slots)

    row_share = block_len // head_count
    rows = block_count * row_share
    near, far = len(NEAR), len(FAR)
    back_shape = (seq_count, 2 * CAP * SEGMENT + 2 * room, head_dim)
    group = 16
    back, *near_rows = pl.pallas_call(
        lambda *refs: grads_kernel(scale, group, *refs),
        out_shape=(
            jax.ShapeDtypeStruct(back_shape, bf16),
            *[jax.ShapeDtypeStruct((far, rows, 2 * head_dim), bf16)] * near,
        ),
        in_specs=[spec(SMEM), spec(SMEM), spec(HBM), spec(VMEM), spec(VMEM), spec(VMEM), spec(HBM)],
        out_specs=(spec(HBM), *[spec(HBM)] * near),
        scratch_shapes=[
            pltpu.VMEM(arrived.shape, bf16),
            pltpu.VMEM(back_shape, bf16),
            pltpu.VMEM((enc_width, block_count * block_len), bf16),
            pltpu.VMEM((block_count * block_len, 2 * head_dim), bf16),
            pltpu.VMEM((near, far, rows, 2 * head_dim), bf16),
            pltpu.VMEM((block_count, block_len, head_dim), f32),
            pltpu.VMEM((block_count, block_len, head_dim), f32),
            pltpu.SemaphoreType.DMA((seq_count // group,)),
            pltpu.SemaphoreType.DMA,
            pltpu.SemaphoreType.DMA((near,)),
            pltpu.SemaphoreType.DMA,
        ],
        compiler_params=params(LARGE_LIMIT),
        name="grads",
    )(blocks, taken_from, arrived, kv, own_stats, other_stats, enc_t)

    back, *near_weights = lax.optimization_barrier((back, *near_weights))
    near_rows = [r if a == 0 else shifted(r, a) for a, r in zip(NEAR, near_rows)]
    returned = lax.all_to_all(back, "seq", split_axis=0, concat_axis=0, tiled=True)
    own, *far_sums = pl.pallas_call(
        project_kernel,
        out_shape=(
            jax.ShapeDtypeStruct((rows, enc_width), f32),
            *[jax.ShapeDtypeStruct((rows, enc_width), bf16)] * (far - 1),
        ),
        in_specs=[spec(HBM)] * (2 * near),
        out_specs=(spec(VMEM),) * far,
        scratch_shapes=[
            pltpu.VMEM((near, far, rows, 2 * head_dim), bf16),
            pltpu.VMEM((near, enc_width, 2 * head_dim), bf16),
            pltpu.SemaphoreType.DMA((2 * near,)),
        ],
        compiler_params=params(SMALL_LIMIT),
        cost_estimate=pl.CostEstimate(flops=6 * 10**10, bytes_accessed=2 * 10**6, transcendentals=0),
        name="project",
    )(*near_rows, *near_weights)
    far_sums = [shifted(part, b) for b, part in zip(FAR[1:], far_sums)]
    attended, query_grad, encoding_grad, key_weight_grad, value_weight_grad = pl.pallas_call(
        finish_kernel,
        out_shape=(
            jax.ShapeDtypeStruct((segments, SEGMENT, head_dim), bf16),
            jax.ShapeDtypeStruct((segments, SEGMENT, head_dim), bf16),
            jax.ShapeDtypeStruct((rows, enc_width), f32),
            jax.ShapeDtypeStruct((share, head_dim), f32),
            jax.ShapeDtypeStruct((share, head_dim), f32),
        ),
        in_specs=[spec(SMEM), *[spec(VMEM)] * (1 + far)],
        out_specs=(spec(VMEM),) * 5,
        compiler_params=params(),
        name="finish",
    )(slots, returned, own, *far_sums)
    return (
        attended.reshape(segments * SEGMENT, head_dim),
        query_grad.reshape(segments * SEGMENT, head_dim),
        encoding_grad.reshape(block_count, row_share, enc_width),
        key_weight_grad,
        value_weight_grad,
    )


def solution(mesh):
    in_specs = (
        P("seq", "head"),
        P("seq", None, None),
        P(None, "head"),
        P(None, "head"),
        P(),
        P("seq", "head"),
    )
    out_specs = (
        P("seq", "head"),
        P("seq", "head"),
        P("seq", "head", None),
        P("seq", "head"),
        P("seq", "head"),
    )
    return jax.shard_map(
        on_device, mesh=mesh, in_specs=in_specs, out_specs=out_specs, check_vma=False
    )
```

```python
import math

import jax
import jax.numpy as jnp
from jax import lax
from jax.experimental import pallas as pl
from jax.experimental.pallas import tpu as pltpu
from jax.sharding import PartitionSpec as P

SEGMENT = 64
NEIGH = 2
CAP = 2
PLACES = 8
NEAR = (0, -1, 2, 1)
FAR = (0, 4, 8, -4)
VMEM_LIMIT = 40 * 1024 * 1024
LARGE_LIMIT = 60 * 1024 * 1024
SMALL_LIMIT = 16 * 1024 * 1024
VMEM = pltpu.VMEM
SMEM = pltpu.SMEM
HBM = pltpu.HBM


def params(limit=VMEM_LIMIT):
    return pltpu.CompilerParams(vmem_limit_bytes=limit)


def spec(space):
    return pl.BlockSpec(memory_space=space)


def nt_dot(a, b):
    return lax.dot_general(a, b, (((1,), (1,)), ((), ())), preferred_element_type=jnp.float32)


def tn_dot(a, b):
    return lax.dot_general(a, b, (((0,), (0,)), ((), ())), preferred_element_type=jnp.float32)


def nn_dot(a, b):
    return jnp.dot(a, b, preferred_element_type=jnp.float32)


def pack_kernel(block_count, reads_ref, q_ref, g_ref, out_ref, slots_ref, used, stage, sem):
    seq_count = used.shape[0]
    read_count = slots_ref.shape[0]
    first = lax.axis_index("seq") * (read_count // NEIGH)

    def leave(slot):
        pltpu.make_async_copy(stage.at[slot], out_ref.at[slot], sem).start()

    for h in range(seq_count):
        used[h] = 0
    for j in range(read_count):
        holder = lax.div(reads_ref[j % NEIGH, first + j // NEIGH], block_count)
        rank = used[holder]
        used[holder] = rank + 1
        slot = holder * CAP + rank
        slots_ref[j] = slot
        stage[slot, 0] = q_ref[j // NEIGH]
        stage[slot, 1] = g_ref[j // NEIGH]
        leave(slot)

    def blank(h, _):
        for k in range(CAP):
            @pl.when(used[h] <= k)
            def _():
                stage[h * CAP + k] = jnp.zeros(stage.shape[1:], stage.dtype)
                leave(h * CAP + k)

        return 0

    lax.fori_loop(0, seq_count, blank, 0)
    pltpu.make_async_copy(stage, out_ref, sem).wait()


def pair_operands(x_ref, s, kv_a, kv_b):
    head_dim = x_ref.shape[3]

    def diagonal(i):
        one, two = x_ref[CAP * s, i], x_ref[CAP * s + 1, i]
        zero = jnp.zeros_like(one)
        return jnp.concatenate(
            [jnp.concatenate([one, zero], axis=1), jnp.concatenate([zero, two], axis=1)], axis=0
        )

    keys = jnp.concatenate([kv_a[:, :head_dim], kv_b[:, :head_dim]], axis=1)
    values = jnp.concatenate([kv_a[:, head_dim:], kv_b[:, head_dim:]], axis=1)
    return diagonal(0), diagonal(1), keys, values


def stats_kernel(scale, blocks_ref, to_ref, x_ref, kv_ref, pair_ref, slot_ref, send_ref, places):
    places[...] = jnp.zeros_like(places)
    left = lax.broadcasted_iota(jnp.int32, (1, CAP * SEGMENT), 1) < SEGMENT
    for s in range(x_ref.shape[0] // CAP):
        kv_a = kv_ref[blocks_ref[CAP * s]]
        kv_b = kv_ref[blocks_ref[CAP * s + 1]]
        q_diag, g_diag, keys, values = pair_operands(x_ref, s, kv_a, kv_b)
        scores = nt_dot(keys, q_diag) * scale
        top = jnp.max(scores, axis=0, keepdims=True)
        weight = jnp.exp(scores - top)
        total = jnp.sum(weight, axis=0, keepdims=True)
        prob_grad = nt_dot(values, g_diag)
        mean = jnp.sum(weight * prob_grad, axis=0, keepdims=True) / total
        lse = top + jnp.log(total)
        pair_ref[s] = jnp.concatenate([lse, mean], axis=0)
        row_a = jnp.where(left, lse, pltpu.roll(mean, SEGMENT, 1))
        row_b = jnp.where(left, pltpu.roll(lse, SEGMENT, 1), mean)
        slot_ref[CAP * s:CAP * s + 1, :] = row_a
        slot_ref[CAP * s + 1:CAP * s + 2, :] = row_b
        places[pl.ds(to_ref[CAP * s], 1), :] = row_a
        places[pl.ds(to_ref[CAP * s + 1], 1), :] = row_b
    send_ref[...] = places[:send_ref.shape[0]]


def swap_kernel(slots_ref, in_ref, out_ref):
    out_ref[...] = jnp.zeros_like(out_ref)
    for c in range(slots_ref.shape[0] // NEIGH):
        slot_a, slot_b = slots_ref[NEIGH * c], slots_ref[NEIGH * c + 1]
        out_ref[pl.ds(slot_a, 1), :] = in_ref[pl.ds(slot_b, 1), :]
        out_ref[pl.ds(slot_b, 1), :] = in_ref[pl.ds(slot_a, 1), :]


def merge_stats(own, row_a, row_b, left):
    other_lse = jnp.where(left, row_a, pltpu.roll(row_b, SEGMENT, 1))
    other_mean = jnp.where(left, pltpu.roll(row_a, SEGMENT, 1), row_b)
    lse, mean = own[0:1], own[1:2]
    top = jnp.maximum(lse, other_lse)
    merged = top + jnp.log(jnp.exp(lse - top) + jnp.exp(other_lse - top))
    delta = jnp.exp(lse - merged) * mean + jnp.exp(other_lse - merged) * other_mean
    return merged, delta


def grads_kernel(scale, group, blocks_ref, from_ref, x_hbm, kv_ref, own_ref, other_ref, enc_hbm, *refs):
    near = len(NEAR)
    out_ref = refs[0]
    rows_refs = refs[1:1 + near]
    x_ref, stage, enc_t, rows_all, rows_near, acc_k, acc_v, x_sems, enc_sem, rows_sems, out_sem = refs[1 + near:]
    head_dim = kv_ref.shape[2] // 2
    seq_count = x_ref.shape[0] // CAP
    pair = CAP * SEGMENT
    parts = 2 * pair

    def arrival(i):
        at = pl.ds(i * group * CAP, group * CAP)
        return pltpu.make_async_copy(x_hbm.at[at], x_ref.at[at], x_sems.at[i])

    for i in range(seq_count // group):
        arrival(i).start()
    fetch = pltpu.make_async_copy(enc_hbm, enc_t, enc_sem)
    fetch.start()
    acc_k[...] = jnp.zeros_like(acc_k)
    acc_v[...] = jnp.zeros_like(acc_v)
    left = lax.broadcasted_iota(jnp.int32, (1, pair), 1) < SEGMENT

    def step(i, _):
        arrival(i).wait()
        sources = [i * group + g for g in range(group)]
        first = [blocks_ref[CAP * s] for s in sources]
        second = [blocks_ref[CAP * s + 1] for s in sources]
        operands = [
            pair_operands(x_ref, s, kv_ref[a], kv_ref[b]) for s, a, b in zip(sources, first, second)
        ]
        stats = [
            merge_stats(
                own_ref[s],
                other_ref[pl.ds(from_ref[CAP * s], 1), :],
                other_ref[pl.ds(from_ref[CAP * s + 1], 1), :],
                left,
            )
            for s in sources
        ]
        scores = [nt_dot(keys, q) * scale for q, _, keys, _ in operands]
        prob_grads = [nt_dot(values, g) for _, g, _, values in operands]
        probs = [jnp.exp(x - stat[0]) for x, stat in zip(scores, stats)]
        score_grads = [
            (p * (x - stat[1]) * scale).astype(jnp.bfloat16)
            for p, x, stat in zip(probs, prob_grads, stats)
        ]
        probs = [p.astype(jnp.bfloat16) for p in probs]
        attended = [tn_dot(p, ops[3]).astype(jnp.bfloat16) for p, ops in zip(probs, operands)]
        query_grads = [tn_dot(x, ops[2]).astype(jnp.bfloat16) for x, ops in zip(score_grads, operands)]
        value_parts = [nn_dot(p, ops[1]) for p, ops in zip(probs, operands)]
        key_parts = [nn_dot(x, ops[0]) for x, ops in zip(score_grads, operands)]
        for s, att, grad in zip(sources, attended, query_grads):
            stage[s, :SEGMENT] = att[:SEGMENT, :head_dim]
            stage[s, SEGMENT:pair] = grad[:SEGMENT, :head_dim]
            stage[s, pair:pair + SEGMENT] = att[SEGMENT:, head_dim:]
            stage[s, pair + SEGMENT:parts] = grad[SEGMENT:, head_dim:]
        for a, b, key_part, value_part in zip(first, second, key_parts, value_parts):
            acc_k[a] += key_part[:, :head_dim]
            acc_v[a] += value_part[:, :head_dim]
            acc_k[b] += key_part[:, head_dim:]
            acc_v[b] += value_part[:, head_dim:]
        at = pl.ds(i * group, group)
        pltpu.make_async_copy(stage.at[at, :parts], out_ref.at[at, :parts], out_sem).start()
        return 0

    lax.fori_loop(0, seq_count // group, step, 0)
    head_count = near * len(FAR)
    block_count, block_len, _ = acc_k.shape
    row_share = block_len // head_count
    z = lax.axis_index("head")
    rows_copies = []
    for i, a in enumerate(NEAR):
        for j, b in enumerate(FAR):
            dest = lax.rem(z + (a + b + head_count), head_count)
            at = pl.ds(pl.multiple_of(dest * row_share, row_share), row_share)
            rows = jnp.concatenate([acc_k[:, at, :], acc_v[:, at, :]], axis=2)
            rows_near[i, j] = rows.reshape(block_count * row_share, 2 * head_dim).astype(jnp.bfloat16)
        rows_copies.append(pltpu.make_async_copy(rows_near.at[i], rows_refs[i], rows_sems.at[i]))
        rows_copies[i].start()
    rows_all[:, :head_dim] = acc_k[...].reshape(-1, head_dim).astype(jnp.bfloat16)
    rows_all[:, head_dim:] = acc_v[...].reshape(-1, head_dim).astype(jnp.bfloat16)
    room = (stage.shape[1] - parts) // 2
    share = enc_t.shape[0] // seq_count
    fetch.wait()
    batch = 8
    for i in range(0, seq_count, batch):
        term = nn_dot(enc_t[i * share:(i + batch) * share], rows_all[...])
        for s in range(batch):
            part = term[s * share:(s + 1) * share]
            if room > share:
                part = jnp.concatenate([part, jnp.zeros((room - share, 2 * head_dim), jnp.float32)], axis=0)
            part = part.astype(jnp.bfloat16)
            stage[i + s, parts:parts + room] = part[:, :head_dim]
            stage[i + s, parts + room:] = part[:, head_dim:]
        pltpu.make_async_copy(
            stage.at[i:i + batch, parts:], out_ref.at[i:i + batch, parts:], out_sem
        ).start()
    for copy in rows_copies:
        copy.wait()
    pltpu.make_async_copy(stage, out_ref, out_sem).wait()


def finish_kernel(slots_ref, in_ref, own_ref, one_ref, two_ref, three_ref, att_ref, qg_ref, enc_ref, kw_ref, vw_ref):
    share = kw_ref.shape[0]
    parts = 2 * CAP * SEGMENT
    room = (in_ref.shape[1] - parts) // 2

    def step(c, _):
        slot_a, slot_b = slots_ref[NEIGH * c], slots_ref[NEIGH * c + 1]

        def part(slot):
            holder = lax.div(slot, CAP)
            row = pl.multiple_of((slot - holder * CAP) * 2 * SEGMENT, 2 * SEGMENT)
            return in_ref[holder, pl.ds(row, 2 * SEGMENT), :].astype(jnp.float32)

        total = (part(slot_a) + part(slot_b)).astype(jnp.bfloat16)
        att_ref[c] = total[:SEGMENT]
        qg_ref[c] = total[SEGMENT:]
        return 0

    lax.fori_loop(0, att_ref.shape[0], step, 0, unroll=4)
    total = in_ref[0, parts:, :].astype(jnp.float32)
    for s in range(1, in_ref.shape[0]):
        total = total + in_ref[s, parts:, :].astype(jnp.float32)
    kw_ref[...] = total[:share]
    vw_ref[...] = total[room:room + share]
    total = own_ref[...] + one_ref[...].astype(jnp.float32)
    enc_ref[...] = total + two_ref[...].astype(jnp.float32) + three_ref[...].astype(jnp.float32)


def project_kernel(*refs):
    near = len(NEAR)
    rows_hbm, weights_hbm, own_ref, far_refs = refs[:near], refs[near:2 * near], refs[2 * near], refs[2 * near + 1:-3]
    rows_ref, weights_ref, sems = refs[-3:]
    _, far, rows, width = rows_ref.shape
    copies = []
    for n in range(near):
        copies.append(pltpu.make_async_copy(weights_hbm[n], weights_ref.at[n], sems.at[n]))
        copies.append(pltpu.make_async_copy(rows_hbm[n], rows_ref.at[n], sems.at[near + n]))
    for copy in copies:
        copy.start()
    for copy in copies:
        copy.wait()
    half = far // 2
    for i in range(0, far, half):
        total = jnp.zeros((half * rows, own_ref.shape[1]), jnp.float32)
        for n in range(near):
            total = total + nt_dot(rows_ref[n, i:i + half].reshape(half * rows, width), weights_ref[n])
        for j in range(half):
            part = total[j * rows:(j + 1) * rows]
            if i + j == 0:
                own_ref[...] = part
            else:
                far_refs[i + j - 1][...] = part.astype(jnp.bfloat16)


def shifted(x, step):
    count = lax.axis_size("head")
    return lax.ppermute(x, "head", [(z, (z + step) % count) for z in range(count)])


def on_device(queries, encodings, key_weight, value_weight, reads, out_grad):
    seq_count = lax.axis_size("seq")
    head_count = lax.axis_size("head")
    me = lax.axis_index("seq")
    block_count, block_len, enc_width = encodings.shape
    head_dim = key_weight.shape[1]
    segments = queries.shape[0] // SEGMENT
    read_count = NEIGH * segments
    slot_count = seq_count * CAP
    scale = 1.0 / math.sqrt(head_dim)
    bf16, f32 = jnp.bfloat16, jnp.float32

    packed, slots = pl.pallas_call(
        lambda *refs: pack_kernel(block_count, *refs),
        out_shape=(
            jax.ShapeDtypeStruct((slot_count, 2, SEGMENT, head_dim), bf16),
            jax.ShapeDtypeStruct((read_count,), jnp.int32),
        ),
        in_specs=[spec(SMEM), spec(VMEM), spec(VMEM)],
        out_specs=(spec(HBM), spec(SMEM)),
        scratch_shapes=[
            pltpu.SMEM((seq_count,), jnp.int32),
            pltpu.VMEM((slot_count, 2, SEGMENT, head_dim), bf16),
            pltpu.SemaphoreType.DMA,
        ],
        compiler_params=params(LARGE_LIMIT),
        name="pack",
    )(
        reads.T,
        queries.reshape(segments, SEGMENT, head_dim),
        out_grad.reshape(segments, SEGMENT, head_dim),
    )
    arrived = lax.all_to_all(packed, "seq", split_axis=0, concat_axis=0, tiled=True)

    key_weight, value_weight, slots = lax.optimization_barrier((key_weight, value_weight, slots))
    weights = jnp.concatenate([key_weight, value_weight], axis=1)
    flat_enc = encodings.reshape(block_count * block_len, enc_width)
    kv = jnp.dot(flat_enc, weights, preferred_element_type=f32).astype(bf16)
    kv = kv.reshape(block_count, block_len, 2 * head_dim)
    share = enc_width // seq_count
    room = -(-share // 16) * 16
    enc_t = flat_enc.T

    tables = reads.reshape(seq_count, read_count)
    holders = tables // block_count
    partners = holders.reshape(-1, NEIGH)[:, ::-1].reshape(seq_count, read_count)
    mine = holders == me
    rank = jnp.cumsum(mine.astype(jnp.int32), axis=1)
    code = (tables % block_count) + (partners + 1) * block_count
    code = jnp.stack(
        [jnp.sum(jnp.where(mine & (rank == k + 1), code, 0), axis=1) for k in range(CAP)], axis=1
    ).reshape(slot_count)
    blocks = code % block_count
    partner = code // block_count - 1
    taken = partner >= 0
    order = jnp.arange(slot_count)
    same = (partner[:, None] == partner[None, :]) & (order[None, :] < order[:, None])
    place = jnp.sum(same.astype(jnp.int32), axis=1)
    twin = place.reshape(-1, CAP)[:, ::-1].reshape(slot_count)
    send_to = jnp.where(taken, partner * PLACES + jnp.minimum(place, PLACES - 1), seq_count * PLACES)
    taken_from = jnp.minimum(jnp.where(partner == me, twin, place), PLACES - 1)
    taken_from = jnp.where(taken, partner * PLACES + taken_from, 0)
    pairs = jax.nn.one_hot(holders.reshape(-1, NEIGH), seq_count, dtype=bf16)
    shared = lax.dot_general(
        pairs[:, 0], pairs[:, 1], (((0,), (0,)), ((), ())), preferred_element_type=f32
    )
    fits = jnp.max(shared + shared.T) <= PLACES
    taken_from = jnp.where(fits, taken_from, order)
    kv, enc_t, blocks, send_to, taken_from, fits, weights = lax.optimization_barrier(
        (kv, enc_t, blocks, send_to, taken_from, fits, weights)
    )
    near_weights = [weights if a == 0 else shifted(weights, a) for a in NEAR]

    place_count = seq_count * PLACES
    own_stats, slot_stats, sent = pl.pallas_call(
        lambda *refs: stats_kernel(scale, *refs),
        out_shape=(
            jax.ShapeDtypeStruct((seq_count, 2, CAP * SEGMENT), f32),
            jax.ShapeDtypeStruct((slot_count, CAP * SEGMENT), f32),
            jax.ShapeDtypeStruct((place_count, CAP * SEGMENT), f32),
        ),
        in_specs=[spec(SMEM), spec(SMEM), spec(VMEM), spec(VMEM)],
        out_specs=(spec(VMEM),) * 3,
        scratch_shapes=[pltpu.VMEM((place_count + 8, CAP * SEGMENT), f32)],
        compiler_params=params(),
        name="stats",
    )(blocks, send_to, arrived, kv)

    def one_hop(sent, slot_stats, slots):
        return lax.all_to_all(sent, "seq", split_axis=0, concat_axis=0, tiled=True)

    def two_hops(sent, slot_stats, slots):
        at_reader = lax.all_to_all(slot_stats, "seq", split_axis=0, concat_axis=0, tiled=True)
        swapped = pl.pallas_call(
            swap_kernel,
            out_shape=jax.ShapeDtypeStruct(slot_stats.shape, f32),
            in_specs=[spec(SMEM), spec(VMEM)],
            out_specs=spec(VMEM),
            compiler_params=params(),
            name="swap",
        )(slots, at_reader)
        swapped = lax.all_to_all(swapped, "seq", split_axis=0, concat_axis=0, tiled=True)
        return jnp.pad(swapped, ((0, place_count - slot_count), (0, 0)))

    other_stats = lax.cond(fits, one_hop, two_hops, sent, slot_stats, slots)

    row_share = block_len // head_count
    rows = block_count * row_share
    near, far = len(NEAR), len(FAR)
    back_shape = (seq_count, 2 * CAP * SEGMENT + 2 * room, head_dim)
    group = 16
    back, *near_rows = pl.pallas_call(
        lambda *refs: grads_kernel(scale, group, *refs),
        out_shape=(
            jax.ShapeDtypeStruct(back_shape, bf16),
            *[jax.ShapeDtypeStruct((far, rows, 2 * head_dim), bf16)] * near,
        ),
        in_specs=[spec(SMEM), spec(SMEM), spec(HBM), spec(VMEM), spec(VMEM), spec(VMEM), spec(HBM)],
        out_specs=(spec(HBM), *[spec(HBM)] * near),
        scratch_shapes=[
            pltpu.VMEM(arrived.shape, bf16),
            pltpu.VMEM(back_shape, bf16),
            pltpu.VMEM((enc_width, block_count * block_len), bf16),
            pltpu.VMEM((block_count * block_len, 2 * head_dim), bf16),
            pltpu.VMEM((near, far, rows, 2 * head_dim), bf16),
            pltpu.VMEM((block_count, block_len, head_dim), f32),
            pltpu.VMEM((block_count, block_len, head_dim), f32),
            pltpu.SemaphoreType.DMA((seq_count // group,)),
            pltpu.SemaphoreType.DMA,
            pltpu.SemaphoreType.DMA((near,)),
            pltpu.SemaphoreType.DMA,
        ],
        compiler_params=params(LARGE_LIMIT),
        name="grads",
    )(blocks, taken_from, arrived, kv, own_stats, other_stats, enc_t)

    back, *near_weights = lax.optimization_barrier((back, *near_weights))
    near_rows = [r if a == 0 else shifted(r, a) for a, r in zip(NEAR, near_rows)]
    returned = lax.all_to_all(back, "seq", split_axis=0, concat_axis=0, tiled=True)
    own, *far_sums = pl.pallas_call(
        project_kernel,
        out_shape=(
            jax.ShapeDtypeStruct((rows, enc_width), f32),
            *[jax.ShapeDtypeStruct((rows, enc_width), bf16)] * (far - 1),
        ),
        in_specs=[spec(HBM)] * (2 * near),
        out_specs=(spec(VMEM),) * far,
        scratch_shapes=[
            pltpu.VMEM((near, far, rows, 2 * head_dim), bf16),
            pltpu.VMEM((near, enc_width, 2 * head_dim), bf16),
            pltpu.SemaphoreType.DMA((2 * near,)),
        ],
        compiler_params=params(SMALL_LIMIT),
        cost_estimate=pl.CostEstimate(flops=6 * 10**10, bytes_accessed=2 * 10**6, transcendentals=0),
        name="project",
    )(*near_rows, *near_weights)
    far_sums = [shifted(part, b) for b, part in zip(FAR[1:], far_sums)]
    attended, query_grad, encoding_grad, key_weight_grad, value_weight_grad = pl.pallas_call(
        finish_kernel,
        out_shape=(
            jax.ShapeDtypeStruct((segments, SEGMENT, head_dim), bf16),
            jax.ShapeDtypeStruct((segments, SEGMENT, head_dim), bf16),
            jax.ShapeDtypeStruct((rows, enc_width), f32),
            jax.ShapeDtypeStruct((share, head_dim), f32),
            jax.ShapeDtypeStruct((share, head_dim), f32),
        ),
        in_specs=[spec(SMEM), *[spec(VMEM)] * (1 + far)],
        out_specs=(spec(VMEM),) * 5,
        compiler_params=params(),
        name="finish",
    )(slots, returned, own, *far_sums)
    return (
        attended.reshape(segments * SEGMENT, head_dim),
        query_grad.reshape(segments * SEGMENT, head_dim),
        encoding_grad.reshape(block_count, row_share, enc_width),
        key_weight_grad,
        value_weight_grad,
    )


def solution(mesh):
    in_specs = (
        P("seq", "head"),
        P("seq", None, None),
        P(None, "head"),
        P(None, "head"),
        P(),
        P("seq", "head"),
    )
    out_specs = (
        P("seq", "head"),
        P("seq", "head"),
        P("seq", "head", None),
        P("seq", "head"),
        P("seq", "head"),
    )
    return jax.shard_map(
        on_device, mesh=mesh, in_specs=in_specs, out_specs=out_specs, check_vma=False
    )
```

```python
import math

import jax
import jax.numpy as jnp
from jax import lax
from jax.experimental import pallas as pl
from jax.experimental.pallas import tpu as pltpu
from jax.sharding import PartitionSpec as P

SEGMENT = 64
NEIGH = 2
CAP = 2
PLACES = 8
NEAR = (0, -1, 2, 1)
FAR = (0, 4, 8, -4)
VMEM_LIMIT = 40 * 1024 * 1024
LARGE_LIMIT = 60 * 1024 * 1024
SMALL_LIMIT = 16 * 1024 * 1024
VMEM = pltpu.VMEM
SMEM = pltpu.SMEM
HBM = pltpu.HBM


def params(limit=VMEM_LIMIT):
    return pltpu.CompilerParams(vmem_limit_bytes=limit)


def spec(space):
    return pl.BlockSpec(memory_space=space)


def nt_dot(a, b):
    return lax.dot_general(a, b, (((1,), (1,)), ((), ())), preferred_element_type=jnp.float32)


def tn_dot(a, b):
    return lax.dot_general(a, b, (((0,), (0,)), ((), ())), preferred_element_type=jnp.float32)


def nn_dot(a, b):
    return jnp.dot(a, b, preferred_element_type=jnp.float32)


def pack_kernel(block_count, reads_ref, q_ref, g_ref, out_ref, slots_ref, used, stage, sem):
    seq_count = used.shape[0]
    read_count = slots_ref.shape[0]
    first = lax.axis_index("seq") * (read_count // NEIGH)

    def leave(slot):
        pltpu.make_async_copy(stage.at[slot], out_ref.at[slot], sem).start()

    for h in range(seq_count):
        used[h] = 0
    for j in range(read_count):
        holder = lax.div(reads_ref[j % NEIGH, first + j // NEIGH], block_count)
        rank = used[holder]
        used[holder] = rank + 1
        slot = holder * CAP + rank
        slots_ref[j] = slot
        stage[slot, 0] = q_ref[j // NEIGH]
        stage[slot, 1] = g_ref[j // NEIGH]
        leave(slot)

    def blank(h, _):
        for k in range(CAP):
            @pl.when(used[h] <= k)
            def _():
                stage[h * CAP + k] = jnp.zeros(stage.shape[1:], stage.dtype)
                leave(h * CAP + k)

        return 0

    lax.fori_loop(0, seq_count, blank, 0)
    pltpu.make_async_copy(stage, out_ref, sem).wait()


def pair_operands(x_ref, s, kv_a, kv_b):
    head_dim = x_ref.shape[3]

    def diagonal(i):
        one, two = x_ref[CAP * s, i], x_ref[CAP * s + 1, i]
        zero = jnp.zeros_like(one)
        return jnp.concatenate(
            [jnp.concatenate([one, zero], axis=1), jnp.concatenate([zero, two], axis=1)], axis=0
        )

    keys = jnp.concatenate([kv_a[:, :head_dim], kv_b[:, :head_dim]], axis=1)
    values = jnp.concatenate([kv_a[:, head_dim:], kv_b[:, head_dim:]], axis=1)
    return diagonal(0), diagonal(1), keys, values


def stats_kernel(scale, blocks_ref, to_ref, x_ref, kv_ref, pair_ref, slot_ref, send_ref, places):
    places[...] = jnp.zeros_like(places)
    left = lax.broadcasted_iota(jnp.int32, (1, CAP * SEGMENT), 1) < SEGMENT
    for s in range(x_ref.shape[0] // CAP):
        kv_a = kv_ref[blocks_ref[CAP * s]]
        kv_b = kv_ref[blocks_ref[CAP * s + 1]]
        q_diag, g_diag, keys, values = pair_operands(x_ref, s, kv_a, kv_b)
        scores = nt_dot(keys, q_diag) * scale
        top = jnp.max(scores, axis=0, keepdims=True)
        weight = jnp.exp(scores - top)
        total = jnp.sum(weight, axis=0, keepdims=True)
        prob_grad = nt_dot(values, g_diag)
        mean = jnp.sum(weight * prob_grad, axis=0, keepdims=True) / total
        lse = top + jnp.log(total)
        pair_ref[s] = jnp.concatenate([lse, mean], axis=0)
        row_a = jnp.where(left, lse, pltpu.roll(mean, SEGMENT, 1))
        row_b = jnp.where(left, pltpu.roll(lse, SEGMENT, 1), mean)
        slot_ref[CAP * s:CAP * s + 1, :] = row_a
        slot_ref[CAP * s + 1:CAP * s + 2, :] = row_b
        places[pl.ds(to_ref[CAP * s], 1), :] = row_a
        places[pl.ds(to_ref[CAP * s + 1], 1), :] = row_b
    send_ref[...] = places[:send_ref.shape[0]]


def swap_kernel(slots_ref, in_ref, out_ref):
    out_ref[...] = jnp.zeros_like(out_ref)
    for c in range(slots_ref.shape[0] // NEIGH):
        slot_a, slot_b = slots_ref[NEIGH * c], slots_ref[NEIGH * c + 1]
        out_ref[pl.ds(slot_a, 1), :] = in_ref[pl.ds(slot_b, 1), :]
        out_ref[pl.ds(slot_b, 1), :] = in_ref[pl.ds(slot_a, 1), :]


def merge_stats(own, row_a, row_b, left):
    other_lse = jnp.where(left, row_a, pltpu.roll(row_b, SEGMENT, 1))
    other_mean = jnp.where(left, pltpu.roll(row_a, SEGMENT, 1), row_b)
    lse, mean = own[0:1], own[1:2]
    top = jnp.maximum(lse, other_lse)
    merged = top + jnp.log(jnp.exp(lse - top) + jnp.exp(other_lse - top))
    delta = jnp.exp(lse - merged) * mean + jnp.exp(other_lse - merged) * other_mean
    return merged, delta


def grads_kernel(scale, group, blocks_ref, from_ref, x_hbm, kv_ref, own_ref, other_ref, enc_hbm, *refs):
    near = len(NEAR)
    out_ref = refs[0]
    rows_refs = refs[1:1 + near]
    x_ref, stage, enc_t, rows_all, rows_near, acc_k, acc_v, x_sems, enc_sem, rows_sems, out_sem = refs[1 + near:]
    head_dim = kv_ref.shape[2] // 2
    seq_count = x_ref.shape[0] // CAP
    pair = CAP * SEGMENT
    parts = 2 * pair

    def arrival(i):
        at = pl.ds(i * group * CAP, group * CAP)
        return pltpu.make_async_copy(x_hbm.at[at], x_ref.at[at], x_sems.at[i])

    for i in range(seq_count // group):
        arrival(i).start()
    fetch = pltpu.make_async_copy(enc_hbm, enc_t, enc_sem)
    fetch.start()
    acc_k[...] = jnp.zeros_like(acc_k)
    acc_v[...] = jnp.zeros_like(acc_v)
    left = lax.broadcasted_iota(jnp.int32, (1, pair), 1) < SEGMENT

    def step(i, _):
        arrival(i).wait()
        sources = [i * group + g for g in range(group)]
        first = [blocks_ref[CAP * s] for s in sources]
        second = [blocks_ref[CAP * s + 1] for s in sources]
        operands = [
            pair_operands(x_ref, s, kv_ref[a], kv_ref[b]) for s, a, b in zip(sources, first, second)
        ]
        stats = [
            merge_stats(
                own_ref[s],
                other_ref[pl.ds(from_ref[CAP * s], 1), :],
                other_ref[pl.ds(from_ref[CAP * s + 1], 1), :],
                left,
            )
            for s in sources
        ]
        scores = [nt_dot(keys, q) * scale for q, _, keys, _ in operands]
        prob_grads = [nt_dot(values, g) for _, g, _, values in operands]
        probs = [jnp.exp(x - stat[0]) for x, stat in zip(scores, stats)]
        score_grads = [
            (p * (x - stat[1]) * scale).astype(jnp.bfloat16)
            for p, x, stat in zip(probs, prob_grads, stats)
        ]
        probs = [p.astype(jnp.bfloat16) for p in probs]
        attended = [tn_dot(p, ops[3]).astype(jnp.bfloat16) for p, ops in zip(probs, operands)]
        query_grads = [tn_dot(x, ops[2]).astype(jnp.bfloat16) for x, ops in zip(score_grads, operands)]
        value_parts = [nn_dot(p, ops[1]) for p, ops in zip(probs, operands)]
        key_parts = [nn_dot(x, ops[0]) for x, ops in zip(score_grads, operands)]
        for s, att, grad in zip(sources, attended, query_grads):
            stage[s, :SEGMENT] = att[:SEGMENT, :head_dim]
            stage[s, SEGMENT:pair] = grad[:SEGMENT, :head_dim]
            stage[s, pair:pair + SEGMENT] = att[SEGMENT:, head_dim:]
            stage[s, pair + SEGMENT:parts] = grad[SEGMENT:, head_dim:]
        for a, b, key_part, value_part in zip(first, second, key_parts, value_parts):
            acc_k[a] += key_part[:, :head_dim]
            acc_v[a] += value_part[:, :head_dim]
            acc_k[b] += key_part[:, head_dim:]
            acc_v[b] += value_part[:, head_dim:]
        at = pl.ds(i * group, group)
        pltpu.make_async_copy(stage.at[at, :parts], out_ref.at[at, :parts], out_sem).start()
        return 0

    lax.fori_loop(0, seq_count // group, step, 0)
    head_count = near * len(FAR)
    block_count, block_len, _ = acc_k.shape
    row_share = block_len // head_count
    z = lax.axis_index("head")
    rows_copies = []
    for i, a in enumerate(NEAR):
        for j, b in enumerate(FAR):
            dest = lax.rem(z + (a + b + head_count), head_count)
            at = pl.ds(pl.multiple_of(dest * row_share, row_share), row_share)
            rows = jnp.concatenate([acc_k[:, at, :], acc_v[:, at, :]], axis=2)
            rows_near[i, j] = rows.reshape(block_count * row_share, 2 * head_dim).astype(jnp.bfloat16)
        rows_copies.append(pltpu.make_async_copy(rows_near.at[i], rows_refs[i], rows_sems.at[i]))
        rows_copies[i].start()
    rows_all[:, :head_dim] = acc_k[...].reshape(-1, head_dim).astype(jnp.bfloat16)
    rows_all[:, head_dim:] = acc_v[...].reshape(-1, head_dim).astype(jnp.bfloat16)
    room = (stage.shape[1] - parts) // 2
    share = enc_t.shape[0] // seq_count
    fetch.wait()
    batch = 8
    for i in range(0, seq_count, batch):
        term = nn_dot(enc_t[i * share:(i + batch) * share], rows_all[...])
        for s in range(batch):
            part = term[s * share:(s + 1) * share]
            if room > share:
                part = jnp.concatenate([part, jnp.zeros((room - share, 2 * head_dim), jnp.float32)], axis=0)
            part = part.astype(jnp.bfloat16)
            stage[i + s, parts:parts + room] = part[:, :head_dim]
            stage[i + s, parts + room:] = part[:, head_dim:]
        pltpu.make_async_copy(
            stage.at[i:i + batch, parts:], out_ref.at[i:i + batch, parts:], out_sem
        ).start()
    for copy in rows_copies:
        copy.wait()
    pltpu.make_async_copy(stage, out_ref, out_sem).wait()


def finish_kernel(slots_ref, in_ref, att_ref, qg_ref, kw_ref, vw_ref, token_ref):
    share = kw_ref.shape[0]
    parts = 2 * CAP * SEGMENT
    room = (in_ref.shape[1] - parts) // 2

    def step(c, _):
        slot_a, slot_b = slots_ref[NEIGH * c], slots_ref[NEIGH * c + 1]

        def part(slot):
            holder = lax.div(slot, CAP)
            row = pl.multiple_of((slot - holder * CAP) * 2 * SEGMENT, 2 * SEGMENT)
            return in_ref[holder, pl.ds(row, 2 * SEGMENT), :].astype(jnp.float32)

        total = (part(slot_a) + part(slot_b)).astype(jnp.bfloat16)
        att_ref[c] = total[:SEGMENT]
        qg_ref[c] = total[SEGMENT:]
        return 0

    lax.fori_loop(0, att_ref.shape[0], step, 0, unroll=4)
    total = in_ref[0, parts:, :].astype(jnp.float32)
    for s in range(1, in_ref.shape[0]):
        total = total + in_ref[s, parts:, :].astype(jnp.float32)
    kw_ref[...] = total[:share]
    vw_ref[...] = total[room:room + share]
    token_ref[0] = slots_ref[0]


def total_kernel(token_ref, own_ref, one_ref, two_ref, three_ref, out_ref):
    total = own_ref[...] + one_ref[...].astype(jnp.float32)
    out_ref[...] = total + two_ref[...].astype(jnp.float32) + three_ref[...].astype(jnp.float32)


def project_kernel(*refs):
    near = len(NEAR)
    rows_hbm, weights_hbm, own_ref, far_refs = refs[:near], refs[near:2 * near], refs[2 * near], refs[2 * near + 1:-4]
    rows_ref, weights_ref, acc, sems = refs[-4:]
    _, far, rows, width = rows_ref.shape
    copies = []
    for n in range(near):
        copies.append(pltpu.make_async_copy(weights_hbm[n], weights_ref.at[n], sems.at[n]))
        copies.append(pltpu.make_async_copy(rows_hbm[n], rows_ref.at[n], sems.at[near + n]))
    for copy in copies:
        copy.start()
    half = far // 2
    for n in range(near):
        copies[2 * n].wait()
        copies[2 * n + 1].wait()
        for i in range(0, far, half):
            at = pl.ds(i * rows, half * rows)
            total = nt_dot(rows_ref[n, i:i + half].reshape(half * rows, width), weights_ref[n])
            if n > 0:
                total = total + acc[at]
            if n < near - 1:
                acc[at] = total
                continue
            for j in range(half):
                part = total[j * rows:(j + 1) * rows]
                if i + j == 0:
                    own_ref[...] = part
                else:
                    far_refs[i + j - 1][...] = part.astype(jnp.bfloat16)


def shifted(x, step):
    count = lax.axis_size("head")
    return lax.ppermute(x, "head", [(z, (z + step) % count) for z in range(count)])


def on_device(queries, encodings, key_weight, value_weight, reads, out_grad):
    seq_count = lax.axis_size("seq")
    head_count = lax.axis_size("head")
    me = lax.axis_index("seq")
    block_count, block_len, enc_width = encodings.shape
    head_dim = key_weight.shape[1]
    segments = queries.shape[0] // SEGMENT
    read_count = NEIGH * segments
    slot_count = seq_count * CAP
    scale = 1.0 / math.sqrt(head_dim)
    bf16, f32 = jnp.bfloat16, jnp.float32

    packed, slots = pl.pallas_call(
        lambda *refs: pack_kernel(block_count, *refs),
        out_shape=(
            jax.ShapeDtypeStruct((slot_count, 2, SEGMENT, head_dim), bf16),
            jax.ShapeDtypeStruct((read_count,), jnp.int32),
        ),
        in_specs=[spec(SMEM), spec(VMEM), spec(VMEM)],
        out_specs=(spec(HBM), spec(SMEM)),
        scratch_shapes=[
            pltpu.SMEM((seq_count,), jnp.int32),
            pltpu.VMEM((slot_count, 2, SEGMENT, head_dim), bf16),
            pltpu.SemaphoreType.DMA,
        ],
        compiler_params=params(LARGE_LIMIT),
        name="pack",
    )(
        reads.T,
        queries.reshape(segments, SEGMENT, head_dim),
        out_grad.reshape(segments, SEGMENT, head_dim),
    )
    arrived = lax.all_to_all(packed, "seq", split_axis=0, concat_axis=0, tiled=True)

    key_weight, value_weight, slots = lax.optimization_barrier((key_weight, value_weight, slots))
    weights = jnp.concatenate([key_weight, value_weight], axis=1)
    flat_enc = encodings.reshape(block_count * block_len, enc_width)
    kv = jnp.dot(flat_enc, weights, preferred_element_type=f32).astype(bf16)
    kv = kv.reshape(block_count, block_len, 2 * head_dim)
    share = enc_width // seq_count
    room = -(-share // 16) * 16
    enc_t = flat_enc.T

    tables = reads.reshape(seq_count, read_count)
    holders = tables // block_count
    partners = holders.reshape(-1, NEIGH)[:, ::-1].reshape(seq_count, read_count)
    mine = holders == me
    rank = jnp.cumsum(mine.astype(jnp.int32), axis=1)
    code = (tables % block_count) + (partners + 1) * block_count
    code = jnp.stack(
        [jnp.sum(jnp.where(mine & (rank == k + 1), code, 0), axis=1) for k in range(CAP)], axis=1
    ).reshape(slot_count)
    blocks = code % block_count
    partner = code // block_count - 1
    taken = partner >= 0
    order = jnp.arange(slot_count)
    same = (partner[:, None] == partner[None, :]) & (order[None, :] < order[:, None])
    place = jnp.sum(same.astype(jnp.int32), axis=1)
    twin = place.reshape(-1, CAP)[:, ::-1].reshape(slot_count)
    send_to = jnp.where(taken, partner * PLACES + jnp.minimum(place, PLACES - 1), seq_count * PLACES)
    taken_from = jnp.minimum(jnp.where(partner == me, twin, place), PLACES - 1)
    taken_from = jnp.where(taken, partner * PLACES + taken_from, 0)
    pairs = jax.nn.one_hot(holders.reshape(-1, NEIGH), seq_count, dtype=bf16)
    shared = lax.dot_general(
        pairs[:, 0], pairs[:, 1], (((0,), (0,)), ((), ())), preferred_element_type=f32
    )
    fits = jnp.max(shared + shared.T) <= PLACES
    taken_from = jnp.where(fits, taken_from, order)
    kv, enc_t, blocks, send_to, taken_from, fits, weights = lax.optimization_barrier(
        (kv, enc_t, blocks, send_to, taken_from, fits, weights)
    )
    near_weights = [weights if a == 0 else shifted(weights, a) for a in NEAR]

    place_count = seq_count * PLACES
    own_stats, slot_stats, sent = pl.pallas_call(
        lambda *refs: stats_kernel(scale, *refs),
        out_shape=(
            jax.ShapeDtypeStruct((seq_count, 2, CAP * SEGMENT), f32),
            jax.ShapeDtypeStruct((slot_count, CAP * SEGMENT), f32),
            jax.ShapeDtypeStruct((place_count, CAP * SEGMENT), f32),
        ),
        in_specs=[spec(SMEM), spec(SMEM), spec(VMEM), spec(VMEM)],
        out_specs=(spec(VMEM),) * 3,
        scratch_shapes=[pltpu.VMEM((place_count + 8, CAP * SEGMENT), f32)],
        compiler_params=params(),
        name="stats",
    )(blocks, send_to, arrived, kv)

    def one_hop(sent, slot_stats, slots):
        return lax.all_to_all(sent, "seq", split_axis=0, concat_axis=0, tiled=True)

    def two_hops(sent, slot_stats, slots):
        at_reader = lax.all_to_all(slot_stats, "seq", split_axis=0, concat_axis=0, tiled=True)
        swapped = pl.pallas_call(
            swap_kernel,
            out_shape=jax.ShapeDtypeStruct(slot_stats.shape, f32),
            in_specs=[spec(SMEM), spec(VMEM)],
            out_specs=spec(VMEM),
            compiler_params=params(),
            name="swap",
        )(slots, at_reader)
        swapped = lax.all_to_all(swapped, "seq", split_axis=0, concat_axis=0, tiled=True)
        return jnp.pad(swapped, ((0, place_count - slot_count), (0, 0)))

    other_stats = lax.cond(fits, one_hop, two_hops, sent, slot_stats, slots)

    row_share = block_len // head_count
    rows = block_count * row_share
    near, far = len(NEAR), len(FAR)
    back_shape = (seq_count, 2 * CAP * SEGMENT + 2 * room, head_dim)
    group = 16
    back, *near_rows = pl.pallas_call(
        lambda *refs: grads_kernel(scale, group, *refs),
        out_shape=(
            jax.ShapeDtypeStruct(back_shape, bf16),
            *[jax.ShapeDtypeStruct((far, rows, 2 * head_dim), bf16)] * near,
        ),
        in_specs=[spec(SMEM), spec(SMEM), spec(HBM), spec(VMEM), spec(VMEM), spec(VMEM), spec(HBM)],
        out_specs=(spec(HBM), *[spec(HBM)] * near),
        scratch_shapes=[
            pltpu.VMEM(arrived.shape, bf16),
            pltpu.VMEM(back_shape, bf16),
            pltpu.VMEM((enc_width, block_count * block_len), bf16),
            pltpu.VMEM((block_count * block_len, 2 * head_dim), bf16),
            pltpu.VMEM((near, far, rows, 2 * head_dim), bf16),
            pltpu.VMEM((block_count, block_len, head_dim), f32),
            pltpu.VMEM((block_count, block_len, head_dim), f32),
            pltpu.SemaphoreType.DMA((seq_count // group,)),
            pltpu.SemaphoreType.DMA,
            pltpu.SemaphoreType.DMA((near,)),
            pltpu.SemaphoreType.DMA,
        ],
        compiler_params=params(LARGE_LIMIT),
        name="grads",
    )(blocks, taken_from, arrived, kv, own_stats, other_stats, enc_t)

    back, *near_weights = lax.optimization_barrier((back, *near_weights))
    near_rows = [r if a == 0 else shifted(r, a) for a, r in zip(NEAR, near_rows)]
    returned = lax.all_to_all(back, "seq", split_axis=0, concat_axis=0, tiled=True)
    own, *far_sums = pl.pallas_call(
        project_kernel,
        out_shape=(
            jax.ShapeDtypeStruct((rows, enc_width), f32),
            *[jax.ShapeDtypeStruct((rows, enc_width), bf16)] * (far - 1),
        ),
        in_specs=[spec(HBM)] * (2 * near),
        out_specs=(spec(VMEM),) * far,
        scratch_shapes=[
            pltpu.VMEM((near, far, rows, 2 * head_dim), bf16),
            pltpu.VMEM((near, enc_width, 2 * head_dim), bf16),
            pltpu.VMEM((far * rows, enc_width), f32),
            pltpu.SemaphoreType.DMA((2 * near,)),
        ],
        compiler_params=params(SMALL_LIMIT),
        cost_estimate=pl.CostEstimate(flops=6 * 10**10, bytes_accessed=2 * 10**6, transcendentals=0),
        name="project",
    )(*near_rows, *near_weights)
    far_sums = [shifted(part, b) for b, part in zip(FAR[1:], far_sums)]
    attended, query_grad, key_weight_grad, value_weight_grad, token = pl.pallas_call(
        finish_kernel,
        out_shape=(
            jax.ShapeDtypeStruct((segments, SEGMENT, head_dim), bf16),
            jax.ShapeDtypeStruct((segments, SEGMENT, head_dim), bf16),
            jax.ShapeDtypeStruct((share, head_dim), f32),
            jax.ShapeDtypeStruct((share, head_dim), f32),
            jax.ShapeDtypeStruct((1,), jnp.int32),
        ),
        in_specs=[spec(SMEM), spec(VMEM)],
        out_specs=(*[spec(VMEM)] * 4, spec(SMEM)),
        compiler_params=params(),
        name="finish",
    )(slots, returned)
    encoding_grad = pl.pallas_call(
        total_kernel,
        out_shape=jax.ShapeDtypeStruct((rows, enc_width), f32),
        in_specs=[spec(SMEM), *[spec(VMEM)] * far],
        out_specs=spec(VMEM),
        compiler_params=params(),
        name="total",
    )(token, own, *far_sums)
    return (
        attended.reshape(segments * SEGMENT, head_dim),
        query_grad.reshape(segments * SEGMENT, head_dim),
        encoding_grad.reshape(block_count, row_share, enc_width),
        key_weight_grad,
        value_weight_grad,
    )


def solution(mesh):
    in_specs = (
        P("seq", "head"),
        P("seq", None, None),
        P(None, "head"),
        P(None, "head"),
        P(),
        P("seq", "head"),
    )
    out_specs = (
        P("seq", "head"),
        P("seq", "head"),
        P("seq", "head", None),
        P("seq", "head"),
        P("seq", "head"),
    )
    return jax.shard_map(
        on_device, mesh=mesh, in_specs=in_specs, out_specs=out_specs, check_vma=False
    )
```

```python
import math

import jax
import jax.numpy as jnp
from jax import lax
from jax.experimental import pallas as pl
from jax.experimental.pallas import tpu as pltpu
from jax.sharding import PartitionSpec as P

SEGMENT = 64
NEIGH = 2
CAP = 2
PLACES = 8
NEAR = (0, 1, -1, 2)
FAR = (0, 4, 8, -4)
VMEM_LIMIT = 40 * 1024 * 1024
LARGE_LIMIT = 60 * 1024 * 1024
SMALL_LIMIT = 16 * 1024 * 1024
VMEM = pltpu.VMEM
SMEM = pltpu.SMEM
HBM = pltpu.HBM


def params(limit=VMEM_LIMIT):
    return pltpu.CompilerParams(vmem_limit_bytes=limit)


def spec(space):
    return pl.BlockSpec(memory_space=space)


def nt_dot(a, b):
    return lax.dot_general(a, b, (((1,), (1,)), ((), ())), preferred_element_type=jnp.float32)


def tn_dot(a, b):
    return lax.dot_general(a, b, (((0,), (0,)), ((), ())), preferred_element_type=jnp.float32)


def nn_dot(a, b):
    return jnp.dot(a, b, preferred_element_type=jnp.float32)


def pack_kernel(block_count, reads_ref, q_ref, g_ref, out_ref, slots_ref, used, stage, sem):
    seq_count = used.shape[0]
    read_count = slots_ref.shape[0]
    first = lax.axis_index("seq") * (read_count // NEIGH)

    def leave(slot):
        pltpu.make_async_copy(stage.at[slot], out_ref.at[slot], sem).start()

    for h in range(seq_count):
        used[h] = 0
    for j in range(read_count):
        holder = lax.div(reads_ref[j % NEIGH, first + j // NEIGH], block_count)
        rank = used[holder]
        used[holder] = rank + 1
        slot = holder * CAP + rank
        slots_ref[j] = slot
        stage[slot, 0] = q_ref[j // NEIGH]
        stage[slot, 1] = g_ref[j // NEIGH]
        leave(slot)

    def blank(h, _):
        for k in range(CAP):
            @pl.when(used[h] <= k)
            def _():
                stage[h * CAP + k] = jnp.zeros(stage.shape[1:], stage.dtype)
                leave(h * CAP + k)

        return 0

    lax.fori_loop(0, seq_count, blank, 0)
    pltpu.make_async_copy(stage, out_ref, sem).wait()


def pair_operands(x_ref, s, kv_a, kv_b):
    head_dim = x_ref.shape[3]

    def diagonal(i):
        one, two = x_ref[CAP * s, i], x_ref[CAP * s + 1, i]
        zero = jnp.zeros_like(one)
        return jnp.concatenate(
            [jnp.concatenate([one, zero], axis=1), jnp.concatenate([zero, two], axis=1)], axis=0
        )

    keys = jnp.concatenate([kv_a[:, :head_dim], kv_b[:, :head_dim]], axis=1)
    values = jnp.concatenate([kv_a[:, head_dim:], kv_b[:, head_dim:]], axis=1)
    return diagonal(0), diagonal(1), keys, values


def stats_kernel(scale, blocks_ref, to_ref, x_ref, kv_ref, pair_ref, slot_ref, send_ref, places):
    places[...] = jnp.zeros_like(places)
    left = lax.broadcasted_iota(jnp.int32, (1, CAP * SEGMENT), 1) < SEGMENT
    for s in range(x_ref.shape[0] // CAP):
        kv_a = kv_ref[blocks_ref[CAP * s]]
        kv_b = kv_ref[blocks_ref[CAP * s + 1]]
        q_diag, g_diag, keys, values = pair_operands(x_ref, s, kv_a, kv_b)
        scores = nt_dot(keys, q_diag) * scale
        top = jnp.max(scores, axis=0, keepdims=True)
        weight = jnp.exp(scores - top)
        total = jnp.sum(weight, axis=0, keepdims=True)
        prob_grad = nt_dot(values, g_diag)
        mean = jnp.sum(weight * prob_grad, axis=0, keepdims=True) / total
        lse = top + jnp.log(total)
        pair_ref[s] = jnp.concatenate([lse, mean], axis=0)
        row_a = jnp.where(left, lse, pltpu.roll(mean, SEGMENT, 1))
        row_b = jnp.where(left, pltpu.roll(lse, SEGMENT, 1), mean)
        slot_ref[CAP * s:CAP * s + 1, :] = row_a
        slot_ref[CAP * s + 1:CAP * s + 2, :] = row_b
        places[pl.ds(to_ref[CAP * s], 1), :] = row_a
        places[pl.ds(to_ref[CAP * s + 1], 1), :] = row_b
    send_ref[...] = places[:send_ref.shape[0]]


def swap_kernel(slots_ref, in_ref, out_ref):
    out_ref[...] = jnp.zeros_like(out_ref)
    for c in range(slots_ref.shape[0] // NEIGH):
        slot_a, slot_b = slots_ref[NEIGH * c], slots_ref[NEIGH * c + 1]
        out_ref[pl.ds(slot_a, 1), :] = in_ref[pl.ds(slot_b, 1), :]
        out_ref[pl.ds(slot_b, 1), :] = in_ref[pl.ds(slot_a, 1), :]


def merge_stats(own, row_a, row_b, left):
    other_lse = jnp.where(left, row_a, pltpu.roll(row_b, SEGMENT, 1))
    other_mean = jnp.where(left, pltpu.roll(row_a, SEGMENT, 1), row_b)
    lse, mean = own[0:1], own[1:2]
    top = jnp.maximum(lse, other_lse)
    merged = top + jnp.log(jnp.exp(lse - top) + jnp.exp(other_lse - top))
    delta = jnp.exp(lse - merged) * mean + jnp.exp(other_lse - merged) * other_mean
    return merged, delta


def grads_kernel(scale, group, blocks_ref, from_ref, x_hbm, kv_ref, own_ref, other_ref, enc_hbm, *refs):
    near = len(NEAR)
    out_ref = refs[0]
    rows_refs = refs[1:1 + near]
    x_ref, stage, enc_t, rows_all, rows_near, acc_k, acc_v, x_sems, enc_sem, rows_sems, out_sem = refs[1 + near:]
    head_dim = kv_ref.shape[2] // 2
    seq_count = x_ref.shape[0] // CAP
    pair = CAP * SEGMENT
    parts = 2 * pair

    def arrival(i):
        at = pl.ds(i * group * CAP, group * CAP)
        return pltpu.make_async_copy(x_hbm.at[at], x_ref.at[at], x_sems.at[i])

    for i in range(seq_count // group):
        arrival(i).start()
    fetch = pltpu.make_async_copy(enc_hbm, enc_t, enc_sem)
    fetch.start()
    acc_k[...] = jnp.zeros_like(acc_k)
    acc_v[...] = jnp.zeros_like(acc_v)
    left = lax.broadcasted_iota(jnp.int32, (1, pair), 1) < SEGMENT

    def step(i, _):
        arrival(i).wait()
        sources = [i * group + g for g in range(group)]
        first = [blocks_ref[CAP * s] for s in sources]
        second = [blocks_ref[CAP * s + 1] for s in sources]
        operands = [
            pair_operands(x_ref, s, kv_ref[a], kv_ref[b]) for s, a, b in zip(sources, first, second)
        ]
        stats = [
            merge_stats(
                own_ref[s],
                other_ref[pl.ds(from_ref[CAP * s], 1), :],
                other_ref[pl.ds(from_ref[CAP * s + 1], 1), :],
                left,
            )
            for s in sources
        ]
        scores = [nt_dot(keys, q) * scale for q, _, keys, _ in operands]
        prob_grads = [nt_dot(values, g) for _, g, _, values in operands]
        probs = [jnp.exp(x - stat[0]) for x, stat in zip(scores, stats)]
        score_grads = [
            (p * (x - stat[1]) * scale).astype(jnp.bfloat16)
            for p, x, stat in zip(probs, prob_grads, stats)
        ]
        probs = [p.astype(jnp.bfloat16) for p in probs]
        attended = [tn_dot(p, ops[3]).astype(jnp.bfloat16) for p, ops in zip(probs, operands)]
        query_grads = [tn_dot(x, ops[2]).astype(jnp.bfloat16) for x, ops in zip(score_grads, operands)]
        value_parts = [nn_dot(p, ops[1]) for p, ops in zip(probs, operands)]
        key_parts = [nn_dot(x, ops[0]) for x, ops in zip(score_grads, operands)]
        for s, att, grad in zip(sources, attended, query_grads):
            stage[s, :SEGMENT] = att[:SEGMENT, :head_dim]
            stage[s, SEGMENT:pair] = grad[:SEGMENT, :head_dim]
            stage[s, pair:pair + SEGMENT] = att[SEGMENT:, head_dim:]
            stage[s, pair + SEGMENT:parts] = grad[SEGMENT:, head_dim:]
        for a, b, key_part, value_part in zip(first, second, key_parts, value_parts):
            acc_k[a] += key_part[:, :head_dim]
            acc_v[a] += value_part[:, :head_dim]
            acc_k[b] += key_part[:, head_dim:]
            acc_v[b] += value_part[:, head_dim:]
        at = pl.ds(i * group, group)
        pltpu.make_async_copy(stage.at[at, :parts], out_ref.at[at, :parts], out_sem).start()
        return 0

    lax.fori_loop(0, seq_count // group, step, 0)
    head_count = near * len(FAR)
    block_count, block_len, _ = acc_k.shape
    row_share = block_len // head_count
    z = lax.axis_index("head")
    rows_copies = []
    for i, a in enumerate(NEAR):
        for j, b in enumerate(FAR):
            dest = lax.rem(z + (a + b + head_count), head_count)
            at = pl.ds(pl.multiple_of(dest * row_share, row_share), row_share)
            rows = jnp.concatenate([acc_k[:, at, :], acc_v[:, at, :]], axis=2)
            rows_near[i, j] = rows.reshape(block_count * row_share, 2 * head_dim).astype(jnp.bfloat16)
        rows_copies.append(pltpu.make_async_copy(rows_near.at[i], rows_refs[i], rows_sems.at[i]))
        rows_copies[i].start()
    rows_all[:, :head_dim] = acc_k[...].reshape(-1, head_dim).astype(jnp.bfloat16)
    rows_all[:, head_dim:] = acc_v[...].reshape(-1, head_dim).astype(jnp.bfloat16)
    room = (stage.shape[1] - parts) // 2
    share = enc_t.shape[0] // seq_count
    fetch.wait()
    batch = 8
    for i in range(0, seq_count, batch):
        term = nn_dot(enc_t[i * share:(i + batch) * share], rows_all[...])
        for s in range(batch):
            part = term[s * share:(s + 1) * share]
            if room > share:
                part = jnp.concatenate([part, jnp.zeros((room - share, 2 * head_dim), jnp.float32)], axis=0)
            part = part.astype(jnp.bfloat16)
            stage[i + s, parts:parts + room] = part[:, :head_dim]
            stage[i + s, parts + room:] = part[:, head_dim:]
        pltpu.make_async_copy(
            stage.at[i:i + batch, parts:], out_ref.at[i:i + batch, parts:], out_sem
        ).start()
    for copy in rows_copies:
        copy.wait()
    pltpu.make_async_copy(stage, out_ref, out_sem).wait()


def finish_kernel(
    slots_ref, in_ref, own_ref, one_ref, two_ref, three_ref,
    att_hbm, qg_hbm, enc_hbm, kw_ref, vw_ref, att_ref, qg_ref, enc_ref, sems,
):
    share = kw_ref.shape[0]
    parts = 2 * CAP * SEGMENT
    room = (in_ref.shape[1] - parts) // 2
    leave_att = pltpu.make_async_copy(att_ref, att_hbm, sems.at[0])
    leave_qg = pltpu.make_async_copy(qg_ref, qg_hbm, sems.at[1])
    leave_enc = pltpu.make_async_copy(enc_ref, enc_hbm, sems.at[2])

    def part(slot):
        holder = lax.div(slot, CAP)
        row = pl.multiple_of((slot - holder * CAP) * 2 * SEGMENT, 2 * SEGMENT)
        return in_ref[holder, pl.ds(row, 2 * SEGMENT), :].astype(jnp.float32)

    for c in range(att_ref.shape[0]):
        total = (part(slots_ref[NEIGH * c]) + part(slots_ref[NEIGH * c + 1])).astype(jnp.bfloat16)
        att_ref[c] = total[:SEGMENT]
        qg_ref[c] = total[SEGMENT:]
    leave_att.start()
    leave_qg.start()
    total = own_ref[...] + one_ref[...].astype(jnp.float32)
    enc_ref[...] = total + two_ref[...].astype(jnp.float32) + three_ref[...].astype(jnp.float32)
    leave_enc.start()
    total = in_ref[0, parts:, :].astype(jnp.float32)
    for s in range(1, in_ref.shape[0]):
        total = total + in_ref[s, parts:, :].astype(jnp.float32)
    kw_ref[...] = total[:share]
    vw_ref[...] = total[room:room + share]
    leave_att.wait()
    leave_qg.wait()
    leave_enc.wait()


def project_kernel(*refs):
    near = len(NEAR)
    rows_hbm, weights_hbm, own_ref, far_refs = refs[:near], refs[near:2 * near], refs[2 * near], refs[2 * near + 1:-3]
    rows_ref, weights_ref, sems = refs[-3:]
    _, far, rows, width = rows_ref.shape
    copies = []
    for n in range(near):
        copies.append(pltpu.make_async_copy(weights_hbm[n], weights_ref.at[n], sems.at[n]))
        copies.append(pltpu.make_async_copy(rows_hbm[n], rows_ref.at[n], sems.at[near + n]))
    for copy in copies:
        copy.start()
    for copy in copies:
        copy.wait()
    half = far // 2
    for i in range(0, far, half):
        total = jnp.zeros((half * rows, own_ref.shape[1]), jnp.float32)
        for n in range(near):
            total = total + nt_dot(rows_ref[n, i:i + half].reshape(half * rows, width), weights_ref[n])
        for j in range(half):
            part = total[j * rows:(j + 1) * rows]
            if i + j == 0:
                own_ref[...] = part
            else:
                far_refs[i + j - 1][...] = part.astype(jnp.bfloat16)


def shifted(x, step):
    count = lax.axis_size("head")
    return lax.ppermute(x, "head", [(z, (z + step) % count) for z in range(count)])


def on_device(queries, encodings, key_weight, value_weight, reads, out_grad):
    seq_count = lax.axis_size("seq")
    head_count = lax.axis_size("head")
    me = lax.axis_index("seq")
    block_count, block_len, enc_width = encodings.shape
    head_dim = key_weight.shape[1]
    segments = queries.shape[0] // SEGMENT
    read_count = NEIGH * segments
    slot_count = seq_count * CAP
    scale = 1.0 / math.sqrt(head_dim)
    bf16, f32 = jnp.bfloat16, jnp.float32

    packed, slots = pl.pallas_call(
        lambda *refs: pack_kernel(block_count, *refs),
        out_shape=(
            jax.ShapeDtypeStruct((slot_count, 2, SEGMENT, head_dim), bf16),
            jax.ShapeDtypeStruct((read_count,), jnp.int32),
        ),
        in_specs=[spec(SMEM), spec(VMEM), spec(VMEM)],
        out_specs=(spec(HBM), spec(SMEM)),
        scratch_shapes=[
            pltpu.SMEM((seq_count,), jnp.int32),
            pltpu.VMEM((slot_count, 2, SEGMENT, head_dim), bf16),
            pltpu.SemaphoreType.DMA,
        ],
        compiler_params=params(LARGE_LIMIT),
        name="pack",
    )(
        reads.T,
        queries.reshape(segments, SEGMENT, head_dim),
        out_grad.reshape(segments, SEGMENT, head_dim),
    )
    arrived = lax.all_to_all(packed, "seq", split_axis=0, concat_axis=0, tiled=True)

    key_weight, value_weight, slots = lax.optimization_barrier((key_weight, value_weight, slots))
    weights = jnp.concatenate([key_weight, value_weight], axis=1)
    flat_enc = encodings.reshape(block_count * block_len, enc_width)
    kv = jnp.dot(flat_enc, weights, preferred_element_type=f32).astype(bf16)
    kv = kv.reshape(block_count, block_len, 2 * head_dim)
    share = enc_width // seq_count
    room = -(-share // 16) * 16
    enc_t = flat_enc.T

    tables = reads.reshape(seq_count, read_count)
    holders = tables // block_count
    partners = holders.reshape(-1, NEIGH)[:, ::-1].reshape(seq_count, read_count)
    mine = holders == me
    rank = jnp.cumsum(mine.astype(jnp.int32), axis=1)
    code = (tables % block_count) + (partners + 1) * block_count
    code = jnp.stack(
        [jnp.sum(jnp.where(mine & (rank == k + 1), code, 0), axis=1) for k in range(CAP)], axis=1
    ).reshape(slot_count)
    blocks = code % block_count
    partner = code // block_count - 1
    taken = partner >= 0
    order = jnp.arange(slot_count)
    same = (partner[:, None] == partner[None, :]) & (order[None, :] < order[:, None])
    place = jnp.sum(same.astype(jnp.int32), axis=1)
    twin = place.reshape(-1, CAP)[:, ::-1].reshape(slot_count)
    send_to = jnp.where(taken, partner * PLACES + jnp.minimum(place, PLACES - 1), seq_count * PLACES)
    taken_from = jnp.minimum(jnp.where(partner == me, twin, place), PLACES - 1)
    taken_from = jnp.where(taken, partner * PLACES + taken_from, 0)
    pairs = jax.nn.one_hot(holders.reshape(-1, NEIGH), seq_count, dtype=bf16)
    shared = lax.dot_general(
        pairs[:, 0], pairs[:, 1], (((0,), (0,)), ((), ())), preferred_element_type=f32
    )
    fits = jnp.max(shared + shared.T) <= PLACES
    taken_from = jnp.where(fits, taken_from, order)
    kv, enc_t, blocks, send_to, taken_from, fits, weights = lax.optimization_barrier(
        (kv, enc_t, blocks, send_to, taken_from, fits, weights)
    )
    near_weights = [weights if a == 0 else shifted(weights, a) for a in NEAR]

    place_count = seq_count * PLACES
    own_stats, slot_stats, sent = pl.pallas_call(
        lambda *refs: stats_kernel(scale, *refs),
        out_shape=(
            jax.ShapeDtypeStruct((seq_count, 2, CAP * SEGMENT), f32),
            jax.ShapeDtypeStruct((slot_count, CAP * SEGMENT), f32),
            jax.ShapeDtypeStruct((place_count, CAP * SEGMENT), f32),
        ),
        in_specs=[spec(SMEM), spec(SMEM), spec(VMEM), spec(VMEM)],
        out_specs=(spec(VMEM),) * 3,
        scratch_shapes=[pltpu.VMEM((place_count + 8, CAP * SEGMENT), f32)],
        compiler_params=params(),
        name="stats",
    )(blocks, send_to, arrived, kv)

    def one_hop(sent, slot_stats, slots):
        return lax.all_to_all(sent, "seq", split_axis=0, concat_axis=0, tiled=True)

    def two_hops(sent, slot_stats, slots):
        at_reader = lax.all_to_all(slot_stats, "seq", split_axis=0, concat_axis=0, tiled=True)
        swapped = pl.pallas_call(
            swap_kernel,
            out_shape=jax.ShapeDtypeStruct(slot_stats.shape, f32),
            in_specs=[spec(SMEM), spec(VMEM)],
            out_specs=spec(VMEM),
            compiler_params=params(),
            name="swap",
        )(slots, at_reader)
        swapped = lax.all_to_all(swapped, "seq", split_axis=0, concat_axis=0, tiled=True)
        return jnp.pad(swapped, ((0, place_count - slot_count), (0, 0)))

    other_stats = lax.cond(fits, one_hop, two_hops, sent, slot_stats, slots)

    row_share = block_len // head_count
    rows = block_count * row_share
    near, far = len(NEAR), len(FAR)
    back_shape = (seq_count, 2 * CAP * SEGMENT + 2 * room, head_dim)
    group = 16
    back, *near_rows = pl.pallas_call(
        lambda *refs: grads_kernel(scale, group, *refs),
        out_shape=(
            jax.ShapeDtypeStruct(back_shape, bf16),
            *[jax.ShapeDtypeStruct((far, rows, 2 * head_dim), bf16)] * near,
        ),
        in_specs=[spec(SMEM), spec(SMEM), spec(HBM), spec(VMEM), spec(VMEM), spec(VMEM), spec(HBM)],
        out_specs=(spec(HBM), *[spec(HBM)] * near),
        scratch_shapes=[
            pltpu.VMEM(arrived.shape, bf16),
            pltpu.VMEM(back_shape, bf16),
            pltpu.VMEM((enc_width, block_count * block_len), bf16),
            pltpu.VMEM((block_count * block_len, 2 * head_dim), bf16),
            pltpu.VMEM((near, far, rows, 2 * head_dim), bf16),
            pltpu.VMEM((block_count, block_len, head_dim), f32),
            pltpu.VMEM((block_count, block_len, head_dim), f32),
            pltpu.SemaphoreType.DMA((seq_count // group,)),
            pltpu.SemaphoreType.DMA,
            pltpu.SemaphoreType.DMA((near,)),
            pltpu.SemaphoreType.DMA,
        ],
        compiler_params=params(LARGE_LIMIT),
        name="grads",
    )(blocks, taken_from, arrived, kv, own_stats, other_stats, enc_t)

    back, *near_weights = lax.optimization_barrier((back, *near_weights))
    near_rows = [r if a == 0 else shifted(r, a) for a, r in zip(NEAR, near_rows)]
    returned = lax.all_to_all(back, "seq", split_axis=0, concat_axis=0, tiled=True)
    own, *far_sums = pl.pallas_call(
        project_kernel,
        out_shape=(
            jax.ShapeDtypeStruct((rows, enc_width), f32),
            *[jax.ShapeDtypeStruct((rows, enc_width), bf16)] * (far - 1),
        ),
        in_specs=[spec(HBM)] * (2 * near),
        out_specs=(spec(VMEM),) * far,
        scratch_shapes=[
            pltpu.VMEM((near, far, rows, 2 * head_dim), bf16),
            pltpu.VMEM((near, enc_width, 2 * head_dim), bf16),
            pltpu.SemaphoreType.DMA((2 * near,)),
        ],
        compiler_params=params(SMALL_LIMIT),
        cost_estimate=pl.CostEstimate(flops=6 * 10**10, bytes_accessed=2 * 10**6, transcendentals=0),
        name="project",
    )(*near_rows, *near_weights)
    far_sums = [shifted(part, b) for b, part in zip(FAR[1:], far_sums)]
    attended, query_grad, encoding_grad, key_weight_grad, value_weight_grad = pl.pallas_call(
        finish_kernel,
        out_shape=(
            jax.ShapeDtypeStruct((segments, SEGMENT, head_dim), bf16),
            jax.ShapeDtypeStruct((segments, SEGMENT, head_dim), bf16),
            jax.ShapeDtypeStruct((rows, enc_width), f32),
            jax.ShapeDtypeStruct((share, head_dim), f32),
            jax.ShapeDtypeStruct((share, head_dim), f32),
        ),
        in_specs=[spec(SMEM), *[spec(VMEM)] * (1 + far)],
        out_specs=(*[spec(HBM)] * 3, spec(VMEM), spec(VMEM)),
        scratch_shapes=[
            pltpu.VMEM((segments, SEGMENT, head_dim), bf16),
            pltpu.VMEM((segments, SEGMENT, head_dim), bf16),
            pltpu.VMEM((rows, enc_width), f32),
            pltpu.SemaphoreType.DMA((3,)),
        ],
        compiler_params=params(),
        name="finish",
    )(slots, returned, own, *far_sums)
    return (
        attended.reshape(segments * SEGMENT, head_dim),
        query_grad.reshape(segments * SEGMENT, head_dim),
        encoding_grad.reshape(block_count, row_share, enc_width),
        key_weight_grad,
        value_weight_grad,
    )


def solution(mesh):
    in_specs = (
        P("seq", "head"),
        P("seq", None, None),
        P(None, "head"),
        P(None, "head"),
        P(),
        P("seq", "head"),
    )
    out_specs = (
        P("seq", "head"),
        P("seq", "head"),
        P("seq", "head", None),
        P("seq", "head"),
        P("seq", "head"),
    )
    return jax.shard_map(
        on_device, mesh=mesh, in_specs=in_specs, out_specs=out_specs, check_vma=False
    )
```
